32 devices in a mesh: ep: 16 (over z, y, x), tp: 2 (over core).
Axes of the slice: x: 2, y: 2, z: 4, core: 2. Of those that a mesh axis runs over, the one named last changes fastest.
Arguments:
- tokens: bfloat16 [2048, 4096], P('ep', 'tp'), may hold values from -6 to 6
- routes: int32 [2048, 8], P('ep'), may hold values from 0 to 31, as said below
- gates: float32 [2048, 8], P('ep'), may hold values from 0.02 to 0.5
- up_weight: bfloat16 [32, 4096, 1024], P('ep', 'tp'), may hold values from -0.09375 to 0.09375
- replica_on: int32 [32], replicated, may hold values from 0 to 1, as said below
- grad_out: bfloat16 [2048, 1024], P('ep', 'tp'), may hold values from -6 to 6
Outputs:
- mixed: bfloat16 [2048, 1024], P('ep', 'tp')
- grad_tokens: bfloat16 [2048, 4096], P('ep', 'tp')
- grad_gates: float32 [2048, 8], P('ep')
- grad_up: bfloat16 [32, 4096, 1024], P('ep', 'tp')
The draws below stay inside these ranges and needn't reach their ends.
Inputs may be any that keep to these rules, and one draw needn't show every extreme that they name: `routes`: each row names 8 different experts; every expert is named by some row. `replica_on`: of the experts j * 2 to (j + 1) * 2 - 1, exactly one has value 1, for every j.
All inputs are finite; a program needn't handle non-finite values.
Results may differ from the reference program's by a relative error of at most 0.0095.
Values may be sent and summed in bfloat16 or wider, within the bound.
No kernel may reach another device: no remote copies, remote signals or barrier semaphores. Data moves between devices by JAX's collectives and lax.ppermute only.
A program may use at most 192 MiB of HBM per device.

```python
import math
import jax
import jax.numpy as jnp
from jax import lax

D = 4096
FF = 1024
TOPK = 8
EXP_DEV = 2
TOK_EP = 128
EXPERTS = 32
TOKENS = 2048
CAP = 24
N_EP = 16


def replica_plan(key):
    picks = jax.random.randint(key, (EXPERTS // EXP_DEV,), 0, EXP_DEV, dtype=jnp.int32)
    expanded = jnp.repeat(picks, EXP_DEV)
    within = jnp.arange(EXPERTS, dtype=jnp.int32) % EXP_DEV
    return within == expanded


def draw_routes(key, part):
    chosen = replica_plan(key)
    key = jax.random.fold_in(key, 3)
    weights = jnp.where(chosen, 4, 1).astype(jnp.int32)
    draws = jax.random.randint(key, (TOKENS, EXPERTS), 0, 65536, dtype=jnp.int32)
    experts_row = jnp.arange(EXPERTS, dtype=jnp.int32)
    scores = draws * weights[None, :] * EXPERTS + experts_row[None, :]
    first = jnp.arange(TOKENS, dtype=jnp.int32) % EXPERTS
    scores = jnp.where(experts_row[None, :] == first[:, None], -1, scores)
    unused, others = lax.top_k(scores, TOPK - 1)
    return jnp.concatenate([first[:, None], others.astype(jnp.int32)], 1)


def draw_replica_on(key, part):
    chosen = replica_plan(key)
    return chosen.astype(jnp.int32)


def levels(rng, dims, pieces, least, top_value):
    level, own = 1.0, jax.random.fold_in(rng, 6)
    for axis_at, shards_of in pieces:
        heights = jnp.exp(jax.random.uniform(jax.random.fold_in(own, axis_at), (shards_of,), jnp.float32, least / len(pieces), top_value / len(pieces)))
        level = level * jnp.repeat(heights, dims[axis_at] // shards_of).reshape([-1 if axis == axis_at else 1 for axis in range(len(dims))])
    return level


def bell_draw(key, shape, width, limit, pieces=(), held_as=jnp.bfloat16):
    array = width * jax.random.normal(key, shape, jnp.float32)
    if pieces:
        array = array * levels(key, shape, pieces, -0.22, 0.18)
    return jnp.clip(array, -limit, limit).astype(held_as)


def setup_inputs(seed: int = 0) -> dict:
    key_list = jax.random.split(jax.random.key(seed), 7)
    return {
        "tokens": bell_draw(key_list[0], (TOKENS, D), 1.0, 6.0, ((0, 16), (1, 2))),
        "routes": draw_routes(jax.random.fold_in(key_list[6], 71), 0),
        "gates": jnp.clip(jnp.exp(math.log(0.5) - 3.218876 * jax.random.uniform(key_list[2], (TOKENS, TOPK), jnp.float32) ** levels(key_list[2], (TOKENS, TOPK), ((0, 16),), -0.2, 0.2)), 0.02, 0.5),
        "up_weight": bell_draw(key_list[3], (EXPERTS, D, FF), D ** -0.5, 0.09375, ((0, 16), (1, 2))),
        "replica_on": draw_replica_on(jax.random.fold_in(key_list[6], 71), 0),
        "grad_out": bell_draw(key_list[5], (TOKENS, FF), 1.0, 6.0, ((0, 16), (1, 2))),
    }


def derivative(hidden):
    sig = jax.nn.sigmoid(hidden)
    return sig * (1.0 + hidden * (1.0 - sig))


def reference(tokens, routes, gates, up_weight, replica_on, grad_out):
    groups = N_EP
    per_group = TOK_EP * TOPK
    flat = routes.reshape(groups, per_group)
    onehot = (flat[:, :, None] == jnp.arange(EXPERTS, dtype=jnp.int32)[None, None, :]).astype(jnp.int32)
    before = jnp.cumsum(onehot, 1) - onehot
    rank = jnp.sum(before * onehot, 2)
    copies = 1 + replica_on[flat]
    copy_index = rank % copies
    slot = rank // copies
    kept = slot < CAP
    group_index = jnp.arange(groups, dtype=jnp.int32)[:, None]
    total = EXPERTS * groups * 2 * CAP
    position = jnp.where(kept, ((flat * groups + group_index) * 2 + copy_index) * CAP + slot, total).astype(jnp.int32)
    pair_ids = jnp.arange(TOKENS * TOPK, dtype=jnp.int32).reshape(groups, per_group)
    table = jnp.full((total + 1,), TOKENS * TOPK, dtype=jnp.int32)
    table = table.at[position.reshape(-1)].set(pair_ids.reshape(-1))[:total].reshape(EXPERTS, groups * 2 * CAP)
    padded_x = jnp.concatenate([tokens, jnp.zeros((1, D), tokens.dtype)], 0)
    row_grad = (gates[:, :, None] * grad_out[:, None, :].astype(jnp.float32)).astype(jnp.bfloat16)
    padded_g = jnp.concatenate([row_grad.reshape(TOKENS * TOPK, FF), jnp.zeros((1, FF), jnp.bfloat16)], 0)

    def per_expert(operands):
        index, w_up = operands
        inputs = padded_x[index // TOPK]
        grads = padded_g[index]
        hidden = jnp.dot(inputs, w_up, preferred_element_type=jnp.float32)
        act = jax.nn.silu(hidden).astype(jnp.bfloat16)
        hidden_grad = (grads.astype(jnp.float32) * derivative(hidden)).astype(jnp.bfloat16)
        g_up = jnp.dot(inputs.T, hidden_grad, preferred_element_type=jnp.float32).astype(jnp.bfloat16)
        input_grad = jnp.dot(hidden_grad, w_up.T, preferred_element_type=jnp.float32).astype(jnp.bfloat16)
        return act, input_grad, g_up

    act, input_grad, grad_up = lax.map(per_expert, (table, up_weight))
    where = position.reshape(TOKENS, TOPK)
    act_flat = jnp.concatenate([act.reshape(total, FF), jnp.zeros((1, FF), jnp.bfloat16)], 0)
    act_pairs = act_flat[where].astype(jnp.float32)
    mixed = jnp.einsum("tk,tkf->tf", gates, act_pairs).astype(jnp.bfloat16)
    grad_gates = jnp.einsum("tkf,tf->tk", act_pairs, grad_out.astype(jnp.float32))
    input_flat = jnp.concatenate([input_grad.reshape(total, D), jnp.zeros((1, D), jnp.bfloat16)], 0)
    grad_tokens = jnp.sum(input_flat[where].astype(jnp.float32), 1).astype(jnp.bfloat16)
    return mixed, grad_tokens, grad_gates, grad_up
```

```python
import functools

import jax
import jax.numpy as jnp
from jax import lax
from jax.experimental import pallas as pl
from jax.experimental.pallas import tpu as pltpu
from jax.sharding import PartitionSpec as P

INNER = 4
CHUNKS = 4
TAIL = 128
LIMIT = 44 * 1024 * 1024
F32, BF16, I32 = jnp.float32, jnp.bfloat16, jnp.int32


def params(**extra):
    return pltpu.CompilerParams(vmem_limit_bytes=LIMIT, **extra)


def cost(flops, moved):
    return pl.CostEstimate(flops=int(flops), bytes_accessed=int(moved), transcendentals=0)


def whole_specs(n):
    return [pl.BlockSpec(memory_space=pltpu.VMEM)] * n


def hot_of(info, device):
    return info[2 + 2 * device + 1]


def rows_joined(pieces):
    if all(piece.shape[0] % 16 == 0 for piece in pieces):
        return jnp.concatenate(pieces, 0)
    return jnp.concatenate([piece.astype(F32) for piece in pieces], 0).astype(BF16)


def payload_kernel(tokens, routes, gates, grad_out, out):
    count, feat = tokens.shape
    share = grad_out.shape[1]
    topk = routes.shape[0]
    out[:, :feat] = tokens[...]
    out[:, feat : feat + share] = grad_out[...]
    ids = routes[...].astype(F32)
    gate = gates[...]
    high = gate.astype(BF16).astype(F32)
    middle = (gate - high).astype(BF16).astype(F32)
    low = (gate - high - middle).astype(BF16).astype(F32)
    rest = jnp.zeros((TAIL - 5 * topk, count), F32)
    tail = jnp.concatenate([ids, ids, high, middle, low, rest], 0)
    out[:, feat + share :] = tail.T.astype(BF16)


def select_kernel(m, hot_rows, cold_rows, topk, n_next, info, *refs):
    payloads, passed, refs = refs[:m], refs[m : m + n_next], refs[m + n_next + 1 :]
    outs, picks, passed_on = refs[:INNER], refs[INNER : INNER + m], refs[INNER + m :]
    for source, target in zip(passed, passed_on):
        target[...] = source[...]
    count, width = payloads[0].shape
    rows = m * (hot_rows + cold_rows)
    cols = INNER * rows
    me = info[0]
    outer, inner = me // INNER, me % INNER
    spot = lax.broadcasted_iota(I32, (8, cols), 1)
    which = jnp.zeros((8, cols), I32)
    for d in range(1, INNER):
        which += (spot >= d * rows).astype(I32)
    within = spot - which * rows
    is_hot = within < m * hot_rows
    group = jnp.zeros((8, cols), I32)
    for s in range(1, m):
        edge = jnp.where(is_hot, s * hot_rows, m * hot_rows + s * cold_rows)
        group += (within >= edge).astype(I32)
    slot = jnp.where(is_hot, within - group * hot_rows, within - m * hot_rows - group * cold_rows)
    expert = jnp.zeros((8, cols), I32)
    for d in range(INNER):
        device = outer * INNER + (inner ^ d)
        hot = hot_of(info, device)
        ids = jnp.where(is_hot, 2 * device + hot, 2 * device + 1 - hot)
        expert = jnp.where(which == d, ids, expert)
    expert = expert.astype(F32)[0:1]
    slot = slot.astype(F32)[0:1]
    group = group[0:1]
    before = lax.broadcasted_iota(I32, (count, count), 1) < lax.broadcasted_iota(I32, (count, count), 0)
    before = jnp.where(before, 1.0, 0.0).astype(BF16)
    found = []
    for s in range(m):
        ids = payloads[s][:, width - TAIL :].astype(F32)
        match = ids[:, 0:1] == expert
        for k in range(1, topk):
            match = match | (ids[:, k : k + 1] == expert)
        ones = jnp.where(match, 1.0, 0.0)
        rank = jnp.dot(before, ones.astype(BF16), preferred_element_type=F32)
        pick = jnp.where((rank == slot) & (group == s), ones, 0.0).astype(BF16)
        picks[s][...] = pick
        found.append(pick)
    step = 384 if width % 384 == 0 else 128
    for at in range(0, width, step):
        total = None
        for s in range(m):
            part = lax.dot_general(
                found[s],
                payloads[s][:, at : at + step],
                (((0,), (0,)), ((), ())),
                preferred_element_type=F32,
            )
            total = part if total is None else total + part
        for d in range(INNER):
            outs[d][:, at : at + step] = total[d * rows : (d + 1) * rows].astype(BF16)


def hidden_kernel(m, hot_rows, cold_rows, feat, info, *refs):
    blocks = refs[:INNER]
    weight, _, part, x_hot, x_cold = refs[INNER:]
    hots = INNER * m * hot_rows
    ff_tile = weight.shape[2]
    ff = part.shape[1] - (blocks[0].shape[1] - feat - TAIL)
    share = part.shape[1] - ff
    j = pl.program_id(0)
    hot = hot_of(info, info[0])

    @pl.when(j == 0)
    def _():
        split = m * hot_rows
        x_hot[...] = rows_joined([b[:split, :feat] for b in blocks])
        x_cold[...] = rows_joined([b[split:, :feat] for b in blocks])
        part[:hots, ff:] = rows_joined([b[:split, feat : feat + share] for b in blocks])
        part[hots:, ff:] = rows_joined([b[split:, feat : feat + share] for b in blocks])

    at = pl.ds(pl.multiple_of(j * ff_tile, ff_tile), ff_tile)
    part[:hots, at] = jnp.dot(x_hot[...], weight[hot], preferred_element_type=F32).astype(BF16)
    part[hots:, at] = jnp.dot(x_cold[...], weight[1 - hot], preferred_element_type=F32).astype(BF16)


def back_kernel(m, hot_rows, cold_rows, n_parts, n_grads, topk, share, info, *refs):
    sums, grads = refs[:n_parts], refs[n_parts : n_parts + n_grads]
    refs = refs[n_parts + n_grads :]
    tails, weight, outs = refs[:INNER], refs[INNER], refs[INNER + 2 : 2 * INNER + 2]
    g_hot, g_cold = refs[2 * INNER + 2 :]
    hots, colds = INNER * m * hot_rows, INNER * m * cold_rows
    ff = weight.shape[2]
    tile = weight.shape[1]
    width = outs[0].shape[1]
    me, tp = info[0], info[1]
    hot = hot_of(info, me)
    split = m * hot_rows
    j = pl.program_id(0)
    own = width - TAIL

    @pl.when(j == 0)
    def _():
        for first, size, piece, target, expert in (
            (0, hots, m * hot_rows, g_hot, 2 * me + hot),
            (hots, colds, m * cold_rows, g_cold, 2 * me + 1 - hot),
        ):
            begin = 0 if first == 0 else split
            tail_rows = [t[begin : begin + piece].astype(F32) for t in tails]
            per = 1 if piece % 16 == 0 else INNER
            for d in range(0, INNER, per):
                count = piece * per
                rows = slice(first + d * piece, first + d * piece + count)
                tail = jnp.concatenate(tail_rows[d : d + per], 0)
                hidden = sums[0][rows, :ff].astype(F32)
                for more in sums[1:]:
                    hidden = hidden + more[rows, :ff].astype(F32)
                if n_grads == 1:
                    grad = grads[0][rows].astype(F32)
                else:
                    mine, other = grads[0][rows].astype(F32), grads[1][rows].astype(F32)
                    even = tp == 0
                    grad = jnp.concatenate(
                        [jnp.where(even, mine, other), jnp.where(even, other, mine)], 1
                    )
                e = expert.astype(F32)
                ids = tail[:, :topk]
                gate = (tail[:, 2 * topk : 3 * topk] + tail[:, 3 * topk : 4 * topk]) + tail[:, 4 * topk : 5 * topk]
                gate = jnp.sum(jnp.where(ids == e, gate, 0.0), 1, keepdims=True)
                sig = 1.0 / (1.0 + jnp.exp(-hidden))
                act = (hidden * sig).astype(BF16).astype(F32)
                row_grad = (gate * grad).astype(BF16).astype(F32)
                hidden_grad = row_grad * (sig * (1.0 + hidden * (1.0 - sig)))
                target[d * piece : d * piece + count] = hidden_grad.astype(BF16)
                gate_grad = jnp.sum(act * grad, 1, keepdims=True)
                high = gate_grad.astype(BF16).astype(F32)
                low = gate_grad - high
                lane = lax.broadcasted_iota(I32, tail.shape, 1)
                values = jnp.where(lane < topk, high, low)
                end = jnp.where((tail == e) & (lane < 2 * topk), values, 0.0)
                gated = None
                for n in range(ff // share):
                    piece_act = jnp.where(tp == n, act[:, n * share : (n + 1) * share], 0.0)
                    gated = piece_act if gated is None else gated + piece_act
                gated = gate * gated
                for n in range(per):
                    at = slice(n * piece, (n + 1) * piece)
                    outs[d + n][begin : begin + piece, own - share : own] = gated[at].astype(BF16)
                    outs[d + n][begin : begin + piece, own:] = end[at].astype(BF16)

    at = pl.ds(pl.multiple_of(j * tile, tile), tile)
    for target, weight_now, begin, piece in (
        (g_hot, weight[hot], 0, m * hot_rows),
        (g_cold, weight[1 - hot], split, m * cold_rows),
    ):
        rows = lax.dot_general(
            target[...], weight_now, (((1,), (1,)), ((), ())), preferred_element_type=F32
        )
        for d in range(INNER):
            outs[d][begin : begin + piece, at] = rows[d * piece : (d + 1) * piece].astype(BF16)


def expand_kernel(m, *refs):
    blocks, picks, outs = refs[:INNER], refs[INNER : INNER + m], refs[INNER + m + 1 :]
    width = blocks[0].shape[1]
    step = 384 if width % 384 == 0 else 128
    for at in range(0, width, step):
        rows = rows_joined([b[:, at : at + step] for b in blocks])
        for s in range(m):
            outs[s][:, at : at + step] = jnp.dot(
                picks[s][...], rows, preferred_element_type=F32
            ).astype(BF16)


def final_kernel(n, topk, *refs):
    parts = refs[:n]
    mixed, grad_tokens, grad_gates = refs[n:]
    feat, share = grad_tokens.shape[1], mixed.shape[1]

    def total(columns):
        out = parts[0][:, columns].astype(F32)
        for part in parts[1:]:
            out = out + part[:, columns].astype(F32)
        return out

    grad_tokens[...] = total(slice(0, feat)).astype(BF16)
    mixed[...] = total(slice(feat, feat + share)).astype(BF16)
    tail = total(slice(feat + share, feat + share + TAIL))
    tail = tail.T
    grad_gates[...] = tail[:topk] + tail[topk : 2 * topk]


def up_kernel(n, info, *refs):
    x_hot, x_cold = refs[:n], refs[n : 2 * n]
    g_hot, g_cold = refs[2 * n : 3 * n], refs[3 * n : 4 * n]
    out = refs[4 * n + 1]

    def total(xs, gs):
        acc = None
        for x, g in zip(xs, gs):
            part = lax.dot_general(
                x[...], g[...], (((0,), (0,)), ((), ())), preferred_element_type=F32
            )
            acc = part if acc is None else acc + part
        out[0] = acc.astype(BF16)

    @pl.when(pl.program_id(0) == 0)
    def _():
        total(x_hot, g_hot)

    @pl.when(pl.program_id(0) == 1)
    def _():
        total(x_cold, g_cold)


def on_device(tokens, routes, gates, up_weight, replica_on, grad_out):
    count, feat = tokens.shape
    topk = routes.shape[1]
    experts = replica_on.shape[0]
    share = grad_out.shape[1]
    ff = up_weight.shape[2]
    n_ep, n_tp = lax.axis_size("ep"), lax.axis_size("tp")
    outer = n_ep // INNER
    capacity = 3 * count * topk // (4 * experts)
    hot_rows, cold_rows = 2 * capacity, capacity
    width = feat + share + TAIL
    me, tp = lax.axis_index("ep"), lax.axis_index("tp")
    info = jnp.concatenate([jnp.stack([me, tp]).astype(I32), replica_on])
    smem = pl.BlockSpec(memory_space=pltpu.SMEM)

    def along(value, shift):
        pairs = [
            (o * INNER + i, ((o + shift) % outer) * INNER + i)
            for o in range(outer)
            for i in range(INNER)
        ]
        return lax.ppermute(value, "ep", pairs)

    def across(value, d):
        pairs = [(o * INNER + i, o * INNER + (i ^ d)) for o in range(outer) for i in range(INNER)]
        return lax.ppermute(value, "ep", pairs)

    payload = pl.pallas_call(
        payload_kernel,
        out_shape=jax.ShapeDtypeStruct((count, width), BF16),
        in_specs=whole_specs(4),
        out_specs=whole_specs(1)[0],
        compiler_params=params(),
        cost_estimate=cost(0, 4 * count * width),
        name="payload",
    )(tokens, routes.T, gates.T, grad_out)

    last = [payload]
    rest_spec = pl.BlockSpec(memory_space=pl.ANY)
    m = max(1, outer // CHUNKS)
    chunks = [list(range(first, first + m)) for first in range(0, outer, m)]
    n = len(chunks)
    rows = m * (hot_rows + cold_rows)
    hots, colds = INNER * m * hot_rows, INNER * m * cold_rows
    ff_tile = 256 if ff % 256 == 0 else ff
    d_tile = 512 if feat % 512 == 0 else feat
    small = cost(10**6, 10**5)

    def block(shape, dtype=BF16):
        return jax.ShapeDtypeStruct(shape, dtype)

    carried = {0: payload, 1: payload}
    picks, blocks, sums, grads, sent, partials = {}, {}, {}, {}, {}, {}
    x_hots, x_colds, g_hots, g_colds = {}, {}, {}, {}

    def select(c):
        passed = [payload] if 0 < c < n - 1 else []
        made = pl.pallas_call(
            functools.partial(select_kernel, m, hot_rows, cold_rows, topk, len(passed)),
            out_shape=[block((rows, width))] * INNER
            + [block((count, INNER * rows))] * m
            + [block((count, width))] * len(passed),
            in_specs=[smem] + whole_specs(m + len(passed)) + [rest_spec],
            out_specs=whole_specs(INNER + m + len(passed)),
            compiler_params=params(),
            cost_estimate=small,
            name="select",
        )(info, *[along(carried[c], s) if s else payload for s in chunks[c]], *passed, last[0])
        picks[c] = made[INNER : INNER + m]
        if passed:
            carried[c + 1] = made[INNER + m]
        blocks[c] = [made[0]] + [across(made[d], d) for d in range(1, INNER)]
        last[0] = picks[c][0]

    def hidden(c):
        part, x_hots[c], x_colds[c] = pl.pallas_call(
            functools.partial(hidden_kernel, m, hot_rows, cold_rows, feat),
            out_shape=[block((INNER * rows, ff + share)), block((hots, feat)), block((colds, feat))],
            grid=(ff // ff_tile,),
            in_specs=[smem]
            + [pl.BlockSpec((rows, width), lambda j: (0, 0))] * INNER
            + [pl.BlockSpec((2, feat, ff_tile), lambda j: (0, 0, j)), rest_spec],
            out_specs=[
                pl.BlockSpec((INNER * rows, ff + share), lambda j: (0, 0)),
                pl.BlockSpec((hots, feat), lambda j: (0, 0)),
                pl.BlockSpec((colds, feat), lambda j: (0, 0)),
            ],
            compiler_params=params(),
            cost_estimate=small,
            name="hidden",
        )(info, *blocks[c], up_weight, last[0])
        last[0] = x_colds[c]
        if n_tp == 2:
            sums[c] = [part, lax.ppermute(part, "tp", [(0, 1), (1, 0)])]
            grads[c] = sums[c]
        else:
            sums[c] = [lax.psum(part[:, :ff].astype(F32), "tp")]
            grads[c] = [lax.all_gather(part[:, ff:], "tp", axis=1, tiled=True)]

    def back(c):
        if n_tp == 2:
            grad_specs = [pl.BlockSpec((INNER * rows, share), lambda j: (0, ff // share))] * 2
        else:
            grad_specs = [pl.BlockSpec((INNER * rows, ff), lambda j: (0, 0))]
        made = pl.pallas_call(
            functools.partial(
                back_kernel, m, hot_rows, cold_rows, len(sums[c]), len(grads[c]), topk, share
            ),
            out_shape=[block((rows, width))] * INNER + [block((hots, ff)), block((colds, ff))],
            grid=(feat // d_tile,),
            in_specs=[smem]
            + [pl.BlockSpec((INNER * rows, ff), lambda j: (0, 0))] * len(sums[c])
            + grad_specs
            + [pl.BlockSpec((rows, TAIL), lambda j: (0, width // TAIL - 1))] * INNER
            + [pl.BlockSpec((2, d_tile, ff), lambda j: (0, j, 0)), rest_spec],
            out_specs=[pl.BlockSpec((rows, width), lambda j: (0, 0))] * INNER
            + [pl.BlockSpec((hots, ff), lambda j: (0, 0)), pl.BlockSpec((colds, ff), lambda j: (0, 0))],
            compiler_params=params(),
            cost_estimate=small,
            name="back",
        )(info, *sums[c], *grads[c], *blocks[c], up_weight, last[0])
        g_hots[c], g_colds[c] = made[INNER:]
        sent[c] = [made[0]] + [across(made[d], d) for d in range(1, INNER)]
        last[0] = g_colds[c]

    def expand(c):
        made = pl.pallas_call(
            functools.partial(expand_kernel, m),
            out_shape=[block((count, width))] * m,
            in_specs=whole_specs(INNER + m) + [rest_spec],
            out_specs=whole_specs(m),
            compiler_params=params(),
            cost_estimate=small,
            name="expand",
        )(*sent[c], *picks[c], last[0])
        for s, value in zip(chunks[c], made):
            partials[s] = along(value, outer - s) if s else value
        last[0] = made[0]

    def weight_grad():
        grad_up = pl.pallas_call(
            functools.partial(up_kernel, n),
            out_shape=block(up_weight.shape),
            grid_spec=pltpu.PrefetchScalarGridSpec(
                num_scalar_prefetch=1,
                grid=(2, feat // 256),
                in_specs=[pl.BlockSpec((hots, 256), lambda e, j, info: (0, j))] * n
                + [pl.BlockSpec((colds, 256), lambda e, j, info: (0, j))] * n
                + [pl.BlockSpec((hots, ff), lambda e, j, info: (0, 0))] * n
                + [pl.BlockSpec((colds, ff), lambda e, j, info: (0, 0))] * n
                + [rest_spec],
                out_specs=pl.BlockSpec(
                    (1, 256, ff),
                    lambda e, j, info: (e + hot_of(info, info[0]) * (1 - 2 * e), j, 0),
                ),
            ),
            compiler_params=params(),
            cost_estimate=small,
            name="grad_up",
        )(
            info,
            *[x_hots[c] for c in range(n)],
            *[x_colds[c] for c in range(n)],
            *[g_hots[c] for c in range(n)],
            *[g_colds[c] for c in range(n)],
            last[0],
        )
        last[0] = grad_up
        return grad_up

    select(0)
    select(1)
    hidden(0)
    hidden(1)
    select(2)
    back(1)
    select(3)
    hidden(2)
    expand(1)
    back(2)
    hidden(3)
    back(3)
    expand(2)
    back(0)
    expand(3)
    grad_up = weight_grad()
    expand(0)

    mixed, grad_tokens, grad_gates = pl.pallas_call(
        functools.partial(final_kernel, outer, topk),
        out_shape=[block((count, share)), block((count, feat)), block((topk, count), F32)],
        in_specs=whole_specs(outer),
        out_specs=whole_specs(3),
        compiler_params=params(),
        cost_estimate=small,
        name="final",
    )(*[partials[s] for s in range(outer)])
    return mixed, grad_tokens, grad_gates.T, grad_up


def solution(mesh):
    return jax.shard_map(
        on_device,
        mesh=mesh,
        in_specs=(
            P("ep", "tp"),
            P("ep", None),
            P("ep", None),
            P("ep", "tp", None),
            P(),
            P("ep", "tp"),
        ),
        out_specs=(P("ep", "tp"), P("ep", "tp"), P("ep", None), P("ep", "tp", None)),
        check_vma=False,
    )
```

```python
import functools

import jax
import jax.numpy as jnp
from jax import lax
from jax.experimental import pallas as pl
from jax.experimental.pallas import tpu as pltpu
from jax.sharding import PartitionSpec as P

INNER = 4
CHUNKS = 4
PLAN = ((0, None), (1, None), (2, None), (3, 0), (None, 1), (None, 2), (None, 3))
ORDER = ("x1", "h0", "x2", "h1", "x3", "h2", "x4", "h3", "x5", "e0", "e1", "x6", "e2", "u", "e3")
PASSED = (3,)
COSTS = {"x": 1, "b": 1, "h": 1, "e": 1, "u": 1}
TAIL = 128
LIMIT = 44 * 1024 * 1024
F32, BF16, I32 = jnp.float32, jnp.bfloat16, jnp.int32


def params(**extra):
    return pltpu.CompilerParams(vmem_limit_bytes=LIMIT, **extra)


def cost(flops, moved):
    return pl.CostEstimate(flops=int(flops), bytes_accessed=int(moved), transcendentals=0)


def whole_specs(n):
    return [pl.BlockSpec(memory_space=pltpu.VMEM)] * n


def hot_of(info, device):
    return info[2 + 2 * device + 1]


def rows_joined(pieces):
    if all(piece.shape[0] % 16 == 0 for piece in pieces):
        return jnp.concatenate(pieces, 0)
    return jnp.concatenate([piece.astype(F32) for piece in pieces], 0).astype(BF16)


def pick_rows(m, hot_rows, cold_rows, topk, info, tails):
    count = tails[0].shape[0]
    rows = m * (hot_rows + cold_rows)
    cols = INNER * rows
    me = info[0]
    outer, inner = me // INNER, me % INNER
    spot = lax.broadcasted_iota(I32, (8, cols), 1)
    which = jnp.zeros((8, cols), I32)
    for d in range(1, INNER):
        which += (spot >= d * rows).astype(I32)
    within = spot - which * rows
    is_hot = within < m * hot_rows
    group = jnp.zeros((8, cols), I32)
    for s in range(1, m):
        edge = jnp.where(is_hot, s * hot_rows, m * hot_rows + s * cold_rows)
        group += (within >= edge).astype(I32)
    slot = jnp.where(is_hot, within - group * hot_rows, within - m * hot_rows - group * cold_rows)
    expert = jnp.zeros((8, cols), I32)
    for d in range(INNER):
        device = outer * INNER + (inner ^ d)
        hot = hot_of(info, device)
        ids = jnp.where(is_hot, 2 * device + hot, 2 * device + 1 - hot)
        expert = jnp.where(which == d, ids, expert)
    expert = expert.astype(F32)[0:1]
    slot = slot.astype(F32)[0:1]
    group = group[0:1]
    before = lax.broadcasted_iota(I32, (count, count), 1) < lax.broadcasted_iota(I32, (count, count), 0)
    before = jnp.where(before, 1.0, 0.0).astype(BF16)
    found = []
    for s, ids in enumerate(tails):
        match = ids[:, 0:1] == expert
        for k in range(1, topk):
            match = match | (ids[:, k : k + 1] == expert)
        ones = jnp.where(match, 1.0, 0.0)
        rank = jnp.dot(before, ones.astype(BF16), preferred_element_type=F32)
        found.append(jnp.where((rank == slot) & (group == s), ones, 0.0).astype(BF16))
    return found


def picked(picks, payloads, columns):
    total = None
    for pick, payload in zip(picks, payloads):
        part = lax.dot_general(
            pick[...], payload[:, columns], (((0,), (0,)), ((), ())), preferred_element_type=F32
        )
        total = part if total is None else total + part
    return total


def select_all(picks, payloads, outs):
    rows, width = outs[0].shape
    step = 384 if width % 384 == 0 else 128
    for at in range(0, width, step):
        columns = slice(at, at + step)
        total = picked(picks, payloads, columns)
        for d in range(INNER):
            outs[d][:, columns] = total[d * rows : (d + 1) * rows].astype(BF16)


def start_kernel(m, hot_rows, cold_rows, info, tokens, routes, gates, grad_out, *refs):
    out, refs = refs[0], refs[1:]
    outs, picks = refs[:INNER], refs[INNER:]
    count, feat = tokens.shape
    share = grad_out.shape[1]
    topk = routes.shape[0]
    out[:, :feat] = tokens[...]
    out[:, feat : feat + share] = grad_out[...]
    ids = routes[...].astype(F32)
    gate = gates[...]
    high = gate.astype(BF16).astype(F32)
    middle = (gate - high).astype(BF16).astype(F32)
    low = (gate - high - middle).astype(BF16).astype(F32)
    rest = jnp.zeros((TAIL - 5 * topk, count), F32)
    tail = jnp.concatenate([ids, ids, high, middle, low, rest], 0).T
    out[:, feat + share :] = tail.astype(BF16)
    if picks:
        picks[0][...] = pick_rows(m, hot_rows, cold_rows, topk, info, [tail])[0]
        select_all(picks, [out], outs)


def select_kernel(m, hot_rows, cold_rows, topk, info, *refs):
    payloads, refs = refs[:m], refs[m + 1 :]
    outs, picks, passed = refs[:INNER], refs[INNER : INNER + m], refs[INNER + m :]
    width = payloads[0].shape[1]
    for source, target in zip(payloads, passed):
        target[...] = source[...]
    tails = [payload[:, width - TAIL :].astype(F32) for payload in payloads]
    for pick, found in zip(picks, pick_rows(m, hot_rows, cold_rows, topk, info, tails)):
        pick[...] = found
    select_all(picks, payloads, outs)


def forward_rows(block, both, hots, columns):
    if not both:
        return block[:hots, columns], block[hots:, columns]
    colds = block.shape[0] // 2 - hots
    return block[:hots, columns], block[2 * hots : 2 * hots + colds, columns]


def returned_rows(block, both, hots, columns):
    if not both:
        return block[:, columns]
    colds = block.shape[0] // 2 - hots
    cold = block[2 * hots :, columns].astype(F32)[colds:]
    return jnp.concatenate([block[hots : 2 * hots, columns].astype(F32), cold], 0)


def hidden_kernel(m, hot_rows, cold_rows, feat, both, info, *refs):
    blocks = refs[:INNER]
    weight, _, part, x_hot, x_cold = refs[INNER:]
    hots = INNER * m * hot_rows
    ff_tile = weight.shape[2]
    share = blocks[0].shape[1] - feat - TAIL
    ff = part.shape[1] - share
    j = pl.program_id(0)
    hot = hot_of(info, info[0])

    @pl.when(j == 0)
    def _():
        split = m * hot_rows
        rows = [forward_rows(b, both, split, slice(0, feat)) for b in blocks]
        x_hot[...] = rows_joined([hot_part for hot_part, _ in rows])
        x_cold[...] = rows_joined([cold_part for _, cold_part in rows])
        rows = [forward_rows(b, both, split, slice(feat, feat + share)) for b in blocks]
        part[:hots, ff:] = rows_joined([hot_part for hot_part, _ in rows])
        part[hots:, ff:] = rows_joined([cold_part for _, cold_part in rows])

    at = pl.ds(pl.multiple_of(j * ff_tile, ff_tile), ff_tile)
    part[:hots, at] = jnp.dot(x_hot[...], weight[hot], preferred_element_type=F32).astype(BF16)
    part[hots:, at] = jnp.dot(x_cold[...], weight[1 - hot], preferred_element_type=F32).astype(BF16)


def back_kernel(m, hot_rows, cold_rows, n_parts, n_grads, topk, share, both, n_pay, info, *refs):
    sums, grads = refs[:n_parts], refs[n_parts : n_parts + n_grads]
    refs = refs[n_parts + n_grads :]
    tails, weight, payloads = refs[:INNER], refs[INNER], refs[INNER + 1 : INNER + 1 + n_pay]
    refs = refs[INNER + 2 + n_pay :]
    outs, g_hot, g_cold, picks = refs[:INNER], refs[INNER], refs[INNER + 1], refs[INNER + 2 :]
    hots, colds = m * hot_rows, m * cold_rows
    rows = hots + colds
    ff = weight.shape[2]
    tile = weight.shape[1]
    width = outs[0].shape[1]
    feat = width - share - TAIL
    me, tp = info[0], info[1]
    hot = hot_of(info, me)
    j = pl.program_id(0)

    def put(columns, back_hot, back_cold):
        there = picked(picks, payloads, columns) if n_pay else None
        for d in range(INNER):
            hot_now = back_hot[d * hots : (d + 1) * hots]
            cold_now = back_cold[d * colds : (d + 1) * colds]
            if n_pay:
                mine = there[d * rows : (d + 1) * rows]
                outs[d][:hots, columns] = mine[:hots].astype(BF16)
                outs[d][hots : 2 * hots, columns] = hot_now.astype(BF16)
                outs[d][2 * hots :, columns] = jnp.concatenate([mine[hots:], cold_now], 0).astype(BF16)
            else:
                outs[d][:hots, columns] = hot_now.astype(BF16)
                outs[d][hots:, columns] = cold_now.astype(BF16)

    @pl.when(j == 0)
    def _():
        if n_pay:
            ids = [payload[:, width - TAIL :].astype(F32) for payload in payloads]
            for pick, found in zip(picks, pick_rows(m, hot_rows, cold_rows, topk, info, ids)):
                pick[...] = found
        tail_rows = [forward_rows(t, both, hots, slice(None)) for t in tails]
        ends = []
        for kind, first, piece, target, expert in (
            (0, 0, hots, g_hot, 2 * me + hot),
            (1, INNER * hots, colds, g_cold, 2 * me + 1 - hot),
        ):
            made = []
            per = 1 if piece % 16 == 0 else INNER
            for d in range(0, INNER, per):
                count = piece * per
                now = slice(first + d * piece, first + d * piece + count)
                tail = jnp.concatenate([t[kind].astype(F32) for t in tail_rows[d : d + per]], 0)
                hidden = sums[0][now, :ff].astype(F32)
                for more in sums[1:]:
                    hidden = hidden + more[now, :ff].astype(F32)
                if n_grads == 1:
                    grad = grads[0][now].astype(F32)
                else:
                    mine, other = grads[0][now].astype(F32), grads[1][now].astype(F32)
                    even = tp == 0
                    grad = jnp.concatenate(
                        [jnp.where(even, mine, other), jnp.where(even, other, mine)], 1
                    )
                e = expert.astype(F32)
                ids = tail[:, :topk]
                gate = (tail[:, 2 * topk : 3 * topk] + tail[:, 3 * topk : 4 * topk]) + tail[:, 4 * topk : 5 * topk]
                gate = jnp.sum(jnp.where(ids == e, gate, 0.0), 1, keepdims=True)
                sig = 1.0 / (1.0 + jnp.exp(-hidden))
                act = (hidden * sig).astype(BF16).astype(F32)
                row_grad = (gate * grad).astype(BF16).astype(F32)
                hidden_grad = row_grad * (sig * (1.0 + hidden * (1.0 - sig)))
                target[d * piece : d * piece + count] = hidden_grad.astype(BF16)
                gate_grad = jnp.sum(act * grad, 1, keepdims=True)
                high = gate_grad.astype(BF16).astype(F32)
                low = gate_grad - high
                lane = lax.broadcasted_iota(I32, tail.shape, 1)
                values = jnp.where(lane < topk, high, low)
                end = jnp.where((tail == e) & (lane < 2 * topk), values, 0.0)
                gated = None
                for n in range(ff // share):
                    piece_act = jnp.where(tp == n, act[:, n * share : (n + 1) * share], 0.0)
                    gated = piece_act if gated is None else gated + piece_act
                made.append(jnp.concatenate([gate * gated, end], 1))
            ends.append(jnp.concatenate(made, 0))
        put(slice(feat, width), *ends)

    at = pl.ds(pl.multiple_of(j * tile, tile), tile)
    across_rows = (((1,), (1,)), ((), ()))
    put(
        at,
        lax.dot_general(g_hot[...], weight[hot], across_rows, preferred_element_type=F32),
        lax.dot_general(g_cold[...], weight[1 - hot], across_rows, preferred_element_type=F32),
    )


def expand_kernel(m, hots, both, n_more, *refs):
    blocks, picks, refs = refs[:INNER], refs[INNER : INNER + m], refs[INNER + m :]
    more, outs = refs[:n_more], refs[n_more + 1 :]
    width = blocks[0].shape[1]
    step = 384 if width % 384 == 0 else 128
    for at in range(0, width, step):
        columns = slice(at, at + step)
        rows = rows_joined([returned_rows(b, both, hots, columns) for b in blocks]).astype(BF16)
        for s in range(m):
            total = jnp.dot(picks[s][...], rows, preferred_element_type=F32)
            if more:
                total = total + more[s][:, columns].astype(F32)
            outs[s][:, columns] = total.astype(BF16)


def final_kernel(n, topk, *refs):
    parts = refs[:n]
    mixed, grad_tokens, grad_gates = refs[n:]
    feat, share = grad_tokens.shape[1], mixed.shape[1]

    def total(columns):
        out = parts[0][:, columns].astype(F32)
        for part in parts[1:]:
            out = out + part[:, columns].astype(F32)
        return out

    grad_tokens[...] = total(slice(0, feat)).astype(BF16)
    mixed[...] = total(slice(feat, feat + share)).astype(BF16)
    tail = total(slice(feat + share, feat + share + TAIL))
    tail = tail.T
    grad_gates[...] = tail[:topk] + tail[topk : 2 * topk]


def up_kernel(n, info, *refs):
    x_hot, x_cold = refs[:n], refs[n : 2 * n]
    g_hot, g_cold = refs[2 * n : 3 * n], refs[3 * n : 4 * n]
    out = refs[4 * n + 1]

    def total(xs, gs):
        acc = None
        for x, g in zip(xs, gs):
            part = lax.dot_general(
                x[...], g[...], (((0,), (0,)), ((), ())), preferred_element_type=F32
            )
            acc = part if acc is None else acc + part
        out[0] = acc.astype(BF16)

    @pl.when(pl.program_id(0) == 0)
    def _():
        total(x_hot, g_hot)

    @pl.when(pl.program_id(0) == 1)
    def _():
        total(x_cold, g_cold)


def on_device(tokens, routes, gates, up_weight, replica_on, grad_out):
    count, feat = tokens.shape
    topk = routes.shape[1]
    experts = replica_on.shape[0]
    share = grad_out.shape[1]
    ff = up_weight.shape[2]
    n_ep, n_tp = lax.axis_size("ep"), lax.axis_size("tp")
    outer = n_ep // INNER
    capacity = 3 * count * topk // (4 * experts)
    hot_rows, cold_rows = 2 * capacity, capacity
    width = feat + share + TAIL
    me, tp = lax.axis_index("ep"), lax.axis_index("tp")
    info = jnp.concatenate([jnp.stack([me, tp]).astype(I32), replica_on])
    smem = pl.BlockSpec(memory_space=pltpu.SMEM)

    def along(value, shift):
        pairs = [
            (o * INNER + i, ((o + shift) % outer) * INNER + i)
            for o in range(outer)
            for i in range(INNER)
        ]
        return lax.ppermute(value, "ep", pairs)

    def across(value, d):
        pairs = [(o * INNER + i, o * INNER + (i ^ d)) for o in range(outer) for i in range(INNER)]
        return lax.ppermute(value, "ep", pairs)

    rest_spec = pl.BlockSpec(memory_space=pl.ANY)
    m = max(1, outer // CHUNKS)
    chunks = [list(range(first, first + m)) for first in range(0, outer, m)]
    n = len(chunks)
    rows = m * (hot_rows + cold_rows)
    hots, colds = INNER * m * hot_rows, INNER * m * cold_rows
    ff_tile = 256 if ff % 256 == 0 else ff
    d_tile = 512 if feat % 512 == 0 else feat
    sizes = (m, hot_rows, cold_rows)

    def block(shape, dtype=BF16):
        return jax.ShapeDtypeStruct(shape, dtype)

    def fixed(shape):
        return pl.BlockSpec(shape, lambda j: (0,) * len(shape))

    going = {f: k for k, (f, _) in enumerate(PLAN) if f is not None}
    coming = {r: k for k, (_, r) in enumerate(PLAN) if r is not None}

    def doubled(k):
        return None not in PLAN[k]

    def weigh(kind):
        return cost(COSTS[kind] * 10**6, COSTS[kind] * 10**4)

    arrived, picks, blocks, sums, grads, partials = {}, {}, {}, {}, {}, {}
    x_hots, x_colds, g_hots, g_colds = {}, {}, {}, {}

    def exchange(k, made):
        blocks[k] = [made[0]] + [across(made[d], d) for d in range(1, INNER)]

    own_rows = m == 1
    made = pl.pallas_call(
        functools.partial(start_kernel, *sizes),
        out_shape=[block((count, width))]
        + ([block((rows, width))] * INNER + [block((count, INNER * rows))] if own_rows else []),
        grid=(1,),
        in_specs=[
            smem,
            fixed((count, feat)),
            fixed((topk, count)),
            fixed((topk, count)),
            fixed((count, share)),
        ],
        out_specs=[fixed((count, width))]
        + ([fixed((rows, width))] * INNER + [fixed((count, INNER * rows))] if own_rows else []),
        compiler_params=params(),
        cost_estimate=weigh("x"),
        name="start",
    )(info, tokens, routes.T, gates.T, grad_out)
    payload = made[0]
    last = [payload]
    for c in range(n):
        for s in chunks[c] if c not in PASSED else ():
            if s == 0:
                arrived[s] = payload
            else:
                arrived[s] = along(arrived[s - m], m) if c else along(payload, s)

    def select(k):
        c = PLAN[k][0]
        more = m if c + 1 in PASSED else 0
        made = pl.pallas_call(
            functools.partial(select_kernel, *sizes, topk),
            out_shape=[block((rows, width))] * INNER
            + [block((count, INNER * rows))] * m
            + [block((count, width))] * more,
            in_specs=[smem] + whole_specs(m) + [rest_spec],
            out_specs=whole_specs(INNER + m + more),
            compiler_params=params(),
            cost_estimate=weigh("x"),
            name="select",
        )(info, *[arrived[s] for s in chunks[c]], last[0])
        picks[c] = made[INNER : INNER + m]
        exchange(k, made)
        if more:
            for s, value in zip(chunks[c + 1], made[INNER + m :]):
                arrived[s] = along(value, m)
        last[0] = picks[c][0]

    def hidden(c):
        k = going[c]
        held = (2 if doubled(k) else 1) * rows
        part, x_hots[c], x_colds[c] = pl.pallas_call(
            functools.partial(hidden_kernel, *sizes, feat, doubled(k)),
            out_shape=[block((INNER * rows, ff + share)), block((hots, feat)), block((colds, feat))],
            grid=(ff // ff_tile,),
            in_specs=[smem]
            + [fixed((held, width))] * INNER
            + [pl.BlockSpec((2, feat, ff_tile), lambda j: (0, 0, j)), rest_spec],
            out_specs=[fixed((INNER * rows, ff + share)), fixed((hots, feat)), fixed((colds, feat))],
            compiler_params=params(),
            cost_estimate=weigh("h"),
            name="hidden",
        )(info, *blocks[k], up_weight, last[0])
        last[0] = x_colds[c]
        if n_tp == 2:
            sums[c] = [part, lax.ppermute(part, "tp", [(0, 1), (1, 0)])]
            grads[c] = sums[c]
        else:
            sums[c] = [lax.psum(part[:, :ff].astype(F32), "tp")]
            grads[c] = [lax.all_gather(part[:, ff:], "tp", axis=1, tiled=True)]

    def step(k):
        f, c = PLAN[k]
        if c is None:
            return select(k)
        if n_tp == 2:
            grad_specs = [pl.BlockSpec((INNER * rows, share), lambda j: (0, ff // share))] * 2
        else:
            grad_specs = [fixed((INNER * rows, ff))]
        came = (2 if doubled(going[c]) else 1) * rows
        sent = (2 if doubled(k) else 1) * rows
        there = [arrived[s] for s in chunks[f]] if f is not None else []
        made = pl.pallas_call(
            functools.partial(
                back_kernel,
                *sizes,
                len(sums[c]),
                len(grads[c]),
                topk,
                share,
                doubled(going[c]),
                len(there),
            ),
            out_shape=[block((sent, width))] * INNER
            + [block((hots, ff)), block((colds, ff))]
            + [block((count, INNER * rows))] * len(there),
            grid=(feat // d_tile,),
            in_specs=[smem]
            + [fixed((INNER * rows, ff))] * len(sums[c])
            + grad_specs
            + [pl.BlockSpec((came, TAIL), lambda j: (0, width // TAIL - 1))] * INNER
            + [pl.BlockSpec((2, d_tile, ff), lambda j: (0, j, 0))]
            + [fixed((count, width))] * len(there)
            + [rest_spec],
            out_specs=[fixed((sent, width))] * INNER
            + [fixed((hots, ff)), fixed((colds, ff))]
            + [fixed((count, INNER * rows))] * len(there),
            compiler_params=params(),
            cost_estimate=weigh("b"),
            name="back",
        )(info, *sums[c], *grads[c], *blocks[going[c]], up_weight, *there, last[0])
        g_hots[c], g_colds[c] = made[INNER : INNER + 2]
        if f is not None:
            picks[f] = made[INNER + 2 :]
        exchange(k, made)
        last[0] = g_colds[c]

    def expand(c):
        more = [along(partials[s - m], m) for s in chunks[c]] if c > 1 else []
        k = coming[c]
        made = pl.pallas_call(
            functools.partial(expand_kernel, m, m * hot_rows, doubled(k), len(more)),
            out_shape=[block((count, width))] * m,
            in_specs=whole_specs(INNER + m + len(more)) + [rest_spec],
            out_specs=whole_specs(m),
            compiler_params=params(),
            cost_estimate=weigh("e"),
            name="expand",
        )(*blocks[k], *picks[c], *more, last[0])
        for s, value in zip(chunks[c], made):
            partials[s] = value
        last[0] = made[0]

    def weight_grad():
        grad_up = pl.pallas_call(
            functools.partial(up_kernel, n),
            out_shape=block(up_weight.shape),
            grid_spec=pltpu.PrefetchScalarGridSpec(
                num_scalar_prefetch=1,
                grid=(2, feat // 256),
                in_specs=[pl.BlockSpec((hots, 256), lambda e, j, info: (0, j))] * n
                + [pl.BlockSpec((colds, 256), lambda e, j, info: (0, j))] * n
                + [pl.BlockSpec((hots, ff), lambda e, j, info: (0, 0))] * n
                + [pl.BlockSpec((colds, ff), lambda e, j, info: (0, 0))] * n
                + [rest_spec],
                out_specs=pl.BlockSpec(
                    (1, 256, ff),
                    lambda e, j, info: (e + hot_of(info, info[0]) * (1 - 2 * e), j, 0),
                ),
            ),
            compiler_params=params(),
            cost_estimate=weigh("u"),
            name="grad_up",
        )(
            info,
            *[x_hots[c] for c in range(n)],
            *[x_colds[c] for c in range(n)],
            *[g_hots[c] for c in range(n)],
            *[g_colds[c] for c in range(n)],
            last[0],
        )
        last[0] = grad_up
        return grad_up

    if own_rows:
        picks[0] = made[INNER + 1 :]
        exchange(0, made[1 : INNER + 1])
    else:
        select(0)
    grad_up = None
    for word in ORDER:
        number = int(word[1:] or 0)
        if word[0] == "u":
            grad_up = weight_grad()
        else:
            {"x": step, "h": hidden, "e": expand}[word[0]](number)

    sums_back = [along(partials[s], m) for s in chunks[n - 1]]
    parts = [sums_back[0], partials[0]]
    for s in chunks[0][1:]:
        parts.append(along(sums_back[s] + partials[s], outer - s))
    mixed, grad_tokens, grad_gates = pl.pallas_call(
        functools.partial(final_kernel, len(parts), topk),
        out_shape=[block((count, share)), block((count, feat)), block((topk, count), F32)],
        in_specs=whole_specs(len(parts)),
        out_specs=whole_specs(3),
        compiler_params=params(),
        cost_estimate=weigh("e"),
        name="final",
    )(*parts)
    return mixed, grad_tokens, grad_gates.T, grad_up


def solution(mesh):
    return jax.shard_map(
        on_device,
        mesh=mesh,
        in_specs=(
            P("ep", "tp"),
            P("ep", None),
            P("ep", None),
            P("ep", "tp", None),
            P(),
            P("ep", "tp"),
        ),
        out_specs=(P("ep", "tp"), P("ep", "tp"), P("ep", None), P("ep", "tp", None)),
        check_vma=False,
    )
```

```python
import functools

import jax
import jax.numpy as jnp
from jax import lax
from jax.experimental import pallas as pl
from jax.experimental.pallas import tpu as pltpu
from jax.sharding import PartitionSpec as P

INNER = 4
CHUNKS = 4
PLAN = ((0, None), (1, None), (2, None), (3, None), (None, 1), (None, 2), (None, 3), (None, 0))
ORDER = ('x1', 'h0', 'x2', 'h1', 'x3', 'h2', 'x4', 'h3', 'e1', 'x5', 'x6', 'e2', 'x7', 'e3', 'u', 'e0')
PASSED = ()
FIRST = 0
COSTS = {'x': 5000, 'b': 100, 'h': 5000, 'e': 20000, 'u': 20000}
TAIL = 128
LIMIT = 20 * 1024 * 1024
WIDE = 56 * 1024 * 1024
F32, BF16, I32 = jnp.float32, jnp.bfloat16, jnp.int32


def params(limit=LIMIT):
    return pltpu.CompilerParams(vmem_limit_bytes=limit)


def cost(flops, moved):
    return pl.CostEstimate(flops=int(flops), bytes_accessed=int(moved), transcendentals=0)


def whole_specs(n):
    return [pl.BlockSpec(memory_space=pltpu.VMEM)] * n


def hot_of(plan, device):
    return plan[2 * device + 1]


def rows_joined(pieces):
    if all(piece.shape[0] % 16 == 0 for piece in pieces):
        return jnp.concatenate(pieces, 0)
    return jnp.concatenate([piece.astype(F32) for piece in pieces], 0).astype(BF16)


def pick_rows(m, hot_rows, cold_rows, topk, plan, tails):
    count = tails[0].shape[0]
    rows = m * (hot_rows + cold_rows)
    cols = INNER * rows
    me = lax.axis_index("ep")
    outer, inner = me // INNER, me % INNER
    spot = lax.broadcasted_iota(I32, (8, cols), 1)
    which = jnp.zeros((8, cols), I32)
    for d in range(1, INNER):
        which += (spot >= d * rows).astype(I32)
    within = spot - which * rows
    is_hot = within < m * hot_rows
    group = jnp.zeros((8, cols), I32)
    for s in range(1, m):
        edge = jnp.where(is_hot, s * hot_rows, m * hot_rows + s * cold_rows)
        group += (within >= edge).astype(I32)
    slot = jnp.where(is_hot, within - group * hot_rows, within - m * hot_rows - group * cold_rows)
    expert = jnp.zeros((8, cols), I32)
    for d in range(INNER):
        device = outer * INNER + (inner ^ d)
        hot = hot_of(plan, device)
        ids = jnp.where(is_hot, 2 * device + hot, 2 * device + 1 - hot)
        expert = jnp.where(which == d, ids, expert)
    expert = expert.astype(F32)[0:1]
    slot = slot.astype(F32)[0:1]
    group = group[0:1]
    before = lax.broadcasted_iota(I32, (count, count), 1) < lax.broadcasted_iota(I32, (count, count), 0)
    before = jnp.where(before, 1.0, 0.0).astype(BF16)
    found = []
    for s, ids in enumerate(tails):
        match = ids[:, 0:1] == expert
        for k in range(1, topk):
            match = match | (ids[:, k : k + 1] == expert)
        ones = jnp.where(match, 1.0, 0.0)
        rank = jnp.dot(before, ones.astype(BF16), preferred_element_type=F32)
        found.append(jnp.where((rank == slot) & (group == s), ones, 0.0).astype(BF16))
    return found


def picked(picks, payloads, columns):
    total = None
    for pick, payload in zip(picks, payloads):
        part = lax.dot_general(
            pick[...], payload[:, columns], (((0,), (0,)), ((), ())), preferred_element_type=F32
        )
        total = part if total is None else total + part
    return total


def select_all(picks, payloads, outs):
    rows, width = outs[0].shape
    step = 384 if width % 384 == 0 else 128
    for at in range(0, width, step):
        columns = slice(at, at + step)
        total = picked(picks, payloads, columns)
        for d in range(INNER):
            outs[d][:, columns] = total[d * rows : (d + 1) * rows].astype(BF16)


def start_kernel(m, hot_rows, cold_rows, plan, tokens, routes, gates, grad_out, *refs):
    out, refs = refs[0], refs[1:]
    here_routes, here_gates, sems = refs[-3:]
    outs, picks = refs[:INNER], refs[INNER:-3]
    count, feat = tokens.shape
    share = grad_out.shape[1]
    topk = routes.shape[0]
    copies = [
        pltpu.make_async_copy(source, target, sems.at[n])
        for n, (source, target) in enumerate(
            (
                (routes, here_routes),
                (gates, here_gates),
                (tokens, out.at[:, :feat]),
                (grad_out, out.at[:, feat : feat + share]),
            )
        )
    ]
    for copy in copies:
        copy.start()
    for copy in copies[:2]:
        copy.wait()
    ids = here_routes[...].astype(F32)
    gate = here_gates[...]
    high = gate.astype(BF16).astype(F32)
    middle = (gate - high).astype(BF16).astype(F32)
    low = (gate - high - middle).astype(BF16).astype(F32)
    rest = jnp.zeros((TAIL - 5 * topk, count), F32)
    tail = jnp.concatenate([ids, ids, high, middle, low, rest], 0).T
    out[:, feat + share :] = tail.astype(BF16)
    if picks:
        picks[0][...] = pick_rows(m, hot_rows, cold_rows, topk, plan, [tail])[0]
    for copy in copies[2:]:
        copy.wait()
    if picks:
        select_all(picks, [out], outs)


def select_kernel(m, hot_rows, cold_rows, topk, waits, plan, *refs):
    payloads, refs = refs[:m], refs[m + waits :]
    outs, picks, passed = refs[:INNER], refs[INNER : INNER + m], refs[INNER + m :]
    width = payloads[0].shape[1]
    for source, target in zip(payloads, passed):
        target[...] = source[...]
    tails = [payload[:, width - TAIL :].astype(F32) for payload in payloads]
    for pick, found in zip(picks, pick_rows(m, hot_rows, cold_rows, topk, plan, tails)):
        pick[...] = found
    select_all(picks, payloads, outs)


def forward_rows(block, both, hots, columns):
    if not both:
        return block[:hots, columns], block[hots:, columns]
    colds = block.shape[0] // 2 - hots
    return block[:hots, columns], block[2 * hots : 2 * hots + colds, columns]


def returned_rows(block, both, hots, columns):
    if not both:
        return block[:, columns]
    colds = block.shape[0] // 2 - hots
    cold = block[2 * hots :, columns].astype(F32)[colds:]
    return jnp.concatenate([block[hots : 2 * hots, columns].astype(F32), cold], 0)


def hidden_kernel(m, hot_rows, cold_rows, feat, both, streamed, plan, *refs):
    blocks = refs[:INNER]
    weight, _, part, x_hot, x_cold = refs[INNER:]
    hots = INNER * m * hot_rows
    share = blocks[0].shape[1] - feat - TAIL
    ff = part.shape[1] - share
    tile = 256 if ff % 256 == 0 else ff
    hot = hot_of(plan, lax.axis_index("ep"))
    split = m * hot_rows

    def gather():
        rows = [forward_rows(b, both, split, slice(0, feat)) for b in blocks]
        x_hot[...] = rows_joined([hot_part for hot_part, _ in rows])
        x_cold[...] = rows_joined([cold_part for _, cold_part in rows])
        rows = [forward_rows(b, both, split, slice(feat, feat + share)) for b in blocks]
        part[:hots, ff:] = rows_joined([hot_part for hot_part, _ in rows])
        part[hots:, ff:] = rows_joined([cold_part for _, cold_part in rows])

    def columns(j, source):
        at = pl.ds(pl.multiple_of(j * tile, tile), tile)
        part[:hots, at] = jnp.dot(
            x_hot[...], weight[hot, :, source], preferred_element_type=F32
        ).astype(BF16)
        part[hots:, at] = jnp.dot(
            x_cold[...], weight[1 - hot, :, source], preferred_element_type=F32
        ).astype(BF16)

    if streamed:
        pl.when(pl.program_id(0) == 0)(gather)
        columns(pl.program_id(0), slice(None))
    else:
        gather()

        @pl.loop(0, ff // tile)
        def _(j):
            columns(j, pl.ds(pl.multiple_of(j * tile, tile), tile))


def back_kernel(m, hot_rows, cold_rows, n_parts, n_grads, topk, share, both, n_pay, plan, *refs):
    sums, grads = refs[:n_parts], refs[n_parts : n_parts + n_grads]
    refs = refs[n_parts + n_grads :]
    tails, weight, payloads = refs[:INNER], refs[INNER], refs[INNER + 1 : INNER + 1 + n_pay]
    refs = refs[INNER + 2 + n_pay :]
    outs, g_hot, g_cold, picks = refs[:INNER], refs[INNER], refs[INNER + 1], refs[INNER + 2 :]
    hots, colds = m * hot_rows, m * cold_rows
    rows = hots + colds
    ff = weight.shape[2]
    width = outs[0].shape[1]
    feat = width - share - TAIL
    tile = 512 if feat % 512 == 0 else feat
    me, tp = lax.axis_index("ep"), lax.axis_index("tp")
    hot = hot_of(plan, me)

    def put(columns, back_hot, back_cold):
        there = picked(picks, payloads, columns) if n_pay else None
        for d in range(INNER):
            hot_now = back_hot[d * hots : (d + 1) * hots]
            cold_now = back_cold[d * colds : (d + 1) * colds]
            if n_pay:
                mine = there[d * rows : (d + 1) * rows]
                outs[d][:hots, columns] = mine[:hots].astype(BF16)
                outs[d][hots : 2 * hots, columns] = hot_now.astype(BF16)
                outs[d][2 * hots :, columns] = jnp.concatenate([mine[hots:], cold_now], 0).astype(BF16)
            else:
                outs[d][:hots, columns] = hot_now.astype(BF16)
                outs[d][hots:, columns] = cold_now.astype(BF16)

    if n_pay:
        ids = [payload[:, width - TAIL :].astype(F32) for payload in payloads]
        for pick, found in zip(picks, pick_rows(m, hot_rows, cold_rows, topk, plan, ids)):
            pick[...] = found
    tail_rows = [forward_rows(t, both, hots, slice(width - TAIL, width)) for t in tails]
    ends = []
    for kind, first, piece, target, expert in (
        (0, 0, hots, g_hot, 2 * me + hot),
        (1, INNER * hots, colds, g_cold, 2 * me + 1 - hot),
    ):
        made = []
        per = 1 if piece % 16 == 0 else INNER
        for d in range(0, INNER, per):
            count = piece * per
            now = slice(first + d * piece, first + d * piece + count)
            tail = jnp.concatenate([t[kind].astype(F32) for t in tail_rows[d : d + per]], 0)
            hidden = sums[0][now, :ff].astype(F32)
            for more in sums[1:]:
                hidden = hidden + more[now, :ff].astype(F32)
            if n_grads == 1:
                grad = grads[0][now].astype(F32)
            else:
                mine, other = (g[now, ff:].astype(F32) for g in grads)
                even = tp == 0
                grad = jnp.concatenate(
                    [jnp.where(even, mine, other), jnp.where(even, other, mine)], 1
                )
            e = expert.astype(F32)
            ids = tail[:, :topk]
            gate = (tail[:, 2 * topk : 3 * topk] + tail[:, 3 * topk : 4 * topk]) + tail[:, 4 * topk : 5 * topk]
            gate = jnp.sum(jnp.where(ids == e, gate, 0.0), 1, keepdims=True)
            sig = 1.0 / (1.0 + jnp.exp(-hidden))
            act = (hidden * sig).astype(BF16).astype(F32)
            row_grad = (gate * grad).astype(BF16).astype(F32)
            hidden_grad = row_grad * (sig * (1.0 + hidden * (1.0 - sig)))
            target[d * piece : d * piece + count] = hidden_grad.astype(BF16)
            gate_grad = jnp.sum(act * grad, 1, keepdims=True)
            high = gate_grad.astype(BF16).astype(F32)
            low = gate_grad - high
            lane = lax.broadcasted_iota(I32, tail.shape, 1)
            values = jnp.where(lane < topk, high, low)
            end = jnp.where((tail == e) & (lane < 2 * topk), values, 0.0)
            gated = None
            for n in range(ff // share):
                piece_act = jnp.where(tp == n, act[:, n * share : (n + 1) * share], 0.0)
                gated = piece_act if gated is None else gated + piece_act
            made.append(jnp.concatenate([gate * gated, end], 1))
        ends.append(jnp.concatenate(made, 0))
    put(slice(feat, width), *ends)

    across_rows = (((1,), (1,)), ((), ()))

    def features(j, carry):
        at = pl.ds(pl.multiple_of(j * tile, tile), tile)
        put(
            at,
            lax.dot_general(
                g_hot[...], weight[hot, at, :], across_rows, preferred_element_type=F32
            ),
            lax.dot_general(
                g_cold[...], weight[1 - hot, at, :], across_rows, preferred_element_type=F32
            ),
        )
        return carry

    lax.fori_loop(0, feat // tile, features, 0)


def expand_kernel(m, hots, both, n_more, *refs):
    blocks, picks, refs = refs[:INNER], refs[INNER : INNER + m], refs[INNER + m :]
    more, outs = refs[:n_more], refs[n_more + 1 :]
    width = blocks[0].shape[1]
    step = 384 if width % 384 == 0 else 128
    for at in range(0, width, step):
        columns = slice(at, at + step)
        rows = rows_joined([returned_rows(b, both, hots, columns) for b in blocks]).astype(BF16)
        for s in range(m):
            total = jnp.dot(picks[s][...], rows, preferred_element_type=F32)
            if more:
                total = total + more[s][:, columns].astype(F32)
            outs[s][:, columns] = total.astype(BF16)


def final_kernel(n, topk, *refs):
    parts = refs[:n]
    mixed, grad_tokens, grad_gates = refs[n:]
    feat, share = grad_tokens.shape[1], mixed.shape[1]

    def total(columns):
        out = parts[0][:, columns].astype(F32)
        for part in parts[1:]:
            out = out + part[:, columns].astype(F32)
        return out

    grad_tokens[...] = total(slice(0, feat)).astype(BF16)
    mixed[...] = total(slice(feat, feat + share)).astype(BF16)
    tail = total(slice(feat + share, feat + share + TAIL))
    tail = tail.T
    grad_gates[...] = tail[:topk] + tail[topk : 2 * topk]


def up_kernel(n, plan, *refs):
    x_hot, x_cold = refs[:n], refs[n : 2 * n]
    g_hot, g_cold = refs[2 * n : 3 * n], refs[3 * n : 4 * n]
    out, token, all_hot, all_cold = refs[4 * n + 1 :]
    tile = out.shape[1]
    e, j = pl.program_id(0), pl.program_id(1)
    hot = hot_of(plan, lax.axis_index("ep"))
    at = pl.ds(pl.multiple_of(j * tile, tile), tile)

    @pl.when((e == 0) & (j == 0))
    def _():
        token[...] = jnp.zeros_like(token)
        all_hot[...] = jnp.concatenate([g[...] for g in g_hot], 0)
        all_cold[...] = jnp.concatenate([g[...] for g in g_cold], 0)

    def total(xs, grads):
        rows = jnp.concatenate([x[:, at] for x in xs], 0)
        out[0] = lax.dot_general(
            rows, grads[...], (((0,), (0,)), ((), ())), preferred_element_type=F32
        ).astype(BF16)

    pl.when(e == hot)(lambda: total(x_hot, all_hot))
    pl.when(e != hot)(lambda: total(x_cold, all_cold))


def on_device(tokens, routes, gates, up_weight, replica_on, grad_out):
    count, feat = tokens.shape
    topk = routes.shape[1]
    experts = replica_on.shape[0]
    share = grad_out.shape[1]
    ff = up_weight.shape[2]
    n_ep, n_tp = lax.axis_size("ep"), lax.axis_size("tp")
    outer = n_ep // INNER
    capacity = 3 * count * topk // (4 * experts)
    hot_rows, cold_rows = 2 * capacity, capacity
    width = feat + share + TAIL
    smem = pl.BlockSpec(memory_space=pltpu.SMEM)

    def along(value, shift):
        pairs = [
            (o * INNER + i, ((o + shift) % outer) * INNER + i)
            for o in range(outer)
            for i in range(INNER)
        ]
        return lax.ppermute(value, "ep", pairs)

    def across(value, d):
        pairs = [(o * INNER + i, o * INNER + (i ^ d)) for o in range(outer) for i in range(INNER)]
        return lax.ppermute(value, "ep", pairs)

    rest_spec = pl.BlockSpec(memory_space=pl.ANY)
    m = max(1, outer // CHUNKS)
    chunks = [list(range(first, first + m)) for first in range(0, outer, m)]
    n = len(chunks)
    rows = m * (hot_rows + cold_rows)
    hots, colds = INNER * m * hot_rows, INNER * m * cold_rows
    sizes = (m, hot_rows, cold_rows)

    def block(shape, dtype=BF16):
        return jax.ShapeDtypeStruct(shape, dtype)

    def fixed(shape):
        return pl.BlockSpec(shape, lambda j: (0,) * len(shape))

    going = {f: k for k, (f, _) in enumerate(PLAN) if f is not None}
    coming = {r: k for k, (_, r) in enumerate(PLAN) if r is not None}

    def doubled(k):
        return None not in PLAN[k]

    def weigh(kind):
        return cost(COSTS[kind] * 10**6, COSTS[kind] * 10**4)

    arrived, picks, blocks, sums, grads, partials = {}, {}, {}, {}, {}, {}
    x_hots, x_colds, g_hots, g_colds = {}, {}, {}, {}

    def exchange(k, made):
        blocks[k] = [made[0]] + [across(made[d], d) for d in range(1, INNER)]

    own_rows = m == 1
    made = pl.pallas_call(
        functools.partial(start_kernel, *sizes),
        out_shape=[block((count, width))]
        + ([block((rows, width))] * INNER + [block((count, INNER * rows))] if own_rows else []),
        in_specs=[smem] + [rest_spec] * 4,
        out_specs=whole_specs(1 + (INNER + 1 if own_rows else 0)),
        scratch_shapes=[
            pltpu.VMEM((topk, count), I32),
            pltpu.VMEM((topk, count), F32),
            pltpu.SemaphoreType.DMA((4,)),
        ],
        compiler_params=params(WIDE),
        cost_estimate=weigh("x"),
        name="start",
    )(replica_on, tokens, routes.T, gates.T, grad_out)
    payload = made[0]
    last = []
    for c in range(n):
        for s in chunks[c] if c not in PASSED else ():
            if s == 0:
                arrived[s] = payload
            else:
                arrived[s] = along(arrived[s - m], m) if c else along(payload, s)

    def select(k):
        c = PLAN[k][0]
        more = m if c + 1 in PASSED else 0
        made = pl.pallas_call(
            functools.partial(select_kernel, *sizes, topk, len(last)),
            out_shape=[block((rows, width))] * INNER
            + [block((count, INNER * rows))] * m
            + [block((count, width))] * more,
            in_specs=[smem] + whole_specs(m) + [rest_spec] * len(last),
            out_specs=whole_specs(INNER + m + more),
            compiler_params=params(),
            cost_estimate=weigh("x"),
            name="select",
        )(replica_on, *[arrived[s] for s in chunks[c]], *last)
        picks[c] = made[INNER : INNER + m]
        exchange(k, made)
        if more:
            for s, value in zip(chunks[c + 1], made[INNER + m :]):
                arrived[s] = along(value, m)
        last[:] = [picks[c][0]]

    def hidden(c):
        k = going[c]
        tile = 256 if ff % 256 == 0 else ff
        shapes = [(INNER * rows, ff + share), (hots, feat), (colds, feat)]
        streamed = c == 0 and FIRST > 0
        if streamed:
            where = dict(
                grid=(ff // tile,),
                in_specs=[smem]
                + [fixed(b.shape) for b in blocks[k]]
                + [pl.BlockSpec((2, feat, tile), lambda j: (0, 0, j)), rest_spec],
                out_specs=[fixed(shape) for shape in shapes],
            )
        else:
            where = dict(
                in_specs=[smem] + whole_specs(INNER + 1) + [rest_spec],
                out_specs=whole_specs(3),
            )
        part, x_hots[c], x_colds[c] = pl.pallas_call(
            functools.partial(hidden_kernel, *sizes, feat, doubled(k), streamed),
            out_shape=[block(shape) for shape in shapes],
            **where,
            compiler_params=params(WIDE if c == 0 and FIRST == 2 else LIMIT),
            cost_estimate=weigh("h"),
            name="hidden",
        )(replica_on, *blocks[k], up_weight, last[0])
        last[0] = x_colds[c]
        if n_tp == 2:
            sums[c] = [part, lax.ppermute(part, "tp", [(0, 1), (1, 0)])]
            grads[c] = sums[c]
        else:
            sums[c] = [lax.psum(part[:, :ff].astype(F32), "tp")]
            grads[c] = [lax.all_gather(part[:, ff:], "tp", axis=1, tiled=True)]

    def step(k):
        f, c = PLAN[k]
        if c is None:
            return select(k)
        sent = (2 if doubled(k) else 1) * rows
        there = [arrived[s] for s in chunks[f]] if f is not None else []
        made = pl.pallas_call(
            functools.partial(
                back_kernel,
                *sizes,
                len(sums[c]),
                len(grads[c]),
                topk,
                share,
                doubled(going[c]),
                len(there),
            ),
            out_shape=[block((sent, width))] * INNER
            + [block((hots, ff)), block((colds, ff))]
            + [block((count, INNER * rows))] * len(there),
            in_specs=[smem]
            + whole_specs(len(sums[c]) + len(grads[c]) + INNER + 1 + len(there))
            + [rest_spec],
            out_specs=whole_specs(INNER + 2 + len(there)),
            compiler_params=params(),
            cost_estimate=weigh("b"),
            name="back",
        )(replica_on, *sums[c], *grads[c], *blocks[going[c]], up_weight, *there, last[0])
        g_hots[c], g_colds[c] = made[INNER : INNER + 2]
        if f is not None:
            picks[f] = made[INNER + 2 :]
        exchange(k, made)
        last[0] = g_colds[c]

    def expand(c):
        more = [along(partials[s - m], m) for s in chunks[c]] if c > 1 else []
        k = coming[c]
        made = pl.pallas_call(
            functools.partial(expand_kernel, m, m * hot_rows, doubled(k), len(more)),
            out_shape=[block((count, width))] * m,
            in_specs=whole_specs(INNER + m + len(more)) + [rest_spec],
            out_specs=whole_specs(m),
            compiler_params=params(),
            cost_estimate=weigh("e"),
            name="expand",
        )(*blocks[k], *picks[c], *more, last[0])
        for s, value in zip(chunks[c], made):
            partials[s] = value
        last[0] = made[0]

    def weight_grad():
        tile = 512 if feat % 512 == 0 else feat
        grad_up, token = pl.pallas_call(
            functools.partial(up_kernel, n),
            out_shape=[block(up_weight.shape), block((8, 128), F32)],
            grid=(up_weight.shape[0], feat // tile),
            in_specs=[smem] + whole_specs(4 * n) + [rest_spec],
            out_specs=[
                pl.BlockSpec((1, tile, ff), lambda e, j: (e, j, 0)),
                pl.BlockSpec((8, 128), lambda e, j: (0, 0)),
            ],
            scratch_shapes=[
                pltpu.VMEM((n * hots, ff), BF16),
                pltpu.VMEM((n * colds, ff), BF16),
            ],
            compiler_params=params(),
            cost_estimate=weigh("u"),
            name="grad_up",
        )(
            replica_on,
            *[x_hots[c] for c in range(n)],
            *[x_colds[c] for c in range(n)],
            *[g_hots[c] for c in range(n)],
            *[g_colds[c] for c in range(n)],
            last[0],
        )
        last[0] = token
        return grad_up

    if own_rows:
        picks[0] = made[INNER + 1 :]
        exchange(0, made[1 : INNER + 1])
    else:
        select(0)
    grad_up = None
    for word in ORDER:
        number = int(word[1:] or 0)
        if word[0] == "u":
            grad_up = weight_grad()
        else:
            {"x": step, "h": hidden, "e": expand}[word[0]](number)

    sums_back = [along(partials[s], m) for s in chunks[n - 1]]
    parts = [sums_back[0], partials[0]]
    for s in chunks[0][1:]:
        parts.append(along(sums_back[s] + partials[s], outer - s))
    mixed, grad_tokens, grad_gates = pl.pallas_call(
        functools.partial(final_kernel, len(parts), topk),
        out_shape=[block((count, share)), block((count, feat)), block((topk, count), F32)],
        in_specs=whole_specs(len(parts)),
        out_specs=whole_specs(3),
        compiler_params=params(),
        cost_estimate=weigh("e"),
        name="final",
    )(*parts)
    return mixed, grad_tokens, grad_gates.T, grad_up


def solution(mesh):
    return jax.shard_map(
        on_device,
        mesh=mesh,
        in_specs=(
            P("ep", "tp"),
            P("ep", None),
            P("ep", None),
            P("ep", "tp", None),
            P(),
            P("ep", "tp"),
        ),
        out_specs=(P("ep", "tp"), P("ep", "tp"), P("ep", None), P("ep", "tp", None)),
        check_vma=False,
    )
```

```python
import functools

import jax
import jax.numpy as jnp
from jax import lax
from jax.experimental import pallas as pl
from jax.experimental.pallas import tpu as pltpu
from jax.sharding import PartitionSpec as P

INNER = 4
CHUNKS = 4
PLAN = ((0, None), (1, None), (2, None), (3, None), (None, 1), (None, 2), (None, 3), (None, 0))
ORDER = ('x1', 'h0', 'x2', 'h1', 'x3', 'h2', 'r0', 'x4', 'h3', 'x5', 'r3', 'e1', 'x6', 'e2', 'r2', 'x7', 'e3', 'u', 'e0')
PASSED = ()
FIRST = 1
COSTS = {'x': 5000, 'b': 20000, 'h': 5000, 'e': 1, 'u': 20000}
TAIL = 128
LIMIT = 20 * 1024 * 1024
WIDE = 56 * 1024 * 1024
F32, BF16, I32 = jnp.float32, jnp.bfloat16, jnp.int32


def params(limit=LIMIT):
    return pltpu.CompilerParams(vmem_limit_bytes=limit)


def cost(flops, moved):
    return pl.CostEstimate(flops=int(flops), bytes_accessed=int(moved), transcendentals=0)


def whole_specs(n):
    return [pl.BlockSpec(memory_space=pltpu.VMEM)] * n


def hot_of(plan, device):
    return plan[2 * device + 1]


def rows_joined(pieces):
    if all(piece.shape[0] % 16 == 0 for piece in pieces):
        return jnp.concatenate(pieces, 0)
    return jnp.concatenate([piece.astype(F32) for piece in pieces], 0).astype(BF16)


def row_plan(m, hot_rows, cold_rows, plan, shape, axis):
    rows = m * (hot_rows + cold_rows)
    me = lax.axis_index("ep")
    outer, inner = me // INNER, me % INNER
    spot = lax.broadcasted_iota(I32, shape, axis)
    which = jnp.zeros(shape, I32)
    for d in range(1, INNER):
        which += (spot >= d * rows).astype(I32)
    within = spot - which * rows
    is_hot = within < m * hot_rows
    group = jnp.zeros(shape, I32)
    for s in range(1, m):
        edge = jnp.where(is_hot, s * hot_rows, m * hot_rows + s * cold_rows)
        group += (within >= edge).astype(I32)
    slot = jnp.where(is_hot, within - group * hot_rows, within - m * hot_rows - group * cold_rows)
    expert = jnp.zeros(shape, I32)
    for d in range(INNER):
        device = outer * INNER + (inner ^ d)
        hot = hot_of(plan, device)
        ids = jnp.where(is_hot, 2 * device + hot, 2 * device + 1 - hot)
        expert = jnp.where(which == d, ids, expert)
    return expert.astype(F32), slot.astype(F32), group


def pick_rows(m, hot_rows, cold_rows, topk, plan, tails):
    count = tails[0].shape[0]
    cols = INNER * m * (hot_rows + cold_rows)
    expert, slot, group = (
        value[0:1] for value in row_plan(m, hot_rows, cold_rows, plan, (8, cols), 1)
    )
    before = lax.broadcasted_iota(I32, (count, count), 1) < lax.broadcasted_iota(I32, (count, count), 0)
    before = jnp.where(before, 1.0, 0.0).astype(BF16)
    found = []
    for s, ids in enumerate(tails):
        match = ids[:, 0:1] == expert
        for k in range(1, topk):
            match = match | (ids[:, k : k + 1] == expert)
        ones = jnp.where(match, 1.0, 0.0)
        rank = jnp.dot(before, ones.astype(BF16), preferred_element_type=F32)
        found.append(jnp.where((rank == slot) & (group == s), ones, 0.0).astype(BF16))
    return found


def picked(picks, payloads, columns):
    total = None
    for pick, payload in zip(picks, payloads):
        part = lax.dot_general(
            pick[...], payload[:, columns], (((0,), (0,)), ((), ())), preferred_element_type=F32
        )
        total = part if total is None else total + part
    return total


def select_all(m, hot_rows, cold_rows, topk, share, plan, picks, payloads, outs, marks):
    rows, width = outs[0].shape
    feat = width - share
    expert, _, _ = row_plan(m, hot_rows, cold_rows, plan, (INNER * rows, TAIL), 0)
    tail = picked(picks, payloads, slice(width, width + TAIL))
    gate = (tail[:, 2 * topk : 3 * topk] + tail[:, 3 * topk : 4 * topk]) + tail[:, 4 * topk : 5 * topk]
    gate = jnp.sum(jnp.where(tail[:, :topk] == expert[:, :topk], gate, 0.0), 1, keepdims=True)
    lane = lax.broadcasted_iota(I32, tail.shape, 1)
    own = jnp.where((tail == expert) & (lane < 2 * topk), 1.0, 0.0)
    marks[...] = jnp.where(lane == 2 * topk, gate, own)
    step = 512 if feat % 512 == 0 else 128
    for at in [*range(0, feat, step), feat]:
        columns = slice(at, at + step) if at < feat else slice(feat, width)
        total = picked(picks, payloads, columns)
        if at == feat:
            total = gate * total
        for d in range(INNER):
            outs[d][:, columns] = total[d * rows : (d + 1) * rows].astype(BF16)


def start_kernel(m, hot_rows, cold_rows, plan, tokens, routes, gates, grad_out, *refs):
    out, refs = refs[0], refs[1:]
    here_routes, here_gates, sems = refs[-3:]
    outs, marks, picks = refs[:INNER], refs[INNER:-3][:1], refs[INNER:-3][1:]
    count, feat = tokens.shape
    share = grad_out.shape[1]
    topk = routes.shape[0]
    copies = [
        pltpu.make_async_copy(source, target, sems.at[n])
        for n, (source, target) in enumerate(
            (
                (routes, here_routes),
                (gates, here_gates),
                (tokens, out.at[:, :feat]),
                (grad_out, out.at[:, feat : feat + share]),
            )
        )
    ]
    for copy in copies:
        copy.start()
    for copy in copies[:2]:
        copy.wait()
    ids = here_routes[...].astype(F32)
    gate = here_gates[...]
    high = gate.astype(BF16).astype(F32)
    middle = (gate - high).astype(BF16).astype(F32)
    low = (gate - high - middle).astype(BF16).astype(F32)
    rest = jnp.zeros((TAIL - 5 * topk, count), F32)
    tail = jnp.concatenate([ids, ids, high, middle, low, rest], 0).T
    out[:, feat + share :] = tail.astype(BF16)
    if picks:
        picks[0][...] = pick_rows(m, hot_rows, cold_rows, topk, plan, [tail])[0]
    for copy in copies[2:]:
        copy.wait()
    if picks:
        select_all(m, hot_rows, cold_rows, topk, share, plan, picks, [out], outs, marks[0])


def select_kernel(m, hot_rows, cold_rows, topk, share, waits, plan, *refs):
    payloads, refs = refs[:m], refs[m + waits :]
    outs, marks, picks, passed = refs[:INNER], refs[INNER], refs[INNER + 1 : INNER + 1 + m], refs[INNER + 1 + m :]
    width = payloads[0].shape[1]
    for source, target in zip(payloads, passed):
        target[...] = source[...]
    tails = [payload[:, width - TAIL :].astype(F32) for payload in payloads]
    for pick, found in zip(picks, pick_rows(m, hot_rows, cold_rows, topk, plan, tails)):
        pick[...] = found
    select_all(m, hot_rows, cold_rows, topk, share, plan, picks, payloads, outs, marks)


def hidden_kernel(m, hot_rows, cold_rows, feat, streamed, waits, plan, *refs):
    blocks = refs[:INNER]
    weight, part, x_hot, x_cold = refs[INNER], *refs[INNER + 1 + waits :]
    hots = INNER * m * hot_rows
    share = blocks[0].shape[1] - feat
    ff = part.shape[1] - share
    tile = 256 if ff % 256 == 0 else ff
    hot = hot_of(plan, lax.axis_index("ep"))
    split = m * hot_rows

    def gather():
        x_hot[...] = rows_joined([b[:split, :feat] for b in blocks])
        x_cold[...] = rows_joined([b[split:, :feat] for b in blocks])
        part[:hots, ff:] = rows_joined([b[:split, feat:] for b in blocks])
        part[hots:, ff:] = rows_joined([b[split:, feat:] for b in blocks])

    def columns(j, source):
        at = pl.ds(pl.multiple_of(j * tile, tile), tile)
        part[:hots, at] = jnp.dot(
            x_hot[...], weight[hot, :, source], preferred_element_type=F32
        ).astype(BF16)
        part[hots:, at] = jnp.dot(
            x_cold[...], weight[1 - hot, :, source], preferred_element_type=F32
        ).astype(BF16)

    if streamed:
        pl.when(pl.program_id(0) == 0)(gather)
        columns(pl.program_id(0), slice(None))
    else:
        gather()

        @pl.loop(0, ff // tile)
        def _(j):
            columns(j, pl.ds(pl.multiple_of(j * tile, tile), tile))


def back_kernel(m, hot_rows, cold_rows, n_parts, n_grads, share, waits, plan, *refs):
    sums, grads = refs[:n_parts], refs[n_parts : n_parts + n_grads]
    weight, refs = refs[n_parts + n_grads], refs[n_parts + n_grads + 1 + waits :]
    outs, g_hot, g_cold = refs[:INNER], refs[INNER], refs[INNER + 1]
    hots, colds = m * hot_rows, m * cold_rows
    ff = weight.shape[2]
    width = outs[0].shape[1]
    feat = width - share - TAIL
    tile = 512 if feat % 512 == 0 else feat
    tp = lax.axis_index("tp")
    hot = hot_of(plan, lax.axis_index("ep"))

    def put(columns, back_hot, back_cold):
        for d in range(INNER):
            outs[d][:hots, columns] = back_hot[d * hots : (d + 1) * hots].astype(BF16)
            outs[d][hots:, columns] = back_cold[d * colds : (d + 1) * colds].astype(BF16)

    ends = []
    for first, piece, target in ((0, hots, g_hot), (INNER * hots, colds, g_cold)):
        made = []
        per = 1 if piece % 16 == 0 else INNER
        for d in range(0, INNER, per):
            count = piece * per
            now = slice(first + d * piece, first + d * piece + count)
            hidden = sums[0][now, :ff].astype(F32)
            for more in sums[1:]:
                hidden = hidden + more[now, :ff].astype(F32)
            if n_grads == 1:
                row_grad = grads[0][now].astype(F32)
            else:
                mine, other = (g[now, ff:].astype(F32) for g in grads)
                even = tp == 0
                row_grad = jnp.concatenate(
                    [jnp.where(even, mine, other), jnp.where(even, other, mine)], 1
                )
            sig = 1.0 / (1.0 + jnp.exp(-hidden))
            act = (hidden * sig).astype(BF16).astype(F32)
            hidden_grad = row_grad * (sig * (1.0 + hidden * (1.0 - sig)))
            target[d * piece : d * piece + count] = hidden_grad.astype(BF16)
            gate_grad = jnp.sum(act * row_grad, 1, keepdims=True)
            high = gate_grad.astype(BF16).astype(F32)
            low = gate_grad - high
            lane = lax.broadcasted_iota(I32, (count, TAIL), 1)
            end = jnp.where(lane == 0, high, jnp.where(lane == 1, low, 0.0))
            half = None
            for n in range(ff // share):
                piece_act = jnp.where(tp == n, act[:, n * share : (n + 1) * share], 0.0)
                half = piece_act if half is None else half + piece_act
            made.append(jnp.concatenate([half, end], 1))
        ends.append(jnp.concatenate(made, 0))
    put(slice(feat, width), *ends)

    across_rows = (((1,), (1,)), ((), ()))

    def features(j, carry):
        at = pl.ds(pl.multiple_of(j * tile, tile), tile)
        put(
            at,
            lax.dot_general(
                g_hot[...], weight[hot, at, :], across_rows, preferred_element_type=F32
            ),
            lax.dot_general(
                g_cold[...], weight[1 - hot, at, :], across_rows, preferred_element_type=F32
            ),
        )
        return carry

    lax.fori_loop(0, feat // tile, features, 0)


def expand_kernel(m, topk, share, n_more, waits, *refs):
    blocks, picks, marks, refs = refs[:INNER], refs[INNER : INNER + m], refs[INNER + m], refs[INNER + m + 1 :]
    more, outs = refs[:n_more], refs[n_more + waits :]
    width = blocks[0].shape[1]
    feat = width - share - TAIL

    def add(columns, rows):
        for s in range(m):
            total = jnp.dot(picks[s][...], rows, preferred_element_type=F32)
            if more:
                total = total + more[s][:, columns].astype(F32)
            outs[s][:, columns] = total.astype(BF16)

    def joined(columns):
        return rows_joined([b[:, columns] for b in blocks])

    step = 512 if feat % 512 == 0 else 128
    for at in range(0, feat, step):
        add(slice(at, at + step), joined(slice(at, at + step)))
    mark = marks[...]
    gate = mark[:, 2 * topk : 2 * topk + 1]
    columns = slice(feat, feat + share)
    add(columns, (gate * joined(columns).astype(F32)).astype(BF16))
    columns = slice(feat + share, width)
    end = joined(columns).astype(F32)
    gate_grad = (end[:, 0:1] + end[:, 1:2]) / jnp.where(gate > 0.0, gate, 1.0)
    high = gate_grad.astype(BF16).astype(F32)
    lane = lax.broadcasted_iota(I32, end.shape, 1)
    values = jnp.where(lane < topk, high, gate_grad - high)
    add(columns, jnp.where((lane < 2 * topk) & (mark > 0.0), values, 0.0).astype(BF16))


def final_kernel(n, topk, *refs):
    parts = refs[:n]
    mixed, grad_tokens, grad_gates = refs[n:]
    feat, share = grad_tokens.shape[1], mixed.shape[1]

    def total(columns):
        out = parts[0][:, columns].astype(F32)
        for part in parts[1:]:
            out = out + part[:, columns].astype(F32)
        return out

    grad_tokens[...] = total(slice(0, feat)).astype(BF16)
    mixed[...] = total(slice(feat, feat + share)).astype(BF16)
    tail = total(slice(feat + share, feat + share + TAIL))
    tail = tail.T
    grad_gates[...] = tail[:topk] + tail[topk : 2 * topk]


def up_kernel(n, waits, plan, *refs):
    x_hot, x_cold = refs[:n], refs[n : 2 * n]
    g_hot, g_cold = refs[2 * n : 3 * n], refs[3 * n : 4 * n]
    out, token, all_hot, all_cold = refs[4 * n + waits :]
    tile = out.shape[1]
    e, j = pl.program_id(0), pl.program_id(1)
    hot = hot_of(plan, lax.axis_index("ep"))
    at = pl.ds(pl.multiple_of(j * tile, tile), tile)

    @pl.when((e == 0) & (j == 0))
    def _():
        token[...] = jnp.zeros_like(token)
        all_hot[...] = jnp.concatenate([g[...] for g in g_hot], 0)
        all_cold[...] = jnp.concatenate([g[...] for g in g_cold], 0)

    def total(xs, grads):
        rows = jnp.concatenate([x[:, at] for x in xs], 0)
        out[0] = lax.dot_general(
            rows, grads[...], (((0,), (0,)), ((), ())), preferred_element_type=F32
        ).astype(BF16)

    pl.when(e == hot)(lambda: total(x_hot, all_hot))
    pl.when(e != hot)(lambda: total(x_cold, all_cold))


def on_device(tokens, routes, gates, up_weight, replica_on, grad_out):
    count, feat = tokens.shape
    topk = routes.shape[1]
    experts = replica_on.shape[0]
    share = grad_out.shape[1]
    ff = up_weight.shape[2]
    n_ep, n_tp = lax.axis_size("ep"), lax.axis_size("tp")
    outer = n_ep // INNER
    capacity = 3 * count * topk // (4 * experts)
    hot_rows, cold_rows = 2 * capacity, capacity
    width = feat + share + TAIL
    there = feat + share
    smem = pl.BlockSpec(memory_space=pltpu.SMEM)

    def along(value, shift):
        pairs = [
            (o * INNER + i, ((o + shift) % outer) * INNER + i)
            for o in range(outer)
            for i in range(INNER)
        ]
        return lax.ppermute(value, "ep", pairs)

    def across(value, d):
        pairs = [(o * INNER + i, o * INNER + (i ^ d)) for o in range(outer) for i in range(INNER)]
        return lax.ppermute(value, "ep", pairs)

    rest_spec = pl.BlockSpec(memory_space=pl.ANY)
    m = max(1, outer // CHUNKS)
    chunks = [list(range(first, first + m)) for first in range(0, outer, m)]
    n = len(chunks)
    rows = m * (hot_rows + cold_rows)
    hots, colds = INNER * m * hot_rows, INNER * m * cold_rows
    sizes = (m, hot_rows, cold_rows)

    def block(shape, dtype=BF16):
        return jax.ShapeDtypeStruct(shape, dtype)

    def fixed(shape):
        return pl.BlockSpec(shape, lambda j: (0,) * len(shape))

    going = {f: k for k, (f, _) in enumerate(PLAN) if f is not None}
    coming = {r: k for k, (_, r) in enumerate(PLAN) if r is not None}

    def weigh(kind):
        return cost(COSTS[kind] * 10**6, COSTS[kind] * 10**4)

    arrived, picks, marks, blocks, sums, grads, partials = {}, {}, {}, {}, {}, {}, {}
    x_hots, x_colds, g_hots, g_colds = {}, {}, {}, {}

    def exchange(k, made):
        blocks[k] = [made[0]] + [across(made[d], d) for d in range(1, INNER)]

    own_rows = m == 1
    made = pl.pallas_call(
        functools.partial(start_kernel, *sizes),
        out_shape=[block((count, width))]
        + (
            [block((rows, there))] * INNER
            + [block((INNER * rows, TAIL), F32), block((count, INNER * rows))]
            if own_rows
            else []
        ),
        in_specs=[smem] + [rest_spec] * 4,
        out_specs=whole_specs(1 + (INNER + 2 if own_rows else 0)),
        scratch_shapes=[
            pltpu.VMEM((topk, count), I32),
            pltpu.VMEM((topk, count), F32),
            pltpu.SemaphoreType.DMA((4,)),
        ],
        compiler_params=params(WIDE),
        cost_estimate=weigh("x"),
        name="start",
    )(replica_on, tokens, routes.T, gates.T, grad_out)
    payload = made[0]
    last = []
    for c in range(n):
        for s in chunks[c] if c not in PASSED else ():
            if s == 0:
                arrived[s] = payload
            else:
                arrived[s] = along(arrived[s - m], m) if c else along(payload, s)

    def select(k):
        c = PLAN[k][0]
        more = m if c + 1 in PASSED else 0
        made = pl.pallas_call(
            functools.partial(select_kernel, *sizes, topk, share, len(last)),
            out_shape=[block((rows, there))] * INNER
            + [block((INNER * rows, TAIL), F32)]
            + [block((count, INNER * rows))] * m
            + [block((count, width))] * more,
            in_specs=[smem] + whole_specs(m) + [rest_spec] * len(last),
            out_specs=whole_specs(INNER + 1 + m + more),
            compiler_params=params(),
            cost_estimate=weigh("x"),
            name="select",
        )(replica_on, *[arrived[s] for s in chunks[c]], *last)
        marks[c], picks[c] = made[INNER], made[INNER + 1 : INNER + 1 + m]
        exchange(k, made)
        if more:
            for s, value in zip(chunks[c + 1], made[INNER + 1 + m :]):
                arrived[s] = along(value, m)
        last[:] = [picks[c][0]]

    def hidden(c):
        k = going[c]
        tile = 256 if ff % 256 == 0 else ff
        shapes = [(INNER * rows, ff + share), (hots, feat), (colds, feat)]
        streamed = c == 0 and FIRST > 0
        if streamed:
            where = dict(
                grid=(ff // tile,),
                in_specs=[smem]
                + [fixed(b.shape) for b in blocks[k]]
                + [pl.BlockSpec((2, feat, tile), lambda j: (0, 0, j))]
                + [rest_spec] * len(last),
                out_specs=[fixed(shape) for shape in shapes],
            )
        else:
            where = dict(
                in_specs=[smem] + whole_specs(INNER + 1) + [rest_spec] * len(last),
                out_specs=whole_specs(3),
            )
        part, x_hots[c], x_colds[c] = pl.pallas_call(
            functools.partial(hidden_kernel, *sizes, feat, streamed, len(last)),
            out_shape=[block(shape) for shape in shapes],
            **where,
            compiler_params=params(WIDE if c == 0 and FIRST == 2 else LIMIT),
            cost_estimate=weigh("h"),
            name="hidden",
        )(replica_on, *blocks[k], up_weight, *last)
        last[:] = [x_colds[c]]
        if n_tp == 2:
            sums[c] = [part, lax.ppermute(part, "tp", [(0, 1), (1, 0)])]
            grads[c] = sums[c]
        else:
            sums[c] = [lax.psum(part[:, :ff].astype(F32), "tp")]
            grads[c] = [lax.all_gather(part[:, ff:], "tp", axis=1, tiled=True)]

    def step(k):
        f, c = PLAN[k]
        if c is None:
            return select(k)
        made = pl.pallas_call(
            functools.partial(
                back_kernel, *sizes, len(sums[c]), len(grads[c]), share, len(last)
            ),
            out_shape=[block((rows, width))] * INNER + [block((hots, ff)), block((colds, ff))],
            in_specs=[smem]
            + whole_specs(len(sums[c]) + len(grads[c]) + 1)
            + [rest_spec] * len(last),
            out_specs=whole_specs(INNER + 2),
            compiler_params=params(),
            cost_estimate=weigh("b"),
            name="back",
        )(replica_on, *sums[c], *grads[c], up_weight, *last)
        g_hots[c], g_colds[c] = made[INNER : INNER + 2]
        exchange(k, made)
        last[:] = [g_colds[c]]

    def expand(c):
        more = [along(partials[s - m], m) for s in chunks[c]] if c > 1 else []
        k = coming[c]
        made = pl.pallas_call(
            functools.partial(expand_kernel, m, topk, share, len(more), len(last)),
            out_shape=[block((count, width))] * m,
            in_specs=whole_specs(INNER + m + 1 + len(more)) + [rest_spec] * len(last),
            out_specs=whole_specs(m),
            compiler_params=params(),
            cost_estimate=weigh("e"),
            name="expand",
        )(*blocks[k], *picks[c], marks[c], *more, *last)
        for s, value in zip(chunks[c], made):
            partials[s] = value
        last[:] = [made[0]]

    def weight_grad():
        tile = 512 if feat % 512 == 0 else feat
        grad_up, token = pl.pallas_call(
            functools.partial(up_kernel, n, len(last)),
            out_shape=[block(up_weight.shape), block((8, 128), F32)],
            grid=(up_weight.shape[0], feat // tile),
            in_specs=[smem] + whole_specs(4 * n) + [rest_spec] * len(last),
            out_specs=[
                pl.BlockSpec((1, tile, ff), lambda e, j: (e, j, 0)),
                pl.BlockSpec((8, 128), lambda e, j: (0, 0)),
            ],
            scratch_shapes=[
                pltpu.VMEM((n * hots, ff), BF16),
                pltpu.VMEM((n * colds, ff), BF16),
            ],
            compiler_params=params(),
            cost_estimate=weigh("u"),
            name="grad_up",
        )(
            replica_on,
            *[x_hots[c] for c in range(n)],
            *[x_colds[c] for c in range(n)],
            *[g_hots[c] for c in range(n)],
            *[g_colds[c] for c in range(n)],
            *last,
        )
        last[:] = [token]
        return grad_up

    if own_rows:
        marks[0], picks[0] = made[INNER + 1], made[INNER + 2 :]
        exchange(0, made[1 : INNER + 1])
    else:
        select(0)
    grad_up = None
    for word in ORDER:
        number = int(word[1:] or 0)
        if word[0] == "u":
            grad_up = weight_grad()
        elif word[0] == "r":
            last.append(sums[number][-1])
        else:
            {"x": step, "h": hidden, "e": expand}[word[0]](number)

    sums_back = [along(partials[s], m) for s in chunks[n - 1]]
    parts = [sums_back[0], partials[0]]
    for s in chunks[0][1:]:
        parts.append(along(sums_back[s] + partials[s], outer - s))
    mixed, grad_tokens, grad_gates = pl.pallas_call(
        functools.partial(final_kernel, len(parts), topk),
        out_shape=[block((count, share)), block((count, feat)), block((topk, count), F32)],
        in_specs=whole_specs(len(parts)),
        out_specs=whole_specs(3),
        compiler_params=params(),
        cost_estimate=weigh("e"),
        name="final",
    )(*parts)
    return mixed, grad_tokens, grad_gates.T, grad_up


def solution(mesh):
    return jax.shard_map(
        on_device,
        mesh=mesh,
        in_specs=(
            P("ep", "tp"),
            P("ep", None),
            P("ep", None),
            P("ep", "tp", None),
            P(),
            P("ep", "tp"),
        ),
        out_specs=(P("ep", "tp"), P("ep", "tp"), P("ep", None), P("ep", "tp", None)),
        check_vma=False,
    )
```

```python
import functools

import jax
import jax.numpy as jnp
from jax import lax
from jax.experimental import pallas as pl
from jax.experimental.pallas import tpu as pltpu
from jax.sharding import PartitionSpec as P

INNER = 4
CHUNKS = 4
PLAN = ((0, None), (1, None), (2, None), (3, None), (None, 1), (None, 2), (None, 3), (None, 0))
ORDER = ('x1', 'h0', 'x2', 'h1', 'x3', 'h2', 'r0', 'x4', 'h3', 'x5', 'r3', 'e1', 'x6', 'e2', 'r2', 'x7', 'e3', 'u', 'e0')
PASSED = ()
FIRST = 1
COSTS = {'x': 5000, 'b': 20000, 'h': 5000, 'e': 1, 'u': 20000}
TAIL = 128
LIMIT = 20 * 1024 * 1024
WIDE = 56 * 1024 * 1024
F32, BF16, I32 = jnp.float32, jnp.bfloat16, jnp.int32


def params(limit=LIMIT):
    return pltpu.CompilerParams(vmem_limit_bytes=limit)


def cost(flops, moved):
    return pl.CostEstimate(flops=int(flops), bytes_accessed=int(moved), transcendentals=0)


def whole_specs(n):
    return [pl.BlockSpec(memory_space=pltpu.VMEM)] * n


def hot_of(plan, device):
    return plan[2 * device + 1]


def rows_joined(pieces):
    if all(piece.shape[0] % 16 == 0 for piece in pieces):
        return jnp.concatenate(pieces, 0)
    return jnp.concatenate([piece.astype(F32) for piece in pieces], 0).astype(BF16)


def row_plan(m, hot_rows, cold_rows, plan, shape, axis):
    rows = m * (hot_rows + cold_rows)
    me = lax.axis_index("ep")
    outer, inner = me // INNER, me % INNER
    spot = lax.broadcasted_iota(I32, shape, axis)
    which = jnp.zeros(shape, I32)
    for d in range(1, INNER):
        which += (spot >= d * rows).astype(I32)
    within = spot - which * rows
    is_hot = within < m * hot_rows
    group = jnp.zeros(shape, I32)
    for s in range(1, m):
        edge = jnp.where(is_hot, s * hot_rows, m * hot_rows + s * cold_rows)
        group += (within >= edge).astype(I32)
    slot = jnp.where(is_hot, within - group * hot_rows, within - m * hot_rows - group * cold_rows)
    expert = jnp.zeros(shape, I32)
    for d in range(INNER):
        device = outer * INNER + (inner ^ d)
        hot = hot_of(plan, device)
        ids = jnp.where(is_hot, 2 * device + hot, 2 * device + 1 - hot)
        expert = jnp.where(which == d, ids, expert)
    return expert.astype(F32), slot.astype(F32), group


def pick_rows(m, hot_rows, cold_rows, topk, plan, tails):
    count = tails[0].shape[0]
    cols = INNER * m * (hot_rows + cold_rows)
    expert, slot, group = (
        value[0:1] for value in row_plan(m, hot_rows, cold_rows, plan, (8, cols), 1)
    )
    before = lax.broadcasted_iota(I32, (count, count), 1) < lax.broadcasted_iota(I32, (count, count), 0)
    before = jnp.where(before, 1.0, 0.0).astype(BF16)
    found = []
    for s, ids in enumerate(tails):
        match = ids[:, 0:1] == expert
        for k in range(1, topk):
            match = match | (ids[:, k : k + 1] == expert)
        ones = jnp.where(match, 1.0, 0.0)
        rank = jnp.dot(before, ones.astype(BF16), preferred_element_type=F32)
        found.append(jnp.where((rank == slot) & (group == s), ones, 0.0).astype(BF16))
    return found


def picked(picks, payloads, columns):
    total = None
    for pick, payload in zip(picks, payloads):
        part = lax.dot_general(
            pick[...], payload[:, columns], (((0,), (0,)), ((), ())), preferred_element_type=F32
        )
        total = part if total is None else total + part
    return total


def select_all(m, hot_rows, cold_rows, topk, share, plan, picks, payloads, outs, marks):
    rows, width = outs[0].shape
    feat = width - share
    expert, _, _ = row_plan(m, hot_rows, cold_rows, plan, (INNER * rows, TAIL), 0)
    tail = picked(picks, payloads, slice(width, width + TAIL))
    gate = (tail[:, 2 * topk : 3 * topk] + tail[:, 3 * topk : 4 * topk]) + tail[:, 4 * topk : 5 * topk]
    gate = jnp.sum(jnp.where(tail[:, :topk] == expert[:, :topk], gate, 0.0), 1, keepdims=True)
    lane = lax.broadcasted_iota(I32, tail.shape, 1)
    own = jnp.where((tail == expert) & (lane < 2 * topk), 1.0, 0.0)
    marks[...] = jnp.where(lane == 2 * topk, gate, own)
    step = 512 if feat % 512 == 0 else 128
    for at in [*range(0, feat, step), feat]:
        columns = slice(at, at + step) if at < feat else slice(feat, width)
        total = picked(picks, payloads, columns)
        if at == feat:
            total = gate * total
        for d in range(INNER):
            outs[d][:, columns] = total[d * rows : (d + 1) * rows].astype(BF16)


def start_kernel(m, hot_rows, cold_rows, plan, tokens, routes, gates, grad_out, *refs):
    out, refs = refs[0], refs[1:]
    here_routes, here_gates, sems = refs[-3:]
    outs, marks, picks = refs[:INNER], refs[INNER:-3][:1], refs[INNER:-3][1:]
    count, feat = tokens.shape
    share = grad_out.shape[1]
    topk = routes.shape[0]
    copies = [
        pltpu.make_async_copy(source, target, sems.at[n])
        for n, (source, target) in enumerate(
            (
                (routes, here_routes),
                (gates, here_gates),
                (tokens, out.at[:, :feat]),
                (grad_out, out.at[:, feat : feat + share]),
            )
        )
    ]
    for copy in copies:
        copy.start()
    for copy in copies[:2]:
        copy.wait()
    ids = here_routes[...].astype(F32)
    gate = here_gates[...]
    high = gate.astype(BF16).astype(F32)
    middle = (gate - high).astype(BF16).astype(F32)
    low = (gate - high - middle).astype(BF16).astype(F32)
    rest = jnp.zeros((TAIL - 5 * topk, count), F32)
    tail = jnp.concatenate([ids, ids, high, middle, low, rest], 0).T
    out[:, feat + share :] = tail.astype(BF16)
    if picks:
        picks[0][...] = pick_rows(m, hot_rows, cold_rows, topk, plan, [tail])[0]
    for copy in copies[2:]:
        copy.wait()
    if picks:
        select_all(m, hot_rows, cold_rows, topk, share, plan, picks, [out], outs, marks[0])


def select_kernel(m, hot_rows, cold_rows, topk, share, waits, plan, *refs):
    payloads, refs = refs[:m], refs[m + waits :]
    outs, marks, picks, passed = refs[:INNER], refs[INNER], refs[INNER + 1 : INNER + 1 + m], refs[INNER + 1 + m :]
    width = payloads[0].shape[1]
    for source, target in zip(payloads, passed):
        target[...] = source[...]
    tails = [payload[:, width - TAIL :].astype(F32) for payload in payloads]
    for pick, found in zip(picks, pick_rows(m, hot_rows, cold_rows, topk, plan, tails)):
        pick[...] = found
    select_all(m, hot_rows, cold_rows, topk, share, plan, picks, payloads, outs, marks)


def hidden_kernel(m, hot_rows, cold_rows, feat, streamed, waits, plan, *refs):
    blocks = refs[:INNER]
    weight, part, x_hot, x_cold = refs[INNER], *refs[INNER + 1 + waits :]
    hots = INNER * m * hot_rows
    share = blocks[0].shape[1] - feat
    ff = part.shape[1] - share
    tile = 256 if ff % 256 == 0 else ff
    hot = hot_of(plan, lax.axis_index("ep"))
    split = m * hot_rows

    def gather():
        x_hot[...] = rows_joined([b[:split, :feat] for b in blocks])
        x_cold[...] = rows_joined([b[split:, :feat] for b in blocks])
        part[:hots, ff:] = rows_joined([b[:split, feat:] for b in blocks])
        part[hots:, ff:] = rows_joined([b[split:, feat:] for b in blocks])

    def columns(j, source):
        at = pl.ds(pl.multiple_of(j * tile, tile), tile)
        part[:hots, at] = jnp.dot(
            x_hot[...], weight[hot, :, source], preferred_element_type=F32
        ).astype(BF16)
        part[hots:, at] = jnp.dot(
            x_cold[...], weight[1 - hot, :, source], preferred_element_type=F32
        ).astype(BF16)

    if streamed:
        pl.when(pl.program_id(0) == 0)(gather)
        columns(pl.program_id(0), slice(None))
    else:
        gather()

        @pl.loop(0, ff // tile)
        def _(j):
            columns(j, pl.ds(pl.multiple_of(j * tile, tile), tile))


def back_kernel(m, hot_rows, cold_rows, n_parts, n_grads, share, tailed, waits, plan, *refs):
    sums, grads = refs[:n_parts], refs[n_parts : n_parts + n_grads]
    weight, refs = refs[n_parts + n_grads], refs[n_parts + n_grads + 1 + waits :]
    outs, g_hot, g_cold = refs[:INNER], refs[INNER], refs[INNER + 1]
    hots, colds = m * hot_rows, m * cold_rows
    feat, ff = weight.shape[1:]
    width = outs[0].shape[1]
    tile = 512 if feat % 512 == 0 else feat
    tp = lax.axis_index("tp")
    hot = hot_of(plan, lax.axis_index("ep"))

    def put(columns, back_hot, back_cold):
        for d in range(INNER):
            outs[d][:hots, columns] = back_hot[d * hots : (d + 1) * hots].astype(BF16)
            outs[d][hots:, columns] = back_cold[d * colds : (d + 1) * colds].astype(BF16)

    ends = []
    for first, piece, target in ((0, hots, g_hot), (INNER * hots, colds, g_cold)):
        made = []
        per = 1 if piece % 16 == 0 else INNER
        for d in range(0, INNER, per):
            count = piece * per
            now = slice(first + d * piece, first + d * piece + count)
            hidden = sums[0][now, :ff].astype(F32)
            for more in sums[1:]:
                hidden = hidden + more[now, :ff].astype(F32)
            if n_grads == 1:
                row_grad = grads[0][now].astype(F32)
            else:
                mine, other = (g[now, ff:].astype(F32) for g in grads)
                even = tp == 0
                row_grad = jnp.concatenate(
                    [jnp.where(even, mine, other), jnp.where(even, other, mine)], 1
                )
            sig = 1.0 / (1.0 + jnp.exp(-hidden))
            act = (hidden * sig).astype(BF16).astype(F32)
            hidden_grad = row_grad * (sig * (1.0 + hidden * (1.0 - sig)))
            target[d * piece : d * piece + count] = hidden_grad.astype(BF16)
            half = None
            for n in range(ff // share):
                piece_act = jnp.where(tp == n, act[:, n * share : (n + 1) * share], 0.0)
                half = piece_act if half is None else half + piece_act
            if tailed:
                gate_grad = jnp.sum(act * row_grad, 1, keepdims=True)
                high = gate_grad.astype(BF16).astype(F32)
                low = gate_grad - high
                lane = lax.broadcasted_iota(I32, (count, TAIL), 1)
                end = jnp.where(lane == 0, high, jnp.where(lane == 1, low, 0.0))
                half = jnp.concatenate([half, end], 1)
            made.append(half)
        ends.append(jnp.concatenate(made, 0))
    put(slice(feat, width), *ends)

    across_rows = (((1,), (1,)), ((), ()))

    def features(j, carry):
        at = pl.ds(pl.multiple_of(j * tile, tile), tile)
        put(
            at,
            lax.dot_general(
                g_hot[...], weight[hot, at, :], across_rows, preferred_element_type=F32
            ),
            lax.dot_general(
                g_cold[...], weight[1 - hot, at, :], across_rows, preferred_element_type=F32
            ),
        )
        return carry

    lax.fori_loop(0, feat // tile, features, 0)


def expand_kernel(m, topk, share, tailed, n_more, waits, *refs):
    blocks, picks, marks, refs = refs[:INNER], refs[INNER : INNER + m], refs[INNER + m], refs[INNER + m + 1 :]
    payloads, refs = ([], refs) if tailed else (refs[:m], refs[m:])
    more, outs, apart = refs[:n_more], refs[n_more + waits :][:m], refs[n_more + waits + m :]
    width = outs[0].shape[1]
    feat = width - share - TAIL

    def add(columns, rows, copies=()):
        for s in range(m):
            total = jnp.dot(picks[s][...], rows, preferred_element_type=F32)
            if more:
                total = total + more[s][:, columns].astype(F32)
            outs[s][:, columns] = total.astype(BF16)
            for copy in copies[s : s + 1]:
                copy[...] = total.astype(BF16)

    def joined(columns):
        return rows_joined([b[:, columns] for b in blocks])

    step = 512 if feat % 512 == 0 else 128
    for at in range(0, feat, step):
        add(slice(at, at + step), joined(slice(at, at + step)))
    mark = marks[...]
    gate = mark[:, 2 * topk : 2 * topk + 1]
    columns = slice(feat, feat + share)
    act = joined(columns).astype(F32)
    add(columns, (gate * act).astype(BF16))
    columns = slice(feat + share, width)
    if tailed:
        end = joined(columns).astype(F32)
        gate_grad = (end[:, 0:1] + end[:, 1:2]) / jnp.where(gate > 0.0, gate, 1.0)
    else:
        grad = picked(picks, payloads, slice(feat, feat + share))
        gate_grad = jnp.sum(act * grad, 1, keepdims=True)
    high = gate_grad.astype(BF16).astype(F32)
    lane = lax.broadcasted_iota(I32, mark.shape, 1)
    values = jnp.where(lane < topk, high, gate_grad - high)
    end = jnp.where((lane < 2 * topk) & (mark > 0.0), values, 0.0)
    add(columns, end.astype(BF16), apart)


def final_kernel(n, n_tails, topk, *refs):
    parts, tails = refs[:n], refs[n : n + n_tails]
    mixed, grad_tokens, grad_gates = refs[n + n_tails :]
    feat, share = grad_tokens.shape[1], mixed.shape[1]

    def total(columns):
        out = parts[0][:, columns].astype(F32)
        for part in parts[1:]:
            out = out + part[:, columns].astype(F32)
        return out

    grad_tokens[...] = total(slice(0, feat)).astype(BF16)
    mixed[...] = total(slice(feat, feat + share)).astype(BF16)
    ends = [tail[...].astype(F32) for tail in tails]
    ends += [part[:, feat + share :].astype(F32) for part in parts if part.shape[1] > feat + share]
    end = ends[0]
    for more in ends[1:]:
        end = end + more
    end = end.T
    grad_gates[...] = end[:topk] + end[topk : 2 * topk]


def up_kernel(n, waits, plan, *refs):
    x_hot, x_cold = refs[:n], refs[n : 2 * n]
    g_hot, g_cold = refs[2 * n : 3 * n], refs[3 * n : 4 * n]
    out, token, all_hot, all_cold = refs[4 * n + waits :]
    tile = out.shape[1]
    e, j = pl.program_id(0), pl.program_id(1)
    hot = hot_of(plan, lax.axis_index("ep"))
    at = pl.ds(pl.multiple_of(j * tile, tile), tile)

    @pl.when((e == 0) & (j == 0))
    def _():
        token[...] = jnp.zeros_like(token)
        all_hot[...] = jnp.concatenate([g[...] for g in g_hot], 0)
        all_cold[...] = jnp.concatenate([g[...] for g in g_cold], 0)

    def total(xs, grads):
        rows = jnp.concatenate([x[:, at] for x in xs], 0)
        out[0] = lax.dot_general(
            rows, grads[...], (((0,), (0,)), ((), ())), preferred_element_type=F32
        ).astype(BF16)

    pl.when(e == hot)(lambda: total(x_hot, all_hot))
    pl.when(e != hot)(lambda: total(x_cold, all_cold))


def on_device(tokens, routes, gates, up_weight, replica_on, grad_out):
    count, feat = tokens.shape
    topk = routes.shape[1]
    experts = replica_on.shape[0]
    share = grad_out.shape[1]
    ff = up_weight.shape[2]
    n_ep, n_tp = lax.axis_size("ep"), lax.axis_size("tp")
    outer = n_ep // INNER
    capacity = 3 * count * topk // (4 * experts)
    hot_rows, cold_rows = 2 * capacity, capacity
    width = feat + share + TAIL
    there = feat + share
    by_hand = n_tp == 2 and outer == CHUNKS
    smem = pl.BlockSpec(memory_space=pltpu.SMEM)

    def along(value, shift):
        pairs = [
            (o * INNER + i, ((o + shift) % outer) * INNER + i)
            for o in range(outer)
            for i in range(INNER)
        ]
        return lax.ppermute(value, "ep", pairs)

    def across(value, d):
        pairs = [(o * INNER + i, o * INNER + (i ^ d)) for o in range(outer) for i in range(INNER)]
        return lax.ppermute(value, "ep", pairs)

    rest_spec = pl.BlockSpec(memory_space=pl.ANY)
    m = max(1, outer // CHUNKS)
    chunks = [list(range(first, first + m)) for first in range(0, outer, m)]
    n = len(chunks)
    rows = m * (hot_rows + cold_rows)
    hots, colds = INNER * m * hot_rows, INNER * m * cold_rows
    sizes = (m, hot_rows, cold_rows)

    def block(shape, dtype=BF16):
        return jax.ShapeDtypeStruct(shape, dtype)

    def fixed(shape):
        return pl.BlockSpec(shape, lambda j: (0,) * len(shape))

    going = {f: k for k, (f, _) in enumerate(PLAN) if f is not None}
    coming = {r: k for k, (_, r) in enumerate(PLAN) if r is not None}

    def weigh(kind):
        return cost(COSTS[kind] * 10**6, COSTS[kind] * 10**4)

    arrived, picks, marks, blocks, sums, grads, partials = {}, {}, {}, {}, {}, {}, {}
    x_hots, x_colds, g_hots, g_colds = {}, {}, {}, {}

    def exchange(k, made):
        blocks[k] = [made[0]] + [across(made[d], d) for d in range(1, INNER)]

    own_rows = m == 1
    made = pl.pallas_call(
        functools.partial(start_kernel, *sizes),
        out_shape=[block((count, width))]
        + (
            [block((rows, there))] * INNER
            + [block((INNER * rows, TAIL), F32), block((count, INNER * rows))]
            if own_rows
            else []
        ),
        in_specs=[smem] + [rest_spec] * 4,
        out_specs=whole_specs(1 + (INNER + 2 if own_rows else 0)),
        scratch_shapes=[
            pltpu.VMEM((topk, count), I32),
            pltpu.VMEM((topk, count), F32),
            pltpu.SemaphoreType.DMA((4,)),
        ],
        compiler_params=params(WIDE),
        cost_estimate=weigh("x"),
        name="start",
    )(replica_on, tokens, routes.T, gates.T, grad_out)
    payload = made[0]
    last = []
    for c in range(n):
        for s in chunks[c] if c not in PASSED else ():
            if s == 0:
                arrived[s] = payload
            else:
                arrived[s] = along(arrived[s - m], m) if c else along(payload, s)

    def select(k):
        c = PLAN[k][0]
        more = m if c + 1 in PASSED else 0
        made = pl.pallas_call(
            functools.partial(select_kernel, *sizes, topk, share, len(last)),
            out_shape=[block((rows, there))] * INNER
            + [block((INNER * rows, TAIL), F32)]
            + [block((count, INNER * rows))] * m
            + [block((count, width))] * more,
            in_specs=[smem] + whole_specs(m) + [rest_spec] * len(last),
            out_specs=whole_specs(INNER + 1 + m + more),
            compiler_params=params(),
            cost_estimate=weigh("x"),
            name="select",
        )(replica_on, *[arrived[s] for s in chunks[c]], *last)
        marks[c], picks[c] = made[INNER], made[INNER + 1 : INNER + 1 + m]
        exchange(k, made)
        if more:
            for s, value in zip(chunks[c + 1], made[INNER + 1 + m :]):
                arrived[s] = along(value, m)
        last[:] = [picks[c][0]]

    def hidden(c):
        k = going[c]
        tile = 256 if ff % 256 == 0 else ff
        shapes = [(INNER * rows, ff + share), (hots, feat), (colds, feat)]
        streamed = c == 0 and FIRST > 0
        if streamed:
            where = dict(
                grid=(ff // tile,),
                in_specs=[smem]
                + [fixed(b.shape) for b in blocks[k]]
                + [pl.BlockSpec((2, feat, tile), lambda j: (0, 0, j))]
                + [rest_spec] * len(last),
                out_specs=[fixed(shape) for shape in shapes],
            )
        else:
            where = dict(
                in_specs=[smem] + whole_specs(INNER + 1) + [rest_spec] * len(last),
                out_specs=whole_specs(3),
            )
        part, x_hots[c], x_colds[c] = pl.pallas_call(
            functools.partial(hidden_kernel, *sizes, feat, streamed, len(last)),
            out_shape=[block(shape) for shape in shapes],
            **where,
            compiler_params=params(WIDE if c == 0 and FIRST == 2 else LIMIT),
            cost_estimate=weigh("h"),
            name="hidden",
        )(replica_on, *blocks[k], up_weight, *last)
        last[:] = [x_colds[c]]
        if n_tp == 2:
            sums[c] = [part, lax.ppermute(part, "tp", [(0, 1), (1, 0)])]
            grads[c] = sums[c]
        else:
            sums[c] = [lax.psum(part[:, :ff].astype(F32), "tp")]
            grads[c] = [lax.all_gather(part[:, ff:], "tp", axis=1, tiled=True)]

    def step(k):
        f, c = PLAN[k]
        if c is None:
            return select(k)
        made = pl.pallas_call(
            functools.partial(
                back_kernel, *sizes, len(sums[c]), len(grads[c]), share, c == 0, len(last)
            ),
            out_shape=[block((rows, there if c else width))] * INNER
            + [block((hots, ff)), block((colds, ff))],
            in_specs=[smem]
            + whole_specs(len(sums[c]) + len(grads[c]) + 1)
            + [rest_spec] * len(last),
            out_specs=whole_specs(INNER + 2),
            compiler_params=params(),
            cost_estimate=weigh("b"),
            name="back",
        )(replica_on, *sums[c], *grads[c], up_weight, *last)
        g_hots[c], g_colds[c] = made[INNER : INNER + 2]
        exchange(k, made)
        last[:] = [g_colds[c]]

    def expand(c):
        more = [along(partials[s - m], m) for s in chunks[c]] if c > 1 else []
        payloads = [arrived[s] for s in chunks[c]] if c else []
        apart = [block((count, TAIL))] if c == n - 1 and by_hand else []
        k = coming[c]
        made = pl.pallas_call(
            functools.partial(expand_kernel, m, topk, share, c == 0, len(more), len(last)),
            out_shape=[block((count, width))] * m + apart,
            in_specs=whole_specs(INNER + m + 1 + len(payloads) + len(more))
            + [rest_spec] * len(last),
            out_specs=whole_specs(m + len(apart)),
            compiler_params=params(),
            cost_estimate=weigh("e"),
            name="expand",
        )(*blocks[k], *picks[c], marks[c], *payloads, *more, *last)
        for s, value in zip(chunks[c], made):
            partials[s] = value
        if apart:
            partials["apart"] = made[m]
        last[:] = [made[0]]

    def weight_grad():
        tile = 512 if feat % 512 == 0 else feat
        grad_up, token = pl.pallas_call(
            functools.partial(up_kernel, n, len(last)),
            out_shape=[block(up_weight.shape), block((8, 128), F32)],
            grid=(up_weight.shape[0], feat // tile),
            in_specs=[smem] + whole_specs(4 * n) + [rest_spec] * len(last),
            out_specs=[
                pl.BlockSpec((1, tile, ff), lambda e, j: (e, j, 0)),
                pl.BlockSpec((8, 128), lambda e, j: (0, 0)),
            ],
            scratch_shapes=[
                pltpu.VMEM((n * hots, ff), BF16),
                pltpu.VMEM((n * colds, ff), BF16),
            ],
            compiler_params=params(),
            cost_estimate=weigh("u"),
            name="grad_up",
        )(
            replica_on,
            *[x_hots[c] for c in range(n)],
            *[x_colds[c] for c in range(n)],
            *[g_hots[c] for c in range(n)],
            *[g_colds[c] for c in range(n)],
            *last,
        )
        last[:] = [token]
        return grad_up

    if own_rows:
        marks[0], picks[0] = made[INNER + 1], made[INNER + 2 :]
        exchange(0, made[1 : INNER + 1])
    else:
        select(0)
    grad_up = None
    for word in ORDER:
        number = int(word[1:] or 0)
        if word[0] == "u":
            grad_up = weight_grad()
        elif word[0] == "r":
            last.append(sums[number][-1])
        else:
            {"x": step, "h": hidden, "e": expand}[word[0]](number)

    sums_back = [along(partials[s], m) for s in chunks[n - 1]]
    if by_hand:
        pairs = [
            (
                (o * INNER + i) * n_tp + t,
                (((o + m) % outer) * INNER + i) * n_tp + 1 - t,
            )
            for o in range(outer)
            for i in range(INNER)
            for t in range(n_tp)
        ]
        tails = [lax.ppermute(partials["apart"], ("ep", "tp"), pairs)]
        parts = [sums_back[0], partials[0]]
    else:
        parts, tails, halves = [], [], 0.0
        for s, value in zip(chunks[0], sums_back):
            ours = partials[s]
            if s == 0:
                parts += [value[:, :there], ours[:, :there]]
                halves = halves + value[:, there:].astype(F32)
                tails.append(ours[:, there:])
            else:
                parts.append(along(value[:, :there] + ours[:, :there], outer - s))
                halves = halves + along(value[:, there:], outer - s).astype(F32)
                tails.append(along(ours[:, there:], outer - s))
        tails.append(lax.psum(halves, "tp"))
    mixed, grad_tokens, grad_gates = pl.pallas_call(
        functools.partial(final_kernel, len(parts), len(tails), topk),
        out_shape=[block((count, share)), block((count, feat)), block((topk, count), F32)],
        in_specs=whole_specs(len(parts) + len(tails)),
        out_specs=whole_specs(3),
        compiler_params=params(),
        cost_estimate=weigh("e"),
        name="final",
    )(*parts, *tails)
    return mixed, grad_tokens, grad_gates.T, grad_up


def solution(mesh):
    return jax.shard_map(
        on_device,
        mesh=mesh,
        in_specs=(
            P("ep", "tp"),
            P("ep", None),
            P("ep", None),
            P("ep", "tp", None),
            P(),
            P("ep", "tp"),
        ),
        out_specs=(P("ep", "tp"), P("ep", "tp"), P("ep", None), P("ep", "tp", None)),
        check_vma=False,
    )
```

```python
import functools

import jax
import jax.numpy as jnp
from jax import lax
from jax.experimental import pallas as pl
from jax.experimental.pallas import tpu as pltpu
from jax.sharding import PartitionSpec as P

INNER = 4
CHUNKS = 4
PLAN = ((0, None), (1, None), (2, None), (3, None), (None, 1), (None, 2), (None, 3), (None, 0))
ORDER = ('x1', 'h0', 'x2', 'h1', 'x3', 'h2', 'r0', 'x4', 'h3', 'x5', 'r3', 'e1', 'x6', 'e2', 'r2', 'x7', 'e3', 'u', 'e0')
FIRST = 1
COSTS = {'x': 5000, 'b': 20000, 'h': 5000, 'e': 1, 'u': 20000}
TAIL = 128
LIMIT = 20 * 1024 * 1024
WIDE = 56 * 1024 * 1024
F32, BF16, I32 = jnp.float32, jnp.bfloat16, jnp.int32


def params(limit=LIMIT):
    return pltpu.CompilerParams(vmem_limit_bytes=limit)


def cost(flops, moved):
    return pl.CostEstimate(flops=int(flops), bytes_accessed=int(moved), transcendentals=0)


def whole_specs(n):
    return [pl.BlockSpec(memory_space=pltpu.VMEM)] * n


def hot_of(plan, device):
    return plan[2 * device + 1]


def rows_joined(pieces):
    if all(piece.shape[0] % 16 == 0 for piece in pieces):
        return jnp.concatenate(pieces, 0)
    return jnp.concatenate([piece.astype(F32) for piece in pieces], 0).astype(BF16)


def row_plan(m, hot_rows, cold_rows, plan, shape, axis):
    rows = m * (hot_rows + cold_rows)
    me = lax.axis_index("ep")
    outer, inner = me // INNER, me % INNER
    spot = lax.broadcasted_iota(I32, shape, axis)
    which = jnp.zeros(shape, I32)
    for d in range(1, INNER):
        which += (spot >= d * rows).astype(I32)
    within = spot - which * rows
    is_hot = within < m * hot_rows
    group = jnp.zeros(shape, I32)
    for s in range(1, m):
        edge = jnp.where(is_hot, s * hot_rows, m * hot_rows + s * cold_rows)
        group += (within >= edge).astype(I32)
    slot = jnp.where(is_hot, within - group * hot_rows, within - m * hot_rows - group * cold_rows)
    expert = jnp.zeros(shape, I32)
    for d in range(INNER):
        device = outer * INNER + (inner ^ d)
        hot = hot_of(plan, device)
        ids = jnp.where(is_hot, 2 * device + hot, 2 * device + 1 - hot)
        expert = jnp.where(which == d, ids, expert)
    return expert.astype(F32), slot.astype(F32), group


def pick_rows(m, hot_rows, cold_rows, topk, plan, tails):
    count = tails[0].shape[0]
    cols = INNER * m * (hot_rows + cold_rows)
    expert, slot, group = (
        value[0:1] for value in row_plan(m, hot_rows, cold_rows, plan, (8, cols), 1)
    )
    before = lax.broadcasted_iota(I32, (count, count), 1) < lax.broadcasted_iota(I32, (count, count), 0)
    before = jnp.where(before, 1.0, 0.0).astype(BF16)
    found = []
    for s, ids in enumerate(tails):
        match = ids[:, 0:1] == expert
        for k in range(1, topk):
            match = match | (ids[:, k : k + 1] == expert)
        ones = jnp.where(match, 1.0, 0.0)
        rank = jnp.dot(before, ones.astype(BF16), preferred_element_type=F32)
        found.append(jnp.where((rank == slot) & (group == s), ones, 0.0).astype(BF16))
    return found


def picked(picks, sources, columns):
    total = None
    for pick, source in zip(picks, sources):
        part = lax.dot_general(
            pick[...], source[:, columns], (((0,), (0,)), ((), ())), preferred_element_type=F32
        )
        total = part if total is None else total + part
    return total


def select_all(m, hot_rows, cold_rows, topk, share, plan, picks, tokens, rests, outs, marks):
    rows, width = outs[0].shape
    feat = width - share
    expert, _, _ = row_plan(m, hot_rows, cold_rows, plan, (INNER * rows, TAIL), 0)
    tail = picked(picks, rests, slice(share, share + TAIL))
    gate = (tail[:, 2 * topk : 3 * topk] + tail[:, 3 * topk : 4 * topk]) + tail[:, 4 * topk : 5 * topk]
    gate = jnp.sum(jnp.where(tail[:, :topk] == expert[:, :topk], gate, 0.0), 1, keepdims=True)
    lane = lax.broadcasted_iota(I32, tail.shape, 1)
    own = jnp.where((tail == expert) & (lane < 2 * topk), 1.0, 0.0)
    marks[...] = jnp.where(lane == 2 * topk, gate, own)
    step = 512 if feat % 512 == 0 else 128
    for at in [*range(0, feat, step), feat]:
        if at < feat:
            columns = slice(at, at + step)
            total = picked(picks, tokens, columns)
        else:
            columns = slice(feat, width)
            total = gate * picked(picks, rests, slice(0, share))
        for d in range(INNER):
            outs[d][:, columns] = total[d * rows : (d + 1) * rows].astype(BF16)


def start_kernel(m, hot_rows, cold_rows, plan, tokens, routes, gates, grad_out, *refs):
    out, refs = refs[0], refs[1:]
    here, here_routes, here_gates, sems = refs[-4:]
    outs, marks, picks = refs[:INNER], refs[INNER:-4][:1], refs[INNER:-4][1:]
    count, feat = tokens.shape
    share = grad_out.shape[1]
    topk = routes.shape[0]
    copies = [
        pltpu.make_async_copy(source, target, sems.at[n])
        for n, (source, target) in enumerate(
            (
                (routes, here_routes),
                (gates, here_gates),
                (tokens, here),
                (grad_out, out.at[:, :share]),
            )
        )
    ]
    for copy in copies:
        copy.start()
    for copy in copies[:2]:
        copy.wait()
    ids = here_routes[...].astype(F32)
    gate = here_gates[...]
    high = gate.astype(BF16).astype(F32)
    middle = (gate - high).astype(BF16).astype(F32)
    low = (gate - high - middle).astype(BF16).astype(F32)
    rest = jnp.zeros((TAIL - 5 * topk, count), F32)
    tail = jnp.concatenate([ids, ids, high, middle, low, rest], 0).T
    out[:, share:] = tail.astype(BF16)
    if picks:
        picks[0][...] = pick_rows(m, hot_rows, cold_rows, topk, plan, [tail])[0]
    for copy in copies[2:]:
        copy.wait()
    if picks:
        select_all(
            m, hot_rows, cold_rows, topk, share, plan, picks, [here], [out], outs, marks[0]
        )


def select_kernel(m, hot_rows, cold_rows, topk, share, waits, plan, *refs):
    tokens, rests, refs = refs[:m], refs[m : 2 * m], refs[2 * m + waits :]
    outs, marks, picks = refs[:INNER], refs[INNER], refs[INNER + 1 :]
    tails = [rest[:, share:].astype(F32) for rest in rests]
    for pick, found in zip(picks, pick_rows(m, hot_rows, cold_rows, topk, plan, tails)):
        pick[...] = found
    select_all(m, hot_rows, cold_rows, topk, share, plan, picks, tokens, rests, outs, marks)


def hidden_kernel(m, hot_rows, cold_rows, feat, streamed, waits, plan, *refs):
    blocks = refs[:INNER]
    weight, part, x_hot, x_cold = refs[INNER], *refs[INNER + 1 + waits :]
    hots = INNER * m * hot_rows
    share = blocks[0].shape[1] - feat
    ff = part.shape[1] - share
    tile = 256 if ff % 256 == 0 else ff
    hot = hot_of(plan, lax.axis_index("ep"))
    split = m * hot_rows

    def gather():
        x_hot[...] = rows_joined([b[:split, :feat] for b in blocks])
        x_cold[...] = rows_joined([b[split:, :feat] for b in blocks])
        part[:hots, ff:] = rows_joined([b[:split, feat:] for b in blocks])
        part[hots:, ff:] = rows_joined([b[split:, feat:] for b in blocks])

    def columns(j, source):
        at = pl.ds(pl.multiple_of(j * tile, tile), tile)
        part[:hots, at] = jnp.dot(
            x_hot[...], weight[hot, :, source], preferred_element_type=F32
        ).astype(BF16)
        part[hots:, at] = jnp.dot(
            x_cold[...], weight[1 - hot, :, source], preferred_element_type=F32
        ).astype(BF16)

    if streamed:
        pl.when(pl.program_id(0) == 0)(gather)
        columns(pl.program_id(0), slice(None))
    else:
        gather()

        @pl.loop(0, ff // tile)
        def _(j):
            columns(j, pl.ds(pl.multiple_of(j * tile, tile), tile))


def back_kernel(m, hot_rows, cold_rows, n_parts, n_grads, share, tailed, waits, plan, *refs):
    sums, grads = refs[:n_parts], refs[n_parts : n_parts + n_grads]
    weight, refs = refs[n_parts + n_grads], refs[n_parts + n_grads + 1 + waits :]
    outs, g_hot, g_cold = refs[:INNER], refs[INNER], refs[INNER + 1]
    hots, colds = m * hot_rows, m * cold_rows
    feat, ff = weight.shape[1:]
    width = outs[0].shape[1]
    tile = 512 if feat % 512 == 0 else feat
    tp = lax.axis_index("tp")
    hot = hot_of(plan, lax.axis_index("ep"))

    def put(columns, back_hot, back_cold):
        for d in range(INNER):
            outs[d][:hots, columns] = back_hot[d * hots : (d + 1) * hots].astype(BF16)
            outs[d][hots:, columns] = back_cold[d * colds : (d + 1) * colds].astype(BF16)

    ends = []
    for first, piece, target in ((0, hots, g_hot), (INNER * hots, colds, g_cold)):
        made = []
        per = 1 if piece % 16 == 0 else INNER
        for d in range(0, INNER, per):
            count = piece * per
            now = slice(first + d * piece, first + d * piece + count)
            hidden = sums[0][now, :ff].astype(F32)
            for more in sums[1:]:
                hidden = hidden + more[now, :ff].astype(F32)
            if n_grads == 1:
                row_grad = grads[0][now].astype(F32)
            else:
                mine, other = (g[now, ff:].astype(F32) for g in grads)
                even = tp == 0
                row_grad = jnp.concatenate(
                    [jnp.where(even, mine, other), jnp.where(even, other, mine)], 1
                )
            sig = 1.0 / (1.0 + jnp.exp(-hidden))
            act = (hidden * sig).astype(BF16).astype(F32)
            hidden_grad = row_grad * (sig * (1.0 + hidden * (1.0 - sig)))
            target[d * piece : d * piece + count] = hidden_grad.astype(BF16)
            half = None
            for n in range(ff // share):
                piece_act = jnp.where(tp == n, act[:, n * share : (n + 1) * share], 0.0)
                half = piece_act if half is None else half + piece_act
            if tailed:
                gate_grad = jnp.sum(act * row_grad, 1, keepdims=True)
                high = gate_grad.astype(BF16).astype(F32)
                low = gate_grad - high
                lane = lax.broadcasted_iota(I32, (count, TAIL), 1)
                end = jnp.where(lane == 0, high, jnp.where(lane == 1, low, 0.0))
                half = jnp.concatenate([half, end], 1)
            made.append(half)
        ends.append(jnp.concatenate(made, 0))
    put(slice(feat, width), *ends)

    across_rows = (((1,), (1,)), ((), ()))

    def features(j, carry):
        at = pl.ds(pl.multiple_of(j * tile, tile), tile)
        put(
            at,
            lax.dot_general(
                g_hot[...], weight[hot, at, :], across_rows, preferred_element_type=F32
            ),
            lax.dot_general(
                g_cold[...], weight[1 - hot, at, :], across_rows, preferred_element_type=F32
            ),
        )
        return carry

    lax.fori_loop(0, feat // tile, features, 0)


def expand_kernel(m, topk, share, c, n_more, waits, *refs):
    blocks, picks, marks, refs = refs[:INNER], refs[INNER : INNER + m], refs[INNER + m], refs[INNER + m + 1 :]
    tailed = c == 0
    rests, refs = ([], refs) if tailed else (refs[:m], refs[m:])
    more, outs, apart = refs[:n_more], refs[n_more + waits :][:m], refs[n_more + waits + m :]
    width = outs[0].shape[1]
    feat = width - share - TAIL

    def add(columns, rows, copies=()):
        for s in range(m):
            total = jnp.dot(picks[s][...], rows, preferred_element_type=F32)
            if more:
                total = total + more[s][:, columns].astype(F32)
            outs[s][:, columns] = total.astype(BF16)
            for copy in copies[s : s + 1]:
                copy[...] = total.astype(BF16)

    def joined(columns):
        return rows_joined([b[:, columns] for b in blocks])

    step = 512 if feat % 512 == 0 else 128
    for at in range(0, feat, step):
        add(slice(at, at + step), joined(slice(at, at + step)))
    mark = marks[...]
    gate = mark[:, 2 * topk : 2 * topk + 1]
    columns = slice(feat, feat + share)
    act = joined(columns).astype(F32)
    add(columns, (gate * act).astype(BF16))
    columns = slice(feat + share, width)
    if tailed:
        end = joined(columns).astype(F32)
        gate_grad = (end[:, 0:1] + end[:, 1:2]) / jnp.where(gate > 0.0, gate, 1.0)
    else:
        grad = picked(picks, rests, slice(0, share))
        gate_grad = jnp.sum(act * grad, 1, keepdims=True)
    high = gate_grad.astype(BF16).astype(F32)
    lane = lax.broadcasted_iota(I32, mark.shape, 1)
    values = jnp.where(lane < topk, high, gate_grad - high)
    end = jnp.where((lane < 2 * topk) & (mark > 0.0), values, 0.0)
    add(columns, end.astype(BF16), apart)


def final_kernel(n, n_tails, topk, *refs):
    parts, tails = refs[:n], refs[n : n + n_tails]
    mixed, grad_tokens, grad_gates = refs[n + n_tails :]
    feat, share = grad_tokens.shape[1], mixed.shape[1]

    def total(columns):
        out = parts[0][:, columns].astype(F32)
        for part in parts[1:]:
            out = out + part[:, columns].astype(F32)
        return out

    grad_tokens[...] = total(slice(0, feat)).astype(BF16)
    mixed[...] = total(slice(feat, feat + share)).astype(BF16)
    ends = [tail[...].astype(F32) for tail in tails]
    ends += [part[:, feat + share :].astype(F32) for part in parts if part.shape[1] > feat + share]
    end = ends[0]
    for more in ends[1:]:
        end = end + more
    end = end.T
    grad_gates[...] = end[:topk] + end[topk : 2 * topk]


def up_kernel(n, waits, plan, *refs):
    x_hot, x_cold = refs[:n], refs[n : 2 * n]
    g_hot, g_cold = refs[2 * n : 3 * n], refs[3 * n : 4 * n]
    out, token, all_hot, all_cold = refs[4 * n + waits :]
    tile = out.shape[1]
    e, j = pl.program_id(0), pl.program_id(1)
    hot = hot_of(plan, lax.axis_index("ep"))
    at = pl.ds(pl.multiple_of(j * tile, tile), tile)

    @pl.when((e == 0) & (j == 0))
    def _():
        token[...] = jnp.zeros_like(token)
        all_hot[...] = jnp.concatenate([g[...] for g in g_hot], 0)
        all_cold[...] = jnp.concatenate([g[...] for g in g_cold], 0)

    def total(xs, grads):
        rows = jnp.concatenate([x[:, at] for x in xs], 0)
        out[0] = lax.dot_general(
            rows, grads[...], (((0,), (0,)), ((), ())), preferred_element_type=F32
        ).astype(BF16)

    pl.when(e == hot)(lambda: total(x_hot, all_hot))
    pl.when(e != hot)(lambda: total(x_cold, all_cold))


def on_device(tokens, routes, gates, up_weight, replica_on, grad_out):
    count, feat = tokens.shape
    topk = routes.shape[1]
    experts = replica_on.shape[0]
    share = grad_out.shape[1]
    ff = up_weight.shape[2]
    n_ep, n_tp = lax.axis_size("ep"), lax.axis_size("tp")
    outer = n_ep // INNER
    capacity = 3 * count * topk // (4 * experts)
    hot_rows, cold_rows = 2 * capacity, capacity
    width = feat + share + TAIL
    there = feat + share
    by_hand = n_tp == 2 and outer == CHUNKS
    smem = pl.BlockSpec(memory_space=pltpu.SMEM)

    def along(value, shift):
        pairs = [
            (o * INNER + i, ((o + shift) % outer) * INNER + i)
            for o in range(outer)
            for i in range(INNER)
        ]
        return lax.ppermute(value, "ep", pairs)

    def across(value, d):
        pairs = [(o * INNER + i, o * INNER + (i ^ d)) for o in range(outer) for i in range(INNER)]
        return lax.ppermute(value, "ep", pairs)

    rest_spec = pl.BlockSpec(memory_space=pl.ANY)
    m = max(1, outer // CHUNKS)
    chunks = [list(range(first, first + m)) for first in range(0, outer, m)]
    n = len(chunks)
    rows = m * (hot_rows + cold_rows)
    hots, colds = INNER * m * hot_rows, INNER * m * cold_rows
    sizes = (m, hot_rows, cold_rows)

    def block(shape, dtype=BF16):
        return jax.ShapeDtypeStruct(shape, dtype)

    def fixed(shape):
        return pl.BlockSpec(shape, lambda j: (0,) * len(shape))

    going = {f: k for k, (f, _) in enumerate(PLAN) if f is not None}
    coming = {r: k for k, (_, r) in enumerate(PLAN) if r is not None}

    def weigh(kind):
        return cost(COSTS[kind] * 10**6, COSTS[kind] * 10**4)

    arrived, picks, marks, blocks, sums, grads, partials = {}, {}, {}, {}, {}, {}, {}
    x_hots, x_colds, g_hots, g_colds = {}, {}, {}, {}

    def exchange(k, made):
        blocks[k] = [made[0]] + [across(made[d], d) for d in range(1, INNER)]

    own_rows = m == 1
    made = pl.pallas_call(
        functools.partial(start_kernel, *sizes),
        out_shape=[block((count, share + TAIL))]
        + (
            [block((rows, there))] * INNER
            + [block((INNER * rows, TAIL), F32), block((count, INNER * rows))]
            if own_rows
            else []
        ),
        in_specs=[smem] + [rest_spec] * 4,
        out_specs=whole_specs(1 + (INNER + 2 if own_rows else 0)),
        scratch_shapes=[
            pltpu.VMEM((count, feat), BF16),
            pltpu.VMEM((topk, count), I32),
            pltpu.VMEM((topk, count), F32),
            pltpu.SemaphoreType.DMA((4,)),
        ],
        compiler_params=params(WIDE),
        cost_estimate=weigh("x"),
        name="start",
    )(replica_on, tokens, routes.T, gates.T, grad_out)
    groups = [[o * INNER + i for o in range(outer)] for i in range(INNER)]
    column = lax.all_gather(made[0], "ep", axis_index_groups=groups)
    here = lax.axis_index("ep") // INNER
    rests = [
        lax.dynamic_index_in_dim(column, (here + outer - s) % outer, 0, keepdims=False)
        for s in range(outer)
    ]

    def rests_of(c):
        return [rests[s] for s in chunks[c]]

    last = []
    for c in range(n):
        for s in chunks[c]:
            if s == 0:
                arrived[s] = tokens
            else:
                arrived[s] = along(arrived[s - m], m) if c else along(tokens, s)

    def select(k):
        c = PLAN[k][0]
        made = pl.pallas_call(
            functools.partial(select_kernel, *sizes, topk, share, len(last)),
            out_shape=[block((rows, there))] * INNER
            + [block((INNER * rows, TAIL), F32)]
            + [block((count, INNER * rows))] * m,
            in_specs=[smem] + whole_specs(2 * m) + [rest_spec] * len(last),
            out_specs=whole_specs(INNER + 1 + m),
            compiler_params=params(),
            cost_estimate=weigh("x"),
            name="select",
        )(replica_on, *[arrived[s] for s in chunks[c]], *rests_of(c), *last)
        marks[c], picks[c] = made[INNER], made[INNER + 1 :]
        exchange(k, made)
        last[:] = [picks[c][0]]

    def hidden(c):
        k = going[c]
        tile = 256 if ff % 256 == 0 else ff
        shapes = [(INNER * rows, ff + share), (hots, feat), (colds, feat)]
        streamed = c == 0 and FIRST > 0
        if streamed:
            where = dict(
                grid=(ff // tile,),
                in_specs=[smem]
                + [fixed(b.shape) for b in blocks[k]]
                + [pl.BlockSpec((2, feat, tile), lambda j: (0, 0, j))]
                + [rest_spec] * len(last),
                out_specs=[fixed(shape) for shape in shapes],
            )
        else:
            where = dict(
                in_specs=[smem] + whole_specs(INNER + 1) + [rest_spec] * len(last),
                out_specs=whole_specs(3),
            )
        part, x_hots[c], x_colds[c] = pl.pallas_call(
            functools.partial(hidden_kernel, *sizes, feat, streamed, len(last)),
            out_shape=[block(shape) for shape in shapes],
            **where,
            compiler_params=params(WIDE if c == 0 and FIRST == 2 else LIMIT),
            cost_estimate=weigh("h"),
            name="hidden",
        )(replica_on, *blocks[k], up_weight, *last)
        last[:] = [x_colds[c]]
        if n_tp == 2:
            sums[c] = [part, lax.ppermute(part, "tp", [(0, 1), (1, 0)])]
            grads[c] = sums[c]
        else:
            sums[c] = [lax.psum(part[:, :ff].astype(F32), "tp")]
            grads[c] = [lax.all_gather(part[:, ff:], "tp", axis=1, tiled=True)]

    def step(k):
        f, c = PLAN[k]
        if c is None:
            return select(k)
        made = pl.pallas_call(
            functools.partial(
                back_kernel, *sizes, len(sums[c]), len(grads[c]), share, c == 0, len(last)
            ),
            out_shape=[block((rows, there if c else width))] * INNER
            + [block((hots, ff)), block((colds, ff))],
            in_specs=[smem]
            + whole_specs(len(sums[c]) + len(grads[c]) + 1)
            + [rest_spec] * len(last),
            out_specs=whole_specs(INNER + 2),
            compiler_params=params(),
            cost_estimate=weigh("b"),
            name="back",
        )(replica_on, *sums[c], *grads[c], up_weight, *last)
        g_hots[c], g_colds[c] = made[INNER : INNER + 2]
        exchange(k, made)
        last[:] = [g_colds[c]]

    def expand(c):
        more = [along(partials[s - m], m) for s in chunks[c]] if c > 1 else []
        sources = rests_of(c) if c else []
        apart = [block((count, TAIL))] if c == n - 1 and by_hand else []
        k = coming[c]
        made = pl.pallas_call(
            functools.partial(expand_kernel, m, topk, share, c, len(more), len(last)),
            out_shape=[block((count, width))] * m + apart,
            in_specs=whole_specs(INNER + m + 1 + len(sources) + len(more))
            + [rest_spec] * len(last),
            out_specs=whole_specs(m + len(apart)),
            compiler_params=params(),
            cost_estimate=weigh("e"),
            name="expand",
        )(*blocks[k], *picks[c], marks[c], *sources, *more, *last)
        for s, value in zip(chunks[c], made):
            partials[s] = value
        if apart:
            partials["apart"] = made[m]
        last[:] = [made[0]]

    def weight_grad():
        tile = 512 if feat % 512 == 0 else feat
        grad_up, token = pl.pallas_call(
            functools.partial(up_kernel, n, len(last)),
            out_shape=[block(up_weight.shape), block((8, 128), F32)],
            grid=(up_weight.shape[0], feat // tile),
            in_specs=[smem] + whole_specs(4 * n) + [rest_spec] * len(last),
            out_specs=[
                pl.BlockSpec((1, tile, ff), lambda e, j: (e, j, 0)),
                pl.BlockSpec((8, 128), lambda e, j: (0, 0)),
            ],
            scratch_shapes=[
                pltpu.VMEM((n * hots, ff), BF16),
                pltpu.VMEM((n * colds, ff), BF16),
            ],
            compiler_params=params(),
            cost_estimate=weigh("u"),
            name="grad_up",
        )(
            replica_on,
            *[x_hots[c] for c in range(n)],
            *[x_colds[c] for c in range(n)],
            *[g_hots[c] for c in range(n)],
            *[g_colds[c] for c in range(n)],
            *last,
        )
        last[:] = [token]
        return grad_up

    if own_rows:
        marks[0], picks[0] = made[INNER + 1], made[INNER + 2 :]
        exchange(0, made[1 : INNER + 1])
    else:
        select(0)
    grad_up = None
    for word in ORDER:
        number = int(word[1:] or 0)
        if word[0] == "u":
            grad_up = weight_grad()
        elif word[0] == "r":
            last.append(sums[number][-1])
        else:
            {"x": step, "h": hidden, "e": expand}[word[0]](number)

    sums_back = [along(partials[s], m) for s in chunks[n - 1]]
    if by_hand:
        pairs = [
            (
                (o * INNER + i) * n_tp + t,
                (((o + m) % outer) * INNER + i) * n_tp + 1 - t,
            )
            for o in range(outer)
            for i in range(INNER)
            for t in range(n_tp)
        ]
        tails = [lax.ppermute(partials["apart"], ("ep", "tp"), pairs)]
        parts = [sums_back[0], partials[0]]
    else:
        parts, tails, halves = [], [], 0.0
        for s, value in zip(chunks[0], sums_back):
            ours = partials[s]
            if s == 0:
                parts += [value[:, :there], ours[:, :there]]
                halves = halves + value[:, there:].astype(F32)
                tails.append(ours[:, there:])
            else:
                parts.append(along(value[:, :there] + ours[:, :there], outer - s))
                halves = halves + along(value[:, there:], outer - s).astype(F32)
                tails.append(along(ours[:, there:], outer - s))
        tails.append(lax.psum(halves, "tp"))
    mixed, grad_tokens, grad_gates = pl.pallas_call(
        functools.partial(final_kernel, len(parts), len(tails), topk),
        out_shape=[block((count, share)), block((count, feat)), block((topk, count), F32)],
        in_specs=whole_specs(len(parts) + len(tails)),
        out_specs=whole_specs(3),
        compiler_params=params(),
        cost_estimate=weigh("e"),
        name="final",
    )(*parts, *tails)
    return mixed, grad_tokens, grad_gates.T, grad_up


def solution(mesh):
    return jax.shard_map(
        on_device,
        mesh=mesh,
        in_specs=(
            P("ep", "tp"),
            P("ep", None),
            P("ep", None),
            P("ep", "tp", None),
            P(),
            P("ep", "tp"),
        ),
        out_specs=(P("ep", "tp"), P("ep", "tp"), P("ep", None), P("ep", "tp", None)),
        check_vma=False,
    )
```

```python
import functools

import jax
import jax.numpy as jnp
from jax import lax
from jax.experimental import pallas as pl
from jax.experimental.pallas import tpu as pltpu
from jax.sharding import PartitionSpec as P

INNER = 4
CHUNKS = 4
PLAN = ((0, None), (1, None), (2, None), (3, None), (None, 1), (None, 2), (None, 3), (None, 0))
ORDER = ('x1', 'h0', 'x2', 'h1', 'x3', 'h2', 'r0', 'x4', 'h3', 'x5', 'r3', 'e1', 'x6', 'e2', 'r2', 'x7', 'e3', 'u', 'e0')
FIRST = 1
COSTS = {'x': 5000, 'b': 20000, 'h': 5000, 'e': 1, 'u': 20000}
TAIL = 128
LIMIT = 20 * 1024 * 1024
WIDE = 56 * 1024 * 1024
F32, BF16, I32 = jnp.float32, jnp.bfloat16, jnp.int32


def params(limit=LIMIT):
    return pltpu.CompilerParams(vmem_limit_bytes=limit)


def cost(flops, moved):
    return pl.CostEstimate(flops=int(flops), bytes_accessed=int(moved), transcendentals=0)


def whole_specs(n):
    return [pl.BlockSpec(memory_space=pltpu.VMEM)] * n


def hot_of(plan, device):
    return plan[2 * device + 1]


def rows_joined(pieces):
    if all(piece.shape[0] % 16 == 0 for piece in pieces):
        return jnp.concatenate(pieces, 0)
    return jnp.concatenate([piece.astype(F32) for piece in pieces], 0).astype(BF16)


def row_plan(m, hot_rows, cold_rows, plan, shape, axis):
    rows = m * (hot_rows + cold_rows)
    me = lax.axis_index("ep")
    outer, inner = me // INNER, me % INNER
    spot = lax.broadcasted_iota(I32, shape, axis)
    which = jnp.zeros(shape, I32)
    for d in range(1, INNER):
        which += (spot >= d * rows).astype(I32)
    within = spot - which * rows
    is_hot = within < m * hot_rows
    group = jnp.zeros(shape, I32)
    for s in range(1, m):
        edge = jnp.where(is_hot, s * hot_rows, m * hot_rows + s * cold_rows)
        group += (within >= edge).astype(I32)
    slot = jnp.where(is_hot, within - group * hot_rows, within - m * hot_rows - group * cold_rows)
    expert = jnp.zeros(shape, I32)
    for d in range(INNER):
        device = outer * INNER + (inner ^ d)
        hot = hot_of(plan, device)
        ids = jnp.where(is_hot, 2 * device + hot, 2 * device + 1 - hot)
        expert = jnp.where(which == d, ids, expert)
    return expert.astype(F32), slot.astype(F32), group


def pick_rows(m, hot_rows, cold_rows, topk, plan, tails):
    count = tails[0].shape[0]
    cols = INNER * m * (hot_rows + cold_rows)
    expert, slot, group = (
        value[0:1] for value in row_plan(m, hot_rows, cold_rows, plan, (8, cols), 1)
    )
    before = lax.broadcasted_iota(I32, (count, count), 1) < lax.broadcasted_iota(I32, (count, count), 0)
    before = jnp.where(before, 1.0, 0.0).astype(BF16)
    found = []
    for s, ids in enumerate(tails):
        match = ids[:, 0:1] == expert
        for k in range(1, topk):
            match = match | (ids[:, k : k + 1] == expert)
        ones = jnp.where(match, 1.0, 0.0)
        rank = jnp.dot(before, ones.astype(BF16), preferred_element_type=F32)
        found.append(jnp.where((rank == slot) & (group == s), ones, 0.0).astype(BF16))
    return found


def picked(picks, sources, columns):
    total = None
    for pick, source in zip(picks, sources):
        part = lax.dot_general(
            pick[...], source[:, columns], (((0,), (0,)), ((), ())), preferred_element_type=F32
        )
        total = part if total is None else total + part
    return total


def select_all(m, hot_rows, cold_rows, topk, share, skip, plan, picks, tokens, rests, outs, marks):
    rows, width = outs[0].shape
    feat = width - share
    expert, _, _ = row_plan(m, hot_rows, cold_rows, plan, (INNER * rows, TAIL), 0)
    tail = picked(picks, rests, slice(skip + share, skip + share + TAIL))
    gate = (tail[:, 2 * topk : 3 * topk] + tail[:, 3 * topk : 4 * topk]) + tail[:, 4 * topk : 5 * topk]
    gate = jnp.sum(jnp.where(tail[:, :topk] == expert[:, :topk], gate, 0.0), 1, keepdims=True)
    lane = lax.broadcasted_iota(I32, tail.shape, 1)
    own = jnp.where((tail == expert) & (lane < 2 * topk), 1.0, 0.0)
    marks[...] = jnp.where(lane == 2 * topk, gate, own)
    step = 512 if feat % 512 == 0 else 128
    for at in [*range(0, feat, step), feat]:
        if at < feat:
            columns = slice(at, at + step)
            total = picked(picks, tokens, columns)
        else:
            columns = slice(feat, width)
            total = gate * picked(picks, rests, slice(skip, skip + share))
        for d in range(INNER):
            outs[d][:, columns] = total[d * rows : (d + 1) * rows].astype(BF16)


def start_kernel(m, hot_rows, cold_rows, plan, tokens, routes, gates, grad_out, *refs):
    out, refs = refs[0], refs[1:]
    here, here_routes, here_gates, sems = refs[-4:]
    outs, marks, picks = refs[:INNER], refs[INNER:-4][:1], refs[INNER:-4][1:]
    count, feat = tokens.shape
    share = grad_out.shape[1]
    topk = routes.shape[0]
    copies = [
        pltpu.make_async_copy(source, target, sems.at[n])
        for n, (source, target) in enumerate(
            (
                (routes, here_routes),
                (gates, here_gates),
                (tokens, here),
                (grad_out, out.at[:, :share]),
            )
        )
    ]
    for copy in copies:
        copy.start()
    for copy in copies[:2]:
        copy.wait()
    ids = here_routes[...].astype(F32)
    gate = here_gates[...]
    high = gate.astype(BF16).astype(F32)
    middle = (gate - high).astype(BF16).astype(F32)
    low = (gate - high - middle).astype(BF16).astype(F32)
    rest = jnp.zeros((TAIL - 5 * topk, count), F32)
    tail = jnp.concatenate([ids, ids, high, middle, low, rest], 0).T
    out[:, share:] = tail.astype(BF16)
    if picks:
        picks[0][...] = pick_rows(m, hot_rows, cold_rows, topk, plan, [tail])[0]
    for copy in copies[2:]:
        copy.wait()
    if picks:
        select_all(
            m, hot_rows, cold_rows, topk, share, 0, plan, picks, [here], [out], outs, marks[0]
        )


def select_kernel(m, hot_rows, cold_rows, topk, share, skip, waits, plan, *refs):
    tokens, rests, refs = refs[:m], refs[m : 2 * m], refs[2 * m + waits :]
    outs, marks, picks, joined = refs[:INNER], refs[INNER], refs[INNER + 1 : INNER + 1 + m], refs[INNER + 1 + m :]
    tails = [rest[:, skip + share :].astype(F32) for rest in rests]
    for pick, found in zip(picks, pick_rows(m, hot_rows, cold_rows, topk, plan, tails)):
        pick[...] = found
    select_all(m, hot_rows, cold_rows, topk, share, skip, plan, picks, tokens, rests, outs, marks)
    for token, rest, target in zip(tokens, rests, joined):
        feat = token.shape[1]
        target[:, :feat] = token[...]
        target[:, feat:] = rest[...]


def hidden_kernel(m, hot_rows, cold_rows, feat, streamed, waits, plan, *refs):
    blocks = refs[:INNER]
    weight, part, x_hot, x_cold = refs[INNER], *refs[INNER + 1 + waits :]
    hots = INNER * m * hot_rows
    share = blocks[0].shape[1] - feat
    ff = part.shape[1] - share
    tile = 256 if ff % 256 == 0 else ff
    hot = hot_of(plan, lax.axis_index("ep"))
    split = m * hot_rows

    def gather():
        x_hot[...] = rows_joined([b[:split, :feat] for b in blocks])
        x_cold[...] = rows_joined([b[split:, :feat] for b in blocks])
        part[:hots, ff:] = rows_joined([b[:split, feat:] for b in blocks])
        part[hots:, ff:] = rows_joined([b[split:, feat:] for b in blocks])

    def columns(j, source):
        at = pl.ds(pl.multiple_of(j * tile, tile), tile)
        part[:hots, at] = jnp.dot(
            x_hot[...], weight[hot, :, source], preferred_element_type=F32
        ).astype(BF16)
        part[hots:, at] = jnp.dot(
            x_cold[...], weight[1 - hot, :, source], preferred_element_type=F32
        ).astype(BF16)

    if streamed:
        pl.when(pl.program_id(0) == 0)(gather)
        columns(pl.program_id(0), slice(None))
    else:
        gather()

        @pl.loop(0, ff // tile)
        def _(j):
            columns(j, pl.ds(pl.multiple_of(j * tile, tile), tile))


def back_kernel(m, hot_rows, cold_rows, n_parts, n_grads, share, tailed, waits, plan, *refs):
    sums, grads = refs[:n_parts], refs[n_parts : n_parts + n_grads]
    weight, refs = refs[n_parts + n_grads], refs[n_parts + n_grads + 1 + waits :]
    outs, g_hot, g_cold = refs[:INNER], refs[INNER], refs[INNER + 1]
    hots, colds = m * hot_rows, m * cold_rows
    feat, ff = weight.shape[1:]
    width = outs[0].shape[1]
    tile = 512 if feat % 512 == 0 else feat
    tp = lax.axis_index("tp")
    hot = hot_of(plan, lax.axis_index("ep"))

    def put(columns, back_hot, back_cold):
        for d in range(INNER):
            outs[d][:hots, columns] = back_hot[d * hots : (d + 1) * hots].astype(BF16)
            outs[d][hots:, columns] = back_cold[d * colds : (d + 1) * colds].astype(BF16)

    ends = []
    for first, piece, target in ((0, hots, g_hot), (INNER * hots, colds, g_cold)):
        made = []
        per = 1 if piece % 16 == 0 else INNER
        for d in range(0, INNER, per):
            count = piece * per
            now = slice(first + d * piece, first + d * piece + count)
            hidden = sums[0][now, :ff].astype(F32)
            for more in sums[1:]:
                hidden = hidden + more[now, :ff].astype(F32)
            if n_grads == 1:
                row_grad = grads[0][now].astype(F32)
            else:
                mine, other = (g[now, ff:].astype(F32) for g in grads)
                even = tp == 0
                row_grad = jnp.concatenate(
                    [jnp.where(even, mine, other), jnp.where(even, other, mine)], 1
                )
            sig = 1.0 / (1.0 + jnp.exp(-hidden))
            act = (hidden * sig).astype(BF16).astype(F32)
            hidden_grad = row_grad * (sig * (1.0 + hidden * (1.0 - sig)))
            target[d * piece : d * piece + count] = hidden_grad.astype(BF16)
            half = None
            for n in range(ff // share):
                piece_act = jnp.where(tp == n, act[:, n * share : (n + 1) * share], 0.0)
                half = piece_act if half is None else half + piece_act
            if tailed:
                gate_grad = jnp.sum(act * row_grad, 1, keepdims=True)
                high = gate_grad.astype(BF16).astype(F32)
                low = gate_grad - high
                lane = lax.broadcasted_iota(I32, (count, TAIL), 1)
                end = jnp.where(lane == 0, high, jnp.where(lane == 1, low, 0.0))
                half = jnp.concatenate([half, end], 1)
            made.append(half)
        ends.append(jnp.concatenate(made, 0))
    put(slice(feat, width), *ends)

    across_rows = (((1,), (1,)), ((), ()))

    def features(j, carry):
        at = pl.ds(pl.multiple_of(j * tile, tile), tile)
        put(
            at,
            lax.dot_general(
                g_hot[...], weight[hot, at, :], across_rows, preferred_element_type=F32
            ),
            lax.dot_general(
                g_cold[...], weight[1 - hot, at, :], across_rows, preferred_element_type=F32
            ),
        )
        return carry

    lax.fori_loop(0, feat // tile, features, 0)


def expand_kernel(m, topk, share, tailed, skip, n_more, waits, *refs):
    blocks, picks, marks, refs = refs[:INNER], refs[INNER : INNER + m], refs[INNER + m], refs[INNER + m + 1 :]
    rests, refs = ([], refs) if tailed else (refs[:m], refs[m:])
    more, outs, apart = refs[:n_more], refs[n_more + waits :][:m], refs[n_more + waits + m :]
    width = outs[0].shape[1]
    feat = width - share - TAIL

    def add(columns, rows, copies=()):
        for s in range(m):
            total = jnp.dot(picks[s][...], rows, preferred_element_type=F32)
            if more:
                total = total + more[s][:, columns].astype(F32)
            outs[s][:, columns] = total.astype(BF16)
            for copy in copies[s : s + 1]:
                copy[...] = total.astype(BF16)

    def joined(columns):
        return rows_joined([b[:, columns] for b in blocks])

    step = 512 if feat % 512 == 0 else 128
    for at in range(0, feat, step):
        add(slice(at, at + step), joined(slice(at, at + step)))
    mark = marks[...]
    gate = mark[:, 2 * topk : 2 * topk + 1]
    columns = slice(feat, feat + share)
    act = joined(columns).astype(F32)
    add(columns, (gate * act).astype(BF16))
    columns = slice(feat + share, width)
    if tailed:
        end = joined(columns).astype(F32)
        gate_grad = (end[:, 0:1] + end[:, 1:2]) / jnp.where(gate > 0.0, gate, 1.0)
    else:
        grad = picked(picks, rests, slice(skip, skip + share))
        gate_grad = jnp.sum(act * grad, 1, keepdims=True)
    high = gate_grad.astype(BF16).astype(F32)
    lane = lax.broadcasted_iota(I32, mark.shape, 1)
    values = jnp.where(lane < topk, high, gate_grad - high)
    end = jnp.where((lane < 2 * topk) & (mark > 0.0), values, 0.0)
    add(columns, end.astype(BF16), apart)


def final_kernel(n, n_tails, topk, *refs):
    parts, tails = refs[:n], refs[n : n + n_tails]
    mixed, grad_tokens, grad_gates = refs[n + n_tails :]
    feat, share = grad_tokens.shape[1], mixed.shape[1]

    def total(columns):
        out = parts[0][:, columns].astype(F32)
        for part in parts[1:]:
            out = out + part[:, columns].astype(F32)
        return out

    grad_tokens[...] = total(slice(0, feat)).astype(BF16)
    mixed[...] = total(slice(feat, feat + share)).astype(BF16)
    ends = [tail[...].astype(F32) for tail in tails]
    ends += [part[:, feat + share :].astype(F32) for part in parts if part.shape[1] > feat + share]
    end = ends[0]
    for more in ends[1:]:
        end = end + more
    end = end.T
    grad_gates[...] = end[:topk] + end[topk : 2 * topk]


def up_kernel(n, waits, plan, *refs):
    x_hot, x_cold = refs[:n], refs[n : 2 * n]
    g_hot, g_cold = refs[2 * n : 3 * n], refs[3 * n : 4 * n]
    out, token, all_hot, all_cold = refs[4 * n + waits :]
    tile = out.shape[1]
    e, j = pl.program_id(0), pl.program_id(1)
    hot = hot_of(plan, lax.axis_index("ep"))
    at = pl.ds(pl.multiple_of(j * tile, tile), tile)

    @pl.when((e == 0) & (j == 0))
    def _():
        token[...] = jnp.zeros_like(token)
        all_hot[...] = jnp.concatenate([g[...] for g in g_hot], 0)
        all_cold[...] = jnp.concatenate([g[...] for g in g_cold], 0)

    def total(xs, grads):
        rows = jnp.concatenate([x[:, at] for x in xs], 0)
        out[0] = lax.dot_general(
            rows, grads[...], (((0,), (0,)), ((), ())), preferred_element_type=F32
        ).astype(BF16)

    pl.when(e == hot)(lambda: total(x_hot, all_hot))
    pl.when(e != hot)(lambda: total(x_cold, all_cold))


def on_device(tokens, routes, gates, up_weight, replica_on, grad_out):
    count, feat = tokens.shape
    topk = routes.shape[1]
    experts = replica_on.shape[0]
    share = grad_out.shape[1]
    ff = up_weight.shape[2]
    n_ep, n_tp = lax.axis_size("ep"), lax.axis_size("tp")
    outer = n_ep // INNER
    capacity = 3 * count * topk // (4 * experts)
    hot_rows, cold_rows = 2 * capacity, capacity
    width = feat + share + TAIL
    there = feat + share
    by_hand = n_tp == 2 and outer == CHUNKS
    smem = pl.BlockSpec(memory_space=pltpu.SMEM)

    def along(value, shift):
        pairs = [
            (o * INNER + i, ((o + shift) % outer) * INNER + i)
            for o in range(outer)
            for i in range(INNER)
        ]
        return lax.ppermute(value, "ep", pairs)

    def across(value, d):
        pairs = [(o * INNER + i, o * INNER + (i ^ d)) for o in range(outer) for i in range(INNER)]
        return lax.ppermute(value, "ep", pairs)

    rest_spec = pl.BlockSpec(memory_space=pl.ANY)
    m = max(1, outer // CHUNKS)
    chunks = [list(range(first, first + m)) for first in range(0, outer, m)]
    n = len(chunks)
    rows = m * (hot_rows + cold_rows)
    hots, colds = INNER * m * hot_rows, INNER * m * cold_rows
    sizes = (m, hot_rows, cold_rows)

    def block(shape, dtype=BF16):
        return jax.ShapeDtypeStruct(shape, dtype)

    def fixed(shape):
        return pl.BlockSpec(shape, lambda j: (0,) * len(shape))

    going = {f: k for k, (f, _) in enumerate(PLAN) if f is not None}
    coming = {r: k for k, (_, r) in enumerate(PLAN) if r is not None}

    def weigh(kind):
        return cost(COSTS[kind] * 10**6, COSTS[kind] * 10**4)

    arrived, picks, marks, blocks, sums, grads, partials = {}, {}, {}, {}, {}, {}, {}
    x_hots, x_colds, g_hots, g_colds = {}, {}, {}, {}

    def exchange(k, made):
        blocks[k] = [made[0]] + [across(made[d], d) for d in range(1, INNER)]

    own_rows = m == 1
    made = pl.pallas_call(
        functools.partial(start_kernel, *sizes),
        out_shape=[block((count, share + TAIL))]
        + (
            [block((rows, there))] * INNER
            + [block((INNER * rows, TAIL), F32), block((count, INNER * rows))]
            if own_rows
            else []
        ),
        in_specs=[smem] + [rest_spec] * 4,
        out_specs=whole_specs(1 + (INNER + 2 if own_rows else 0)),
        scratch_shapes=[
            pltpu.VMEM((count, feat), BF16),
            pltpu.VMEM((topk, count), I32),
            pltpu.VMEM((topk, count), F32),
            pltpu.SemaphoreType.DMA((4,)),
        ],
        compiler_params=params(WIDE),
        cost_estimate=weigh("x"),
        name="start",
    )(replica_on, tokens, routes.T, gates.T, grad_out)
    last = []
    for c in (0, 1):
        for s in chunks[c]:
            if c:
                arrived[s] = [along(piece, m) for piece in arrived[s - m]]
            else:
                arrived[s] = [along(piece, s) if s else piece for piece in (tokens, made[0])]

    def skip_of(c):
        return 0 if c < 2 else feat

    def select(k):
        c = PLAN[k][0]
        joins = m if c == 1 else 0
        chosen = pl.pallas_call(
            functools.partial(select_kernel, *sizes, topk, share, skip_of(c), len(last)),
            out_shape=[block((rows, there))] * INNER
            + [block((INNER * rows, TAIL), F32)]
            + [block((count, INNER * rows))] * m
            + [block((count, width))] * joins,
            in_specs=[smem] + whole_specs(2 * m) + [rest_spec] * len(last),
            out_specs=whole_specs(INNER + 1 + m + joins),
            compiler_params=params(),
            cost_estimate=weigh("x"),
            name="select",
        )(
            replica_on,
            *[arrived[s][0] for s in chunks[c]],
            *[arrived[s][-1] for s in chunks[c]],
            *last,
        )
        marks[c], picks[c] = chosen[INNER], chosen[INNER + 1 : INNER + 1 + m]
        if joins:
            now = chosen[INNER + 1 + m :]
            for after in (2, 3):
                now = [along(value, m) for value in now]
                for s, value in zip(chunks[after], now):
                    arrived[s] = [value]
        exchange(k, chosen)
        last[:] = [picks[c][0]]

    def hidden(c):
        k = going[c]
        tile = 256 if ff % 256 == 0 else ff
        shapes = [(INNER * rows, ff + share), (hots, feat), (colds, feat)]
        streamed = c == 0 and FIRST > 0
        if streamed:
            where = dict(
                grid=(ff // tile,),
                in_specs=[smem]
                + [fixed(b.shape) for b in blocks[k]]
                + [pl.BlockSpec((2, feat, tile), lambda j: (0, 0, j))]
                + [rest_spec] * len(last),
                out_specs=[fixed(shape) for shape in shapes],
            )
        else:
            where = dict(
                in_specs=[smem] + whole_specs(INNER + 1) + [rest_spec] * len(last),
                out_specs=whole_specs(3),
            )
        part, x_hots[c], x_colds[c] = pl.pallas_call(
            functools.partial(hidden_kernel, *sizes, feat, streamed, len(last)),
            out_shape=[block(shape) for shape in shapes],
            **where,
            compiler_params=params(WIDE if c == 0 and FIRST == 2 else LIMIT),
            cost_estimate=weigh("h"),
            name="hidden",
        )(replica_on, *blocks[k], up_weight, *last)
        last[:] = [x_colds[c]]
        if n_tp == 2:
            sums[c] = [part, lax.ppermute(part, "tp", [(0, 1), (1, 0)])]
            grads[c] = sums[c]
        else:
            sums[c] = [lax.psum(part[:, :ff].astype(F32), "tp")]
            grads[c] = [lax.all_gather(part[:, ff:], "tp", axis=1, tiled=True)]

    def step(k):
        f, c = PLAN[k]
        if c is None:
            return select(k)
        made = pl.pallas_call(
            functools.partial(
                back_kernel, *sizes, len(sums[c]), len(grads[c]), share, c == 0, len(last)
            ),
            out_shape=[block((rows, there if c else width))] * INNER
            + [block((hots, ff)), block((colds, ff))],
            in_specs=[smem]
            + whole_specs(len(sums[c]) + len(grads[c]) + 1)
            + [rest_spec] * len(last),
            out_specs=whole_specs(INNER + 2),
            compiler_params=params(),
            cost_estimate=weigh("b"),
            name="back",
        )(replica_on, *sums[c], *grads[c], up_weight, *last)
        g_hots[c], g_colds[c] = made[INNER : INNER + 2]
        exchange(k, made)
        last[:] = [g_colds[c]]

    def expand(c):
        more = [along(partials[s - m], m) for s in chunks[c]] if c > 1 else []
        sources = [arrived[s][-1] for s in chunks[c]] if c else []
        apart = [block((count, TAIL))] if c == n - 1 and by_hand else []
        k = coming[c]
        made = pl.pallas_call(
            functools.partial(
                expand_kernel, m, topk, share, c == 0, skip_of(c), len(more), len(last)
            ),
            out_shape=[block((count, width))] * m + apart,
            in_specs=whole_specs(INNER + m + 1 + len(sources) + len(more))
            + [rest_spec] * len(last),
            out_specs=whole_specs(m + len(apart)),
            compiler_params=params(),
            cost_estimate=weigh("e"),
            name="expand",
        )(*blocks[k], *picks[c], marks[c], *sources, *more, *last)
        for s, value in zip(chunks[c], made):
            partials[s] = value
        if apart:
            partials["apart"] = made[m]
        last[:] = [made[0]]

    def weight_grad():
        tile = 512 if feat % 512 == 0 else feat
        grad_up, token = pl.pallas_call(
            functools.partial(up_kernel, n, len(last)),
            out_shape=[block(up_weight.shape), block((8, 128), F32)],
            grid=(up_weight.shape[0], feat // tile),
            in_specs=[smem] + whole_specs(4 * n) + [rest_spec] * len(last),
            out_specs=[
                pl.BlockSpec((1, tile, ff), lambda e, j: (e, j, 0)),
                pl.BlockSpec((8, 128), lambda e, j: (0, 0)),
            ],
            scratch_shapes=[
                pltpu.VMEM((n * hots, ff), BF16),
                pltpu.VMEM((n * colds, ff), BF16),
            ],
            compiler_params=params(),
            cost_estimate=weigh("u"),
            name="grad_up",
        )(
            replica_on,
            *[x_hots[c] for c in range(n)],
            *[x_colds[c] for c in range(n)],
            *[g_hots[c] for c in range(n)],
            *[g_colds[c] for c in range(n)],
            *last,
        )
        last[:] = [token]
        return grad_up

    if own_rows:
        marks[0], picks[0] = made[INNER + 1], made[INNER + 2 :]
        exchange(0, made[1 : INNER + 1])
    else:
        select(0)
    grad_up = None
    for word in ORDER:
        number = int(word[1:] or 0)
        if word[0] == "u":
            grad_up = weight_grad()
        elif word[0] == "r":
            last.append(sums[number][-1])
        else:
            {"x": step, "h": hidden, "e": expand}[word[0]](number)

    sums_back = [along(partials[s], m) for s in chunks[n - 1]]
    if by_hand:
        pairs = [
            (
                (o * INNER + i) * n_tp + t,
                (((o + m) % outer) * INNER + i) * n_tp + 1 - t,
            )
            for o in range(outer)
            for i in range(INNER)
            for t in range(n_tp)
        ]
        tails = [lax.ppermute(partials["apart"], ("ep", "tp"), pairs)]
        parts = [sums_back[0], partials[0]]
    else:
        parts, tails, halves = [], [], 0.0
        for s, value in zip(chunks[0], sums_back):
            ours = partials[s]
            if s == 0:
                parts += [value[:, :there], ours[:, :there]]
                halves = halves + value[:, there:].astype(F32)
                tails.append(ours[:, there:])
            else:
                parts.append(along(value[:, :there] + ours[:, :there], outer - s))
                halves = halves + along(value[:, there:], outer - s).astype(F32)
                tails.append(along(ours[:, there:], outer - s))
        tails.append(lax.psum(halves, "tp"))
    mixed, grad_tokens, grad_gates = pl.pallas_call(
        functools.partial(final_kernel, len(parts), len(tails), topk),
        out_shape=[block((count, share)), block((count, feat)), block((topk, count), F32)],
        in_specs=whole_specs(len(parts) + len(tails)),
        out_specs=whole_specs(3),
        compiler_params=params(),
        cost_estimate=weigh("e"),
        name="final",
    )(*parts, *tails)
    return mixed, grad_tokens, grad_gates.T, grad_up


def solution(mesh):
    return jax.shard_map(
        on_device,
        mesh=mesh,
        in_specs=(
            P("ep", "tp"),
            P("ep", None),
            P("ep", None),
            P("ep", "tp", None),
            P(),
            P("ep", "tp"),
        ),
        out_specs=(P("ep", "tp"), P("ep", "tp"), P("ep", None), P("ep", "tp", None)),
        check_vma=False,
    )
```

```python
import functools

import jax
import jax.numpy as jnp
from jax import lax
from jax.experimental import pallas as pl
from jax.experimental.pallas import tpu as pltpu
from jax.sharding import PartitionSpec as P

INNER = 4
CHUNKS = 4
PLAN = ((0, None), (1, None), (2, None), (3, None), (None, 1), (None, 2), (None, 3), (None, 0))
ORDER = ('x1', 'h0', 'x2', 'h1', 'x3', 'h2', 'r0', 'x4', 'h3', 'x5', 'r3', 'e1', 'x6', 'e2', 'r2', 'x7', 'z', 'e3', 'u', 'e0')
FIRST = 1
COSTS = {'x': 5000, 'b': 20000, 'h': 5000, 'e': 1, 'u': 20000}
TAIL = 128
LIMIT = 20 * 1024 * 1024
WIDE = 56 * 1024 * 1024
F32, BF16, I32 = jnp.float32, jnp.bfloat16, jnp.int32


def params(limit=LIMIT):
    return pltpu.CompilerParams(vmem_limit_bytes=limit)


def cost(flops, moved):
    return pl.CostEstimate(flops=int(flops), bytes_accessed=int(moved), transcendentals=0)


def whole_specs(n):
    return [pl.BlockSpec(memory_space=pltpu.VMEM)] * n


def hot_of(plan, device):
    return plan[2 * device + 1]


def rows_joined(pieces):
    if all(piece.shape[0] % 16 == 0 for piece in pieces):
        return jnp.concatenate(pieces, 0)
    return jnp.concatenate([piece.astype(F32) for piece in pieces], 0).astype(BF16)


def row_plan(m, hot_rows, cold_rows, plan, shape, axis):
    rows = m * (hot_rows + cold_rows)
    me = lax.axis_index("ep")
    outer, inner = me // INNER, me % INNER
    spot = lax.broadcasted_iota(I32, shape, axis)
    which = jnp.zeros(shape, I32)
    for d in range(1, INNER):
        which += (spot >= d * rows).astype(I32)
    within = spot - which * rows
    is_hot = within < m * hot_rows
    group = jnp.zeros(shape, I32)
    for s in range(1, m):
        edge = jnp.where(is_hot, s * hot_rows, m * hot_rows + s * cold_rows)
        group += (within >= edge).astype(I32)
    slot = jnp.where(is_hot, within - group * hot_rows, within - m * hot_rows - group * cold_rows)
    expert = jnp.zeros(shape, I32)
    for d in range(INNER):
        device = outer * INNER + (inner ^ d)
        hot = hot_of(plan, device)
        ids = jnp.where(is_hot, 2 * device + hot, 2 * device + 1 - hot)
        expert = jnp.where(which == d, ids, expert)
    return expert.astype(F32), slot.astype(F32), group


def pick_rows(m, hot_rows, cold_rows, topk, plan, tails):
    count = tails[0].shape[0]
    cols = INNER * m * (hot_rows + cold_rows)
    expert, slot, group = (
        value[0:1] for value in row_plan(m, hot_rows, cold_rows, plan, (8, cols), 1)
    )
    before = lax.broadcasted_iota(I32, (count, count), 1) < lax.broadcasted_iota(I32, (count, count), 0)
    before = jnp.where(before, 1.0, 0.0).astype(BF16)
    found = []
    for s, ids in enumerate(tails):
        match = ids[:, 0:1] == expert
        for k in range(1, topk):
            match = match | (ids[:, k : k + 1] == expert)
        ones = jnp.where(match, 1.0, 0.0)
        rank = jnp.dot(before, ones.astype(BF16), preferred_element_type=F32)
        found.append(jnp.where((rank == slot) & (group == s), ones, 0.0).astype(BF16))
    return found


def picked(picks, sources, columns):
    total = None
    for pick, source in zip(picks, sources):
        part = lax.dot_general(
            pick[...], source[:, columns], (((0,), (0,)), ((), ())), preferred_element_type=F32
        )
        total = part if total is None else total + part
    return total


def select_all(m, hot_rows, cold_rows, topk, share, skip, plan, picks, tokens, rests, outs, marks):
    rows, width = outs[0].shape
    feat = width - share
    expert, _, _ = row_plan(m, hot_rows, cold_rows, plan, (INNER * rows, TAIL), 0)
    tail = picked(picks, rests, slice(skip + share, skip + share + TAIL))
    gate = (tail[:, 2 * topk : 3 * topk] + tail[:, 3 * topk : 4 * topk]) + tail[:, 4 * topk : 5 * topk]
    gate = jnp.sum(jnp.where(tail[:, :topk] == expert[:, :topk], gate, 0.0), 1, keepdims=True)
    lane = lax.broadcasted_iota(I32, tail.shape, 1)
    own = jnp.where((tail == expert) & (lane < 2 * topk), 1.0, 0.0)
    marks[...] = jnp.where(lane == 2 * topk, gate, own)
    step = 512 if feat % 512 == 0 else 128
    for at in [*range(0, feat, step), feat]:
        if at < feat:
            columns = slice(at, at + step)
            total = picked(picks, tokens, columns)
        else:
            columns = slice(feat, width)
            total = gate * picked(picks, rests, slice(skip, skip + share))
        for d in range(INNER):
            outs[d][:, columns] = total[d * rows : (d + 1) * rows].astype(BF16)


def start_kernel(m, hot_rows, cold_rows, plan, tokens, routes, gates, grad_out, *refs):
    out, refs = refs[0], refs[1:]
    here, here_routes, here_gates, sems = refs[-4:]
    outs, marks, picks = refs[:INNER], refs[INNER:-4][:1], refs[INNER:-4][1:]
    count, feat = tokens.shape
    share = grad_out.shape[1]
    topk = routes.shape[0]
    copies = [
        pltpu.make_async_copy(source, target, sems.at[n])
        for n, (source, target) in enumerate(
            (
                (routes, here_routes),
                (gates, here_gates),
                (tokens, here),
                (grad_out, out.at[:, :share]),
            )
        )
    ]
    for copy in copies:
        copy.start()
    for copy in copies[:2]:
        copy.wait()
    ids = here_routes[...].astype(F32)
    gate = here_gates[...]
    high = gate.astype(BF16).astype(F32)
    middle = (gate - high).astype(BF16).astype(F32)
    low = (gate - high - middle).astype(BF16).astype(F32)
    rest = jnp.zeros((TAIL - 5 * topk, count), F32)
    tail = jnp.concatenate([ids, ids, high, middle, low, rest], 0).T
    out[:, share:] = tail.astype(BF16)
    if picks:
        picks[0][...] = pick_rows(m, hot_rows, cold_rows, topk, plan, [tail])[0]
    for copy in copies[2:]:
        copy.wait()
    if picks:
        select_all(
            m, hot_rows, cold_rows, topk, share, 0, plan, picks, [here], [out], outs, marks[0]
        )


def select_kernel(m, hot_rows, cold_rows, topk, share, skip, waits, plan, *refs):
    tokens, rests, refs = refs[:m], refs[m : 2 * m], refs[2 * m + waits :]
    outs, marks, picks, joined = refs[:INNER], refs[INNER], refs[INNER + 1 : INNER + 1 + m], refs[INNER + 1 + m :]
    tails = [rest[:, skip + share :].astype(F32) for rest in rests]
    for pick, found in zip(picks, pick_rows(m, hot_rows, cold_rows, topk, plan, tails)):
        pick[...] = found
    select_all(m, hot_rows, cold_rows, topk, share, skip, plan, picks, tokens, rests, outs, marks)
    for token, rest, target in zip(tokens, rests, joined):
        feat = token.shape[1]
        target[:, :feat] = token[...]
        target[:, feat:] = rest[...]


def hidden_kernel(m, hot_rows, cold_rows, feat, streamed, waits, plan, *refs):
    blocks = refs[:INNER]
    weight, part, x_hot, x_cold = refs[INNER], *refs[INNER + 1 + waits :]
    hots = INNER * m * hot_rows
    share = blocks[0].shape[1] - feat
    ff = part.shape[1] - share
    tile = 256 if ff % 256 == 0 else ff
    hot = hot_of(plan, lax.axis_index("ep"))
    split = m * hot_rows

    def gather():
        x_hot[...] = rows_joined([b[:split, :feat] for b in blocks])
        x_cold[...] = rows_joined([b[split:, :feat] for b in blocks])
        part[:hots, ff:] = rows_joined([b[:split, feat:] for b in blocks])
        part[hots:, ff:] = rows_joined([b[split:, feat:] for b in blocks])

    def columns(j, source):
        at = pl.ds(pl.multiple_of(j * tile, tile), tile)
        part[:hots, at] = jnp.dot(
            x_hot[...], weight[hot, :, source], preferred_element_type=F32
        ).astype(BF16)
        part[hots:, at] = jnp.dot(
            x_cold[...], weight[1 - hot, :, source], preferred_element_type=F32
        ).astype(BF16)

    if streamed:
        pl.when(pl.program_id(0) == 0)(gather)
        columns(pl.program_id(0), slice(None))
    else:
        gather()

        @pl.loop(0, ff // tile)
        def _(j):
            columns(j, pl.ds(pl.multiple_of(j * tile, tile), tile))


def back_kernel(m, hot_rows, cold_rows, n_parts, n_grads, share, tailed, waits, plan, *refs):
    sums, grads = refs[:n_parts], refs[n_parts : n_parts + n_grads]
    weight, refs = refs[n_parts + n_grads], refs[n_parts + n_grads + 1 + waits :]
    outs, g_hot, g_cold = refs[:INNER], refs[INNER], refs[INNER + 1]
    hots, colds = m * hot_rows, m * cold_rows
    feat, ff = weight.shape[1:]
    width = outs[0].shape[1]
    tile = 512 if feat % 512 == 0 else feat
    tp = lax.axis_index("tp")
    hot = hot_of(plan, lax.axis_index("ep"))

    def put(columns, back_hot, back_cold):
        for d in range(INNER):
            outs[d][:hots, columns] = back_hot[d * hots : (d + 1) * hots].astype(BF16)
            outs[d][hots:, columns] = back_cold[d * colds : (d + 1) * colds].astype(BF16)

    ends = []
    for first, piece, target in ((0, hots, g_hot), (INNER * hots, colds, g_cold)):
        made = []
        per = 1 if piece % 16 == 0 else INNER
        for d in range(0, INNER, per):
            count = piece * per
            now = slice(first + d * piece, first + d * piece + count)
            hidden = sums[0][now, :ff].astype(F32)
            for more in sums[1:]:
                hidden = hidden + more[now, :ff].astype(F32)
            if n_grads == 1:
                row_grad = grads[0][now].astype(F32)
            else:
                mine, other = (g[now, ff:].astype(F32) for g in grads)
                even = tp == 0
                row_grad = jnp.concatenate(
                    [jnp.where(even, mine, other), jnp.where(even, other, mine)], 1
                )
            sig = 1.0 / (1.0 + jnp.exp(-hidden))
            act = (hidden * sig).astype(BF16).astype(F32)
            hidden_grad = row_grad * (sig * (1.0 + hidden * (1.0 - sig)))
            target[d * piece : d * piece + count] = hidden_grad.astype(BF16)
            half = None
            for n in range(ff // share):
                piece_act = jnp.where(tp == n, act[:, n * share : (n + 1) * share], 0.0)
                half = piece_act if half is None else half + piece_act
            if tailed:
                gate_grad = jnp.sum(act * row_grad, 1, keepdims=True)
                high = gate_grad.astype(BF16).astype(F32)
                low = gate_grad - high
                lane = lax.broadcasted_iota(I32, (count, TAIL), 1)
                end = jnp.where(lane == 0, high, jnp.where(lane == 1, low, 0.0))
                half = jnp.concatenate([half, end], 1)
            made.append(half)
        ends.append(jnp.concatenate(made, 0))
    put(slice(feat, width), *ends)

    across_rows = (((1,), (1,)), ((), ()))

    def features(j, carry):
        at = pl.ds(pl.multiple_of(j * tile, tile), tile)
        put(
            at,
            lax.dot_general(
                g_hot[...], weight[hot, at, :], across_rows, preferred_element_type=F32
            ),
            lax.dot_general(
                g_cold[...], weight[1 - hot, at, :], across_rows, preferred_element_type=F32
            ),
        )
        return carry

    lax.fori_loop(0, feat // tile, features, 0)


def expand_kernel(m, topk, share, tailed, skip, n_more, waits, *refs):
    blocks, picks, marks, refs = refs[:INNER], refs[INNER : INNER + m], refs[INNER + m], refs[INNER + m + 1 :]
    rests, refs = ([], refs) if tailed else (refs[:m], refs[m:])
    more, outs, apart = refs[:n_more], refs[n_more + waits :][:m], refs[n_more + waits + m :]
    width = outs[0].shape[1]
    feat = width - share - TAIL

    def add(columns, rows, copies=()):
        for s in range(m):
            total = jnp.dot(picks[s][...], rows, preferred_element_type=F32)
            if more:
                total = total + more[s][:, columns].astype(F32)
            outs[s][:, columns] = total.astype(BF16)
            for copy in copies[s : s + 1]:
                copy[...] = total.astype(BF16)

    def joined(columns):
        return rows_joined([b[:, columns] for b in blocks])

    step = 512 if feat % 512 == 0 else 128
    for at in range(0, feat, step):
        add(slice(at, at + step), joined(slice(at, at + step)))
    mark = marks[...]
    gate = mark[:, 2 * topk : 2 * topk + 1]
    columns = slice(feat, feat + share)
    act = joined(columns).astype(F32)
    add(columns, (gate * act).astype(BF16))
    columns = slice(feat + share, width)
    if tailed:
        end = joined(columns).astype(F32)
        gate_grad = (end[:, 0:1] + end[:, 1:2]) / jnp.where(gate > 0.0, gate, 1.0)
    else:
        grad = picked(picks, rests, slice(skip, skip + share))
        gate_grad = jnp.sum(act * grad, 1, keepdims=True)
    high = gate_grad.astype(BF16).astype(F32)
    lane = lax.broadcasted_iota(I32, mark.shape, 1)
    values = jnp.where(lane < topk, high, gate_grad - high)
    end = jnp.where((lane < 2 * topk) & (mark > 0.0), values, 0.0)
    add(columns, end.astype(BF16), apart)


def final_kernel(n, n_tails, topk, *refs):
    parts, tails = refs[:n], refs[n : n + n_tails]
    mixed, grad_tokens, grad_gates = refs[n + n_tails :]
    feat, share = grad_tokens.shape[1], mixed.shape[1]

    def total(columns):
        out = parts[0][:, columns].astype(F32)
        for part in parts[1:]:
            out = out + part[:, columns].astype(F32)
        return out

    grad_tokens[...] = total(slice(0, feat)).astype(BF16)
    mixed[...] = total(slice(feat, feat + share)).astype(BF16)
    ends = [tail[...].astype(F32) for tail in tails]
    ends += [part[:, feat + share :].astype(F32) for part in parts if part.shape[1] > feat + share]
    end = ends[0]
    for more in ends[1:]:
        end = end + more
    end = end.T
    grad_gates[...] = end[:topk] + end[topk : 2 * topk]


def up_kernel(n, waits, plan, *refs):
    x_hot, x_cold = refs[:n], refs[n : 2 * n]
    g_hot, g_cold = refs[2 * n : 3 * n], refs[3 * n : 4 * n]
    out, token, all_hot, all_cold = refs[4 * n + waits :]
    tile = out.shape[1]
    e, j = pl.program_id(0), pl.program_id(1)
    hot = hot_of(plan, lax.axis_index("ep"))
    at = pl.ds(pl.multiple_of(j * tile, tile), tile)

    @pl.when((e == 0) & (j == 0))
    def _():
        token[...] = jnp.zeros_like(token)
        all_hot[...] = jnp.concatenate([g[...] for g in g_hot], 0)
        all_cold[...] = jnp.concatenate([g[...] for g in g_cold], 0)

    def total(xs, grads):
        rows = jnp.concatenate([x[:, at] for x in xs], 0)
        out[0] = lax.dot_general(
            rows, grads[...], (((0,), (0,)), ((), ())), preferred_element_type=F32
        ).astype(BF16)

    pl.when(e == hot)(lambda: total(x_hot, all_hot))
    pl.when(e != hot)(lambda: total(x_cold, all_cold))


def on_device(tokens, routes, gates, up_weight, replica_on, grad_out):
    count, feat = tokens.shape
    topk = routes.shape[1]
    experts = replica_on.shape[0]
    share = grad_out.shape[1]
    ff = up_weight.shape[2]
    n_ep, n_tp = lax.axis_size("ep"), lax.axis_size("tp")
    outer = n_ep // INNER
    capacity = 3 * count * topk // (4 * experts)
    hot_rows, cold_rows = 2 * capacity, capacity
    width = feat + share + TAIL
    there = feat + share
    by_hand = n_tp == 2 and outer == CHUNKS
    smem = pl.BlockSpec(memory_space=pltpu.SMEM)

    def along(value, shift):
        pairs = [
            (o * INNER + i, ((o + shift) % outer) * INNER + i)
            for o in range(outer)
            for i in range(INNER)
        ]
        return lax.ppermute(value, "ep", pairs)

    def across(value, d):
        pairs = [(o * INNER + i, o * INNER + (i ^ d)) for o in range(outer) for i in range(INNER)]
        return lax.ppermute(value, "ep", pairs)

    rest_spec = pl.BlockSpec(memory_space=pl.ANY)
    m = max(1, outer // CHUNKS)
    chunks = [list(range(first, first + m)) for first in range(0, outer, m)]
    n = len(chunks)
    rows = m * (hot_rows + cold_rows)
    hots, colds = INNER * m * hot_rows, INNER * m * cold_rows
    sizes = (m, hot_rows, cold_rows)

    def block(shape, dtype=BF16):
        return jax.ShapeDtypeStruct(shape, dtype)

    def fixed(shape):
        return pl.BlockSpec(shape, lambda j: (0,) * len(shape))

    going = {f: k for k, (f, _) in enumerate(PLAN) if f is not None}
    coming = {r: k for k, (_, r) in enumerate(PLAN) if r is not None}

    def weigh(kind):
        return cost(COSTS[kind] * 10**6, COSTS[kind] * 10**4)

    arrived, picks, marks, blocks, sums, grads, partials = {}, {}, {}, {}, {}, {}, {}
    x_hots, x_colds, g_hots, g_colds = {}, {}, {}, {}

    def exchange(k, made):
        blocks[k] = [made[0]] + [across(made[d], d) for d in range(1, INNER)]

    own_rows = m == 1
    made = pl.pallas_call(
        functools.partial(start_kernel, *sizes),
        out_shape=[block((count, share + TAIL))]
        + (
            [block((rows, there))] * INNER
            + [block((INNER * rows, TAIL), F32), block((count, INNER * rows))]
            if own_rows
            else []
        ),
        in_specs=[smem] + [rest_spec] * 4,
        out_specs=whole_specs(1 + (INNER + 2 if own_rows else 0)),
        scratch_shapes=[
            pltpu.VMEM((count, feat), BF16),
            pltpu.VMEM((topk, count), I32),
            pltpu.VMEM((topk, count), F32),
            pltpu.SemaphoreType.DMA((4,)),
        ],
        compiler_params=params(WIDE),
        cost_estimate=weigh("x"),
        name="start",
    )(replica_on, tokens, routes.T, gates.T, grad_out)
    last = []
    for c in (0, 1):
        for s in chunks[c]:
            if c:
                arrived[s] = [along(piece, m) for piece in arrived[s - m]]
            else:
                arrived[s] = [along(piece, s) if s else piece for piece in (tokens, made[0])]

    def skip_of(c):
        return 0 if c < 2 else feat

    def select(k):
        c = PLAN[k][0]
        joins = m if c == 1 else 0
        chosen = pl.pallas_call(
            functools.partial(select_kernel, *sizes, topk, share, skip_of(c), len(last)),
            out_shape=[block((rows, there))] * INNER
            + [block((INNER * rows, TAIL), F32)]
            + [block((count, INNER * rows))] * m
            + [block((count, width))] * joins,
            in_specs=[smem] + whole_specs(2 * m) + [rest_spec] * len(last),
            out_specs=whole_specs(INNER + 1 + m + joins),
            compiler_params=params(),
            cost_estimate=weigh("x"),
            name="select",
        )(
            replica_on,
            *[arrived[s][0] for s in chunks[c]],
            *[arrived[s][-1] for s in chunks[c]],
            *last,
        )
        marks[c], picks[c] = chosen[INNER], chosen[INNER + 1 : INNER + 1 + m]
        if joins:
            now = chosen[INNER + 1 + m :]
            for after in (2, 3):
                now = [along(value, m) for value in now]
                for s, value in zip(chunks[after], now):
                    arrived[s] = [value]
        exchange(k, chosen)
        last[:] = [picks[c][0]]

    def hidden(c):
        k = going[c]
        tile = 256 if ff % 256 == 0 else ff
        shapes = [(INNER * rows, ff + share), (hots, feat), (colds, feat)]
        streamed = c == 0 and FIRST > 0
        if streamed:
            where = dict(
                grid=(ff // tile,),
                in_specs=[smem]
                + [fixed(b.shape) for b in blocks[k]]
                + [pl.BlockSpec((2, feat, tile), lambda j: (0, 0, j))]
                + [rest_spec] * len(last),
                out_specs=[fixed(shape) for shape in shapes],
            )
        else:
            where = dict(
                in_specs=[smem] + whole_specs(INNER + 1) + [rest_spec] * len(last),
                out_specs=whole_specs(3),
            )
        part, x_hots[c], x_colds[c] = pl.pallas_call(
            functools.partial(hidden_kernel, *sizes, feat, streamed, len(last)),
            out_shape=[block(shape) for shape in shapes],
            **where,
            compiler_params=params(WIDE if c == 0 and FIRST == 2 else LIMIT),
            cost_estimate=weigh("h"),
            name="hidden",
        )(replica_on, *blocks[k], up_weight, *last)
        last[:] = [x_colds[c]]
        if n_tp == 2:
            sums[c] = [part, lax.ppermute(part, "tp", [(0, 1), (1, 0)])]
            grads[c] = sums[c]
        else:
            sums[c] = [lax.psum(part[:, :ff].astype(F32), "tp")]
            grads[c] = [lax.all_gather(part[:, ff:], "tp", axis=1, tiled=True)]

    def step(k):
        f, c = PLAN[k]
        if c is None:
            return select(k)
        made = pl.pallas_call(
            functools.partial(
                back_kernel, *sizes, len(sums[c]), len(grads[c]), share, c < 2, len(last)
            ),
            out_shape=[block((rows, width if c < 2 else there))] * INNER
            + [block((hots, ff)), block((colds, ff))],
            in_specs=[smem]
            + whole_specs(len(sums[c]) + len(grads[c]) + 1)
            + [rest_spec] * len(last),
            out_specs=whole_specs(INNER + 2),
            compiler_params=params(),
            cost_estimate=weigh("b"),
            name="back",
        )(replica_on, *sums[c], *grads[c], up_weight, *last)
        g_hots[c], g_colds[c] = made[INNER : INNER + 2]
        exchange(k, made)
        last[:] = [g_colds[c]]

    homes = {}

    def expand(c):
        more = [along(partials[s - m], m) for s in chunks[c]] if c > 2 else []
        sources = [arrived[s][-1] for s in chunks[c]] if c > 1 else []
        apart = [block((count, TAIL))] if c == n - 1 and by_hand else []
        k = coming[c]
        made = pl.pallas_call(
            functools.partial(
                expand_kernel, m, topk, share, c < 2, skip_of(c), len(more), len(last)
            ),
            out_shape=[block((count, width))] * m + apart,
            in_specs=whole_specs(INNER + m + 1 + len(sources) + len(more))
            + [rest_spec] * len(last),
            out_specs=whole_specs(m + len(apart)),
            compiler_params=params(),
            cost_estimate=weigh("e"),
            name="expand",
        )(*blocks[k], *picks[c], marks[c], *sources, *more, *last)
        for s, value in zip(chunks[c], made):
            partials[s] = value
            if c == 1:
                homes[s - m] = along(value, outer - m)
        if apart:
            partials["apart"] = made[m]
        last[:] = [made[0]]

    def weight_grad():
        tile = 512 if feat % 512 == 0 else feat
        grad_up, token = pl.pallas_call(
            functools.partial(up_kernel, n, len(last)),
            out_shape=[block(up_weight.shape), block((8, 128), F32)],
            grid=(up_weight.shape[0], feat // tile),
            in_specs=[smem] + whole_specs(4 * n) + [rest_spec] * len(last),
            out_specs=[
                pl.BlockSpec((1, tile, ff), lambda e, j: (e, j, 0)),
                pl.BlockSpec((8, 128), lambda e, j: (0, 0)),
            ],
            scratch_shapes=[
                pltpu.VMEM((n * hots, ff), BF16),
                pltpu.VMEM((n * colds, ff), BF16),
            ],
            compiler_params=params(),
            cost_estimate=weigh("u"),
            name="grad_up",
        )(
            replica_on,
            *[x_hots[c] for c in range(n)],
            *[x_colds[c] for c in range(n)],
            *[g_hots[c] for c in range(n)],
            *[g_colds[c] for c in range(n)],
            *last,
        )
        last[:] = [token]
        return grad_up

    if own_rows:
        marks[0], picks[0] = made[INNER + 1], made[INNER + 2 :]
        exchange(0, made[1 : INNER + 1])
    else:
        select(0)
    grad_up = None
    for word in ORDER:
        number = int(word[1:] or 0)
        if word[0] == "u":
            grad_up = weight_grad()
        elif word[0] == "r":
            last.append(sums[number][-1])
        elif word[0] == "z":
            last.append(homes[0])
        else:
            {"x": step, "h": hidden, "e": expand}[word[0]](number)

    sums_back = [along(partials[s], m) for s in chunks[n - 1]]
    if by_hand:
        pairs = [
            (
                (o * INNER + i) * n_tp + t,
                (((o + m) % outer) * INNER + i) * n_tp + 1 - t,
            )
            for o in range(outer)
            for i in range(INNER)
            for t in range(n_tp)
        ]
        tails = [lax.ppermute(partials["apart"], ("ep", "tp"), pairs)]
        parts = [sums_back[0], partials[0], homes[0]]
    else:
        parts, tails, halves = [], [], 0.0
        for s, value in zip(chunks[0], sums_back):
            if s == 0:
                parts += [array[:, :there] for array in (value, partials[0], homes[0])]
                halves = halves + value[:, there:].astype(F32)
                tails += [partials[0][:, there:], homes[0][:, there:]]
            else:
                ours = partials[s] + homes[s]
                parts.append(along(value[:, :there] + ours[:, :there], outer - s))
                halves = halves + along(value[:, there:], outer - s).astype(F32)
                tails.append(along(ours[:, there:], outer - s))
        tails.append(lax.psum(halves, "tp"))
    mixed, grad_tokens, grad_gates = pl.pallas_call(
        functools.partial(final_kernel, len(parts), len(tails), topk),
        out_shape=[block((count, share)), block((count, feat)), block((topk, count), F32)],
        in_specs=whole_specs(len(parts) + len(tails)),
        out_specs=whole_specs(3),
        compiler_params=params(),
        cost_estimate=weigh("e"),
        name="final",
    )(*parts, *tails)
    return mixed, grad_tokens, grad_gates.T, grad_up


def solution(mesh):
    return jax.shard_map(
        on_device,
        mesh=mesh,
        in_specs=(
            P("ep", "tp"),
            P("ep", None),
            P("ep", None),
            P("ep", "tp", None),
            P(),
            P("ep", "tp"),
        ),
        out_specs=(P("ep", "tp"), P("ep", "tp"), P("ep", None), P("ep", "tp", None)),
        check_vma=False,
    )
```

```python
import functools

import jax
import jax.numpy as jnp
from jax import lax
from jax.experimental import pallas as pl
from jax.experimental.pallas import tpu as pltpu
from jax.sharding import PartitionSpec as P

INNER = 4
CHUNKS = 4
PLAN = ((0, None), (1, None), (2, None), (3, None), (None, 1), (None, 2), (None, 3), (None, 0))
ORDER = ('x1', 'h0', 'x2', 'h1', 'x3', 'h2', 'r0', 'x4', 'h3', 'x5', 'r3', 'e1', 'x6', 'z', 'e2', 'r2', 'x7', 'e3', 'u', 'e0')
FIRST = 1
COSTS = {'x': 5000, 'b': 20000, 'h': 5000, 'e': 1, 'u': 20000}
TAIL = 128
LIMIT = 20 * 1024 * 1024
WIDE = 56 * 1024 * 1024
F32, BF16, I32 = jnp.float32, jnp.bfloat16, jnp.int32


def params(limit=LIMIT):
    return pltpu.CompilerParams(vmem_limit_bytes=limit)


def cost(flops, moved):
    return pl.CostEstimate(flops=int(flops), bytes_accessed=int(moved), transcendentals=0)


def whole_specs(n):
    return [pl.BlockSpec(memory_space=pltpu.VMEM)] * n


def hot_of(plan, device):
    return plan[2 * device + 1]


def rows_joined(pieces):
    if all(piece.shape[0] % 16 == 0 for piece in pieces):
        return jnp.concatenate(pieces, 0)
    return jnp.concatenate([piece.astype(F32) for piece in pieces], 0).astype(BF16)


def row_plan(m, hot_rows, cold_rows, plan, shape, axis):
    rows = m * (hot_rows + cold_rows)
    me = lax.axis_index("ep")
    outer, inner = me // INNER, me % INNER
    spot = lax.broadcasted_iota(I32, shape, axis)
    which = jnp.zeros(shape, I32)
    for d in range(1, INNER):
        which += (spot >= d * rows).astype(I32)
    within = spot - which * rows
    is_hot = within < m * hot_rows
    group = jnp.zeros(shape, I32)
    for s in range(1, m):
        edge = jnp.where(is_hot, s * hot_rows, m * hot_rows + s * cold_rows)
        group += (within >= edge).astype(I32)
    slot = jnp.where(is_hot, within - group * hot_rows, within - m * hot_rows - group * cold_rows)
    expert = jnp.zeros(shape, I32)
    for d in range(INNER):
        device = outer * INNER + (inner ^ d)
        hot = hot_of(plan, device)
        ids = jnp.where(is_hot, 2 * device + hot, 2 * device + 1 - hot)
        expert = jnp.where(which == d, ids, expert)
    return expert.astype(F32), slot.astype(F32), group


def pick_rows(m, hot_rows, cold_rows, topk, plan, tails):
    count = tails[0].shape[0]
    cols = INNER * m * (hot_rows + cold_rows)
    expert, slot, group = (
        value[0:1] for value in row_plan(m, hot_rows, cold_rows, plan, (8, cols), 1)
    )
    before = lax.broadcasted_iota(I32, (count, count), 1) < lax.broadcasted_iota(I32, (count, count), 0)
    before = jnp.where(before, 1.0, 0.0).astype(BF16)
    found = []
    for s, ids in enumerate(tails):
        match = ids[:, 0:1] == expert
        for k in range(1, topk):
            match = match | (ids[:, k : k + 1] == expert)
        ones = jnp.where(match, 1.0, 0.0)
        rank = jnp.dot(before, ones.astype(BF16), preferred_element_type=F32)
        found.append(jnp.where((rank == slot) & (group == s), ones, 0.0).astype(BF16))
    return found


def picked(picks, sources, columns):
    total = None
    for pick, source in zip(picks, sources):
        part = lax.dot_general(
            pick[...], source[:, columns], (((0,), (0,)), ((), ())), preferred_element_type=F32
        )
        total = part if total is None else total + part
    return total


def select_all(m, hot_rows, cold_rows, topk, share, skip, plan, picks, tokens, rests, outs, marks):
    rows, width = outs[0].shape
    feat = width - share
    expert, _, _ = row_plan(m, hot_rows, cold_rows, plan, (INNER * rows, TAIL), 0)
    tail = picked(picks, rests, slice(skip + share, skip + share + TAIL))
    gate = (tail[:, 2 * topk : 3 * topk] + tail[:, 3 * topk : 4 * topk]) + tail[:, 4 * topk : 5 * topk]
    gate = jnp.sum(jnp.where(tail[:, :topk] == expert[:, :topk], gate, 0.0), 1, keepdims=True)
    lane = lax.broadcasted_iota(I32, tail.shape, 1)
    own = jnp.where((tail == expert) & (lane < 2 * topk), 1.0, 0.0)
    marks[...] = jnp.where(lane == 2 * topk, gate, own)
    step = 512 if feat % 512 == 0 else 128
    for at in [*range(0, feat, step), feat]:
        if at < feat:
            columns = slice(at, at + step)
            total = picked(picks, tokens, columns)
        else:
            columns = slice(feat, width)
            total = gate * picked(picks, rests, slice(skip, skip + share))
        for d in range(INNER):
            outs[d][:, columns] = total[d * rows : (d + 1) * rows].astype(BF16)


def start_kernel(m, hot_rows, cold_rows, plan, tokens, routes, gates, grad_out, *refs):
    out, refs = refs[0], refs[1:]
    here, here_routes, here_gates, sems = refs[-4:]
    outs, marks, picks = refs[:INNER], refs[INNER:-4][:1], refs[INNER:-4][1:]
    count, feat = tokens.shape
    share = grad_out.shape[1]
    topk = routes.shape[0]
    copies = [
        pltpu.make_async_copy(source, target, sems.at[n])
        for n, (source, target) in enumerate(
            (
                (routes, here_routes),
                (gates, here_gates),
                (tokens, here),
                (grad_out, out.at[:, :share]),
            )
        )
    ]
    for copy in copies:
        copy.start()
    for copy in copies[:2]:
        copy.wait()
    ids = here_routes[...].astype(F32)
    gate = here_gates[...]
    high = gate.astype(BF16).astype(F32)
    middle = (gate - high).astype(BF16).astype(F32)
    low = (gate - high - middle).astype(BF16).astype(F32)
    rest = jnp.zeros((TAIL - 5 * topk, count), F32)
    tail = jnp.concatenate([ids, ids, high, middle, low, rest], 0).T
    out[:, share:] = tail.astype(BF16)
    if picks:
        picks[0][...] = pick_rows(m, hot_rows, cold_rows, topk, plan, [tail])[0]
    for copy in copies[2:]:
        copy.wait()
    if picks:
        select_all(
            m, hot_rows, cold_rows, topk, share, 0, plan, picks, [here], [out], outs, marks[0]
        )


def select_kernel(m, hot_rows, cold_rows, topk, share, skip, waits, plan, *refs):
    tokens, rests, refs = refs[:m], refs[m : 2 * m], refs[2 * m + waits :]
    outs, marks, picks, joined = refs[:INNER], refs[INNER], refs[INNER + 1 : INNER + 1 + m], refs[INNER + 1 + m :]
    tails = [rest[:, skip + share :].astype(F32) for rest in rests]
    for pick, found in zip(picks, pick_rows(m, hot_rows, cold_rows, topk, plan, tails)):
        pick[...] = found
    select_all(m, hot_rows, cold_rows, topk, share, skip, plan, picks, tokens, rests, outs, marks)
    for token, rest, target in zip(tokens, rests, joined):
        feat = token.shape[1]
        target[:, :feat] = token[...]
        target[:, feat:] = rest[...]


def hidden_kernel(m, hot_rows, cold_rows, feat, streamed, waits, plan, *refs):
    blocks = refs[:INNER]
    weight, part, x_hot, x_cold = refs[INNER], *refs[INNER + 1 + waits :]
    hots = INNER * m * hot_rows
    share = blocks[0].shape[1] - feat
    ff = part.shape[1] - share
    tile = 256 if ff % 256 == 0 else ff
    hot = hot_of(plan, lax.axis_index("ep"))
    split = m * hot_rows

    def gather():
        x_hot[...] = rows_joined([b[:split, :feat] for b in blocks])
        x_cold[...] = rows_joined([b[split:, :feat] for b in blocks])
        part[:hots, ff:] = rows_joined([b[:split, feat:] for b in blocks])
        part[hots:, ff:] = rows_joined([b[split:, feat:] for b in blocks])

    def columns(j, source):
        at = pl.ds(pl.multiple_of(j * tile, tile), tile)
        part[:hots, at] = jnp.dot(
            x_hot[...], weight[hot, :, source], preferred_element_type=F32
        ).astype(BF16)
        part[hots:, at] = jnp.dot(
            x_cold[...], weight[1 - hot, :, source], preferred_element_type=F32
        ).astype(BF16)

    if streamed:
        pl.when(pl.program_id(0) == 0)(gather)
        columns(pl.program_id(0), slice(None))
    else:
        gather()

        @pl.loop(0, ff // tile)
        def _(j):
            columns(j, pl.ds(pl.multiple_of(j * tile, tile), tile))


def back_kernel(m, hot_rows, cold_rows, n_parts, n_grads, share, tailed, waits, plan, *refs):
    sums, grads = refs[:n_parts], refs[n_parts : n_parts + n_grads]
    weight, refs = refs[n_parts + n_grads], refs[n_parts + n_grads + 1 + waits :]
    outs, g_hot, g_cold = refs[:INNER], refs[INNER], refs[INNER + 1]
    hots, colds = m * hot_rows, m * cold_rows
    feat, ff = weight.shape[1:]
    width = outs[0].shape[1]
    tile = 512 if feat % 512 == 0 else feat
    tp = lax.axis_index("tp")
    hot = hot_of(plan, lax.axis_index("ep"))

    def put(columns, back_hot, back_cold):
        for d in range(INNER):
            outs[d][:hots, columns] = back_hot[d * hots : (d + 1) * hots].astype(BF16)
            outs[d][hots:, columns] = back_cold[d * colds : (d + 1) * colds].astype(BF16)

    ends = []
    for first, piece, target in ((0, hots, g_hot), (INNER * hots, colds, g_cold)):
        made = []
        per = 1 if piece % 16 == 0 else INNER
        for d in range(0, INNER, per):
            count = piece * per
            now = slice(first + d * piece, first + d * piece + count)
            hidden = sums[0][now, :ff].astype(F32)
            for more in sums[1:]:
                hidden = hidden + more[now, :ff].astype(F32)
            if n_grads == 1:
                row_grad = grads[0][now].astype(F32)
            else:
                mine, other = (g[now, ff:].astype(F32) for g in grads)
                even = tp == 0
                row_grad = jnp.concatenate(
                    [jnp.where(even, mine, other), jnp.where(even, other, mine)], 1
                )
            sig = 1.0 / (1.0 + jnp.exp(-hidden))
            act = (hidden * sig).astype(BF16).astype(F32)
            hidden_grad = row_grad * (sig * (1.0 + hidden * (1.0 - sig)))
            target[d * piece : d * piece + count] = hidden_grad.astype(BF16)
            half = None
            for n in range(ff // share):
                piece_act = jnp.where(tp == n, act[:, n * share : (n + 1) * share], 0.0)
                half = piece_act if half is None else half + piece_act
            if tailed:
                gate_grad = jnp.sum(act * row_grad, 1, keepdims=True)
                high = gate_grad.astype(BF16).astype(F32)
                low = gate_grad - high
                lane = lax.broadcasted_iota(I32, (count, TAIL), 1)
                end = jnp.where(lane == 0, high, jnp.where(lane == 1, low, 0.0))
                half = jnp.concatenate([half, end], 1)
            made.append(half)
        ends.append(jnp.concatenate(made, 0))
    put(slice(feat, width), *ends)

    across_rows = (((1,), (1,)), ((), ()))

    def features(j, carry):
        at = pl.ds(pl.multiple_of(j * tile, tile), tile)
        put(
            at,
            lax.dot_general(
                g_hot[...], weight[hot, at, :], across_rows, preferred_element_type=F32
            ),
            lax.dot_general(
                g_cold[...], weight[1 - hot, at, :], across_rows, preferred_element_type=F32
            ),
        )
        return carry

    lax.fori_loop(0, feat // tile, features, 0)


def expand_kernel(m, topk, share, tailed, skip, n_more, waits, *refs):
    blocks, picks, marks, refs = refs[:INNER], refs[INNER : INNER + m], refs[INNER + m], refs[INNER + m + 1 :]
    rests, refs = ([], refs) if tailed else (refs[:m], refs[m:])
    more, outs, apart = refs[:n_more], refs[n_more + waits :][:m], refs[n_more + waits + m :]
    width = outs[0].shape[1]
    feat = width - share - TAIL

    def add(columns, rows, copies=()):
        for s in range(m):
            total = jnp.dot(picks[s][...], rows, preferred_element_type=F32)
            if more:
                total = total + more[s][:, columns].astype(F32)
            outs[s][:, columns] = total.astype(BF16)
            for copy in copies[s : s + 1]:
                copy[...] = total.astype(BF16)

    def joined(columns):
        return rows_joined([b[:, columns] for b in blocks])

    step = 512 if feat % 512 == 0 else 128
    for at in range(0, feat, step):
        add(slice(at, at + step), joined(slice(at, at + step)))
    mark = marks[...]
    gate = mark[:, 2 * topk : 2 * topk + 1]
    columns = slice(feat, feat + share)
    act = joined(columns).astype(F32)
    add(columns, (gate * act).astype(BF16))
    columns = slice(feat + share, width)
    if tailed:
        end = joined(columns).astype(F32)
        gate_grad = (end[:, 0:1] + end[:, 1:2]) / jnp.where(gate > 0.0, gate, 1.0)
    else:
        grad = picked(picks, rests, slice(skip, skip + share))
        gate_grad = jnp.sum(act * grad, 1, keepdims=True)
    high = gate_grad.astype(BF16).astype(F32)
    lane = lax.broadcasted_iota(I32, mark.shape, 1)
    values = jnp.where(lane < topk, high, gate_grad - high)
    end = jnp.where((lane < 2 * topk) & (mark > 0.0), values, 0.0)
    add(columns, end.astype(BF16), apart)


def final_kernel(n, n_tails, topk, *refs):
    parts, tails = refs[:n], refs[n : n + n_tails]
    mixed, grad_tokens, grad_gates = refs[n + n_tails :]
    feat, share = grad_tokens.shape[1], mixed.shape[1]

    def total(columns):
        out = parts[0][:, columns].astype(F32)
        for part in parts[1:]:
            out = out + part[:, columns].astype(F32)
        return out

    grad_tokens[...] = total(slice(0, feat)).astype(BF16)
    mixed[...] = total(slice(feat, feat + share)).astype(BF16)
    ends = [tail[...].astype(F32) for tail in tails]
    ends += [part[:, feat + share :].astype(F32) for part in parts if part.shape[1] > feat + share]
    end = ends[0]
    for more in ends[1:]:
        end = end + more
    end = end.T
    grad_gates[...] = end[:topk] + end[topk : 2 * topk]


def up_kernel(n, waits, plan, *refs):
    x_hot, x_cold = refs[:n], refs[n : 2 * n]
    g_hot, g_cold = refs[2 * n : 3 * n], refs[3 * n : 4 * n]
    out, token, all_hot, all_cold = refs[4 * n + waits :]
    tile = out.shape[1]
    e, j = pl.program_id(0), pl.program_id(1)
    hot = hot_of(plan, lax.axis_index("ep"))
    at = pl.ds(pl.multiple_of(j * tile, tile), tile)

    @pl.when((e == 0) & (j == 0))
    def _():
        token[...] = jnp.zeros_like(token)
        all_hot[...] = jnp.concatenate([g[...] for g in g_hot], 0)
        all_cold[...] = jnp.concatenate([g[...] for g in g_cold], 0)

    def total(xs, grads):
        rows = jnp.concatenate([x[:, at] for x in xs], 0)
        out[0] = lax.dot_general(
            rows, grads[...], (((0,), (0,)), ((), ())), preferred_element_type=F32
        ).astype(BF16)

    pl.when(e == hot)(lambda: total(x_hot, all_hot))
    pl.when(e != hot)(lambda: total(x_cold, all_cold))


def on_device(tokens, routes, gates, up_weight, replica_on, grad_out):
    count, feat = tokens.shape
    topk = routes.shape[1]
    experts = replica_on.shape[0]
    share = grad_out.shape[1]
    ff = up_weight.shape[2]
    n_ep, n_tp = lax.axis_size("ep"), lax.axis_size("tp")
    outer = n_ep // INNER
    capacity = 3 * count * topk // (4 * experts)
    hot_rows, cold_rows = 2 * capacity, capacity
    width = feat + share + TAIL
    there = feat + share
    by_hand = n_tp == 2 and outer == CHUNKS
    smem = pl.BlockSpec(memory_space=pltpu.SMEM)

    def along(value, shift):
        pairs = [
            (o * INNER + i, ((o + shift) % outer) * INNER + i)
            for o in range(outer)
            for i in range(INNER)
        ]
        return lax.ppermute(value, "ep", pairs)

    def across(value, d):
        pairs = [(o * INNER + i, o * INNER + (i ^ d)) for o in range(outer) for i in range(INNER)]
        return lax.ppermute(value, "ep", pairs)

    rest_spec = pl.BlockSpec(memory_space=pl.ANY)
    m = max(1, outer // CHUNKS)
    chunks = [list(range(first, first + m)) for first in range(0, outer, m)]
    n = len(chunks)
    rows = m * (hot_rows + cold_rows)
    hots, colds = INNER * m * hot_rows, INNER * m * cold_rows
    sizes = (m, hot_rows, cold_rows)

    def block(shape, dtype=BF16):
        return jax.ShapeDtypeStruct(shape, dtype)

    def fixed(shape):
        return pl.BlockSpec(shape, lambda j: (0,) * len(shape))

    going = {f: k for k, (f, _) in enumerate(PLAN) if f is not None}
    coming = {r: k for k, (_, r) in enumerate(PLAN) if r is not None}

    def weigh(kind):
        return cost(COSTS[kind] * 10**6, COSTS[kind] * 10**4)

    arrived, picks, marks, blocks, sums, grads, partials = {}, {}, {}, {}, {}, {}, {}
    x_hots, x_colds, g_hots, g_colds = {}, {}, {}, {}

    def exchange(k, made):
        blocks[k] = [made[0]] + [across(made[d], d) for d in range(1, INNER)]

    own_rows = m == 1
    made = pl.pallas_call(
        functools.partial(start_kernel, *sizes),
        out_shape=[block((count, share + TAIL))]
        + (
            [block((rows, there))] * INNER
            + [block((INNER * rows, TAIL), F32), block((count, INNER * rows))]
            if own_rows
            else []
        ),
        in_specs=[smem] + [rest_spec] * 4,
        out_specs=whole_specs(1 + (INNER + 2 if own_rows else 0)),
        scratch_shapes=[
            pltpu.VMEM((count, feat), BF16),
            pltpu.VMEM((topk, count), I32),
            pltpu.VMEM((topk, count), F32),
            pltpu.SemaphoreType.DMA((4,)),
        ],
        compiler_params=params(WIDE),
        cost_estimate=weigh("x"),
        name="start",
    )(replica_on, tokens, routes.T, gates.T, grad_out)
    last = []
    for c in (0, 1):
        for s in chunks[c]:
            if c:
                arrived[s] = [along(piece, m) for piece in arrived[s - m]]
            else:
                arrived[s] = [along(piece, s) if s else piece for piece in (tokens, made[0])]

    def skip_of(c):
        return 0 if c < 2 else feat

    def select(k):
        c = PLAN[k][0]
        joins = m if c == 1 else 0
        chosen = pl.pallas_call(
            functools.partial(select_kernel, *sizes, topk, share, skip_of(c), len(last)),
            out_shape=[block((rows, there))] * INNER
            + [block((INNER * rows, TAIL), F32)]
            + [block((count, INNER * rows))] * m
            + [block((count, width))] * joins,
            in_specs=[smem] + whole_specs(2 * m) + [rest_spec] * len(last),
            out_specs=whole_specs(INNER + 1 + m + joins),
            compiler_params=params(),
            cost_estimate=weigh("x"),
            name="select",
        )(
            replica_on,
            *[arrived[s][0] for s in chunks[c]],
            *[arrived[s][-1] for s in chunks[c]],
            *last,
        )
        marks[c], picks[c] = chosen[INNER], chosen[INNER + 1 : INNER + 1 + m]
        if joins:
            now = chosen[INNER + 1 + m :]
            for after in (2, 3):
                now = [along(value, m) for value in now]
                for s, value in zip(chunks[after], now):
                    arrived[s] = [value]
        exchange(k, chosen)
        last[:] = [picks[c][0]]

    def hidden(c):
        k = going[c]
        tile = 256 if ff % 256 == 0 else ff
        shapes = [(INNER * rows, ff + share), (hots, feat), (colds, feat)]
        streamed = c == 0 and FIRST > 0
        if streamed:
            where = dict(
                grid=(ff // tile,),
                in_specs=[smem]
                + [fixed(b.shape) for b in blocks[k]]
                + [pl.BlockSpec((2, feat, tile), lambda j: (0, 0, j))]
                + [rest_spec] * len(last),
                out_specs=[fixed(shape) for shape in shapes],
            )
        else:
            where = dict(
                in_specs=[smem] + whole_specs(INNER + 1) + [rest_spec] * len(last),
                out_specs=whole_specs(3),
            )
        part, x_hots[c], x_colds[c] = pl.pallas_call(
            functools.partial(hidden_kernel, *sizes, feat, streamed, len(last)),
            out_shape=[block(shape) for shape in shapes],
            **where,
            compiler_params=params(WIDE if c == 0 and FIRST == 2 else LIMIT),
            cost_estimate=weigh("h"),
            name="hidden",
        )(replica_on, *blocks[k], up_weight, *last)
        last[:] = [x_colds[c]]
        if n_tp == 2:
            sums[c] = [part, lax.ppermute(part, "tp", [(0, 1), (1, 0)])]
            grads[c] = sums[c]
        else:
            sums[c] = [lax.psum(part[:, :ff].astype(F32), "tp")]
            grads[c] = [lax.all_gather(part[:, ff:], "tp", axis=1, tiled=True)]

    def step(k):
        f, c = PLAN[k]
        if c is None:
            return select(k)
        made = pl.pallas_call(
            functools.partial(
                back_kernel, *sizes, len(sums[c]), len(grads[c]), share, c < 2, len(last)
            ),
            out_shape=[block((rows, width if c < 2 else there))] * INNER
            + [block((hots, ff)), block((colds, ff))],
            in_specs=[smem]
            + whole_specs(len(sums[c]) + len(grads[c]) + 1)
            + [rest_spec] * len(last),
            out_specs=whole_specs(INNER + 2),
            compiler_params=params(),
            cost_estimate=weigh("b"),
            name="back",
        )(replica_on, *sums[c], *grads[c], up_weight, *last)
        g_hots[c], g_colds[c] = made[INNER : INNER + 2]
        exchange(k, made)
        last[:] = [g_colds[c]]

    homes = {}

    def expand(c):
        more = [along(partials[s - m], m) for s in chunks[c]] if c > 2 else []
        sources = [arrived[s][-1] for s in chunks[c]] if c > 1 else []
        apart = [block((count, TAIL))] if c == n - 1 and by_hand else []
        k = coming[c]
        made = pl.pallas_call(
            functools.partial(
                expand_kernel, m, topk, share, c < 2, skip_of(c), len(more), len(last)
            ),
            out_shape=[block((count, width))] * m + apart,
            in_specs=whole_specs(INNER + m + 1 + len(sources) + len(more))
            + [rest_spec] * len(last),
            out_specs=whole_specs(m + len(apart)),
            compiler_params=params(),
            cost_estimate=weigh("e"),
            name="expand",
        )(*blocks[k], *picks[c], marks[c], *sources, *more, *last)
        for s, value in zip(chunks[c], made):
            partials[s] = value
            if c == 1:
                homes[s - m] = along(value, outer - m)
        if apart:
            partials["apart"] = made[m]
        last[:] = [made[0]]

    def weight_grad():
        tile = 512 if feat % 512 == 0 else feat
        grad_up, token = pl.pallas_call(
            functools.partial(up_kernel, n, len(last)),
            out_shape=[block(up_weight.shape), block((8, 128), F32)],
            grid=(up_weight.shape[0], feat // tile),
            in_specs=[smem] + whole_specs(4 * n) + [rest_spec] * len(last),
            out_specs=[
                pl.BlockSpec((1, tile, ff), lambda e, j: (e, j, 0)),
                pl.BlockSpec((8, 128), lambda e, j: (0, 0)),
            ],
            scratch_shapes=[
                pltpu.VMEM((n * hots, ff), BF16),
                pltpu.VMEM((n * colds, ff), BF16),
            ],
            compiler_params=params(),
            cost_estimate=weigh("u"),
            name="grad_up",
        )(
            replica_on,
            *[x_hots[c] for c in range(n)],
            *[x_colds[c] for c in range(n)],
            *[g_hots[c] for c in range(n)],
            *[g_colds[c] for c in range(n)],
            *last,
        )
        last[:] = [token]
        return grad_up

    if own_rows:
        marks[0], picks[0] = made[INNER + 1], made[INNER + 2 :]
        exchange(0, made[1 : INNER + 1])
    else:
        select(0)
    grad_up = None
    for word in ORDER:
        number = int(word[1:] or 0)
        if word[0] == "u":
            grad_up = weight_grad()
        elif word[0] == "r":
            last.append(sums[number][-1])
        elif word[0] == "z":
            last.append(homes[0])
        else:
            {"x": step, "h": hidden, "e": expand}[word[0]](number)

    sums_back = [along(partials[s], m) for s in chunks[n - 1]]
    if by_hand:
        pairs = [
            (
                (o * INNER + i) * n_tp + t,
                (((o + m) % outer) * INNER + i) * n_tp + 1 - t,
            )
            for o in range(outer)
            for i in range(INNER)
            for t in range(n_tp)
        ]
        tails = [lax.ppermute(partials["apart"], ("ep", "tp"), pairs)]
        parts = [sums_back[0], partials[0], homes[0]]
    else:
        parts, tails, halves = [], [], 0.0
        for s, value in zip(chunks[0], sums_back):
            if s == 0:
                parts += [array[:, :there] for array in (value, partials[0], homes[0])]
                halves = halves + value[:, there:].astype(F32)
                tails += [partials[0][:, there:], homes[0][:, there:]]
            else:
                ours = partials[s] + homes[s]
                parts.append(along(value[:, :there] + ours[:, :there], outer - s))
                halves = halves + along(value[:, there:], outer - s).astype(F32)
                tails.append(along(ours[:, there:], outer - s))
        tails.append(lax.psum(halves, "tp"))
    mixed, grad_tokens, grad_gates = pl.pallas_call(
        functools.partial(final_kernel, len(parts), len(tails), topk),
        out_shape=[block((count, share)), block((count, feat)), block((topk, count), F32)],
        in_specs=whole_specs(len(parts) + len(tails)),
        out_specs=whole_specs(3),
        compiler_params=params(),
        cost_estimate=weigh("e"),
        name="final",
    )(*parts, *tails)
    return mixed, grad_tokens, grad_gates.T, grad_up


def solution(mesh):
    return jax.shard_map(
        on_device,
        mesh=mesh,
        in_specs=(
            P("ep", "tp"),
            P("ep", None),
            P("ep", None),
            P("ep", "tp", None),
            P(),
            P("ep", "tp"),
        ),
        out_specs=(P("ep", "tp"), P("ep", "tp"), P("ep", None), P("ep", "tp", None)),
        check_vma=False,
    )
```
